32 devices in a mesh: fsdp: 8 (over y, x, core), ctx: 4 (over z).
Axes of the slice: x: 2, y: 2, z: 4, core: 2. Of those that a mesh axis runs over, the one named last changes fastest.
Arguments:
- tokens_in: bfloat16 [8192, 1536], P(('fsdp', 'ctx')), may hold values from -6 to 6
- block_order: int32 [8, 4], P('fsdp'), may hold values from 0 to 3, each once within a row
- norm_attn: bfloat16 [1536], P('fsdp'), may hold values from 0.099609375 to 1.8984375
- w_qkv: bfloat16 [1536, 2048], P('fsdp'), may hold values from -0.15625 to 0.15625
- b_qkv: bfloat16 [2048], P('fsdp'), may hold values from -3 to 3
- w_out: bfloat16 [1536, 1536], P('fsdp'), may hold values from -0.625 to 0.625
- norm_mlp: bfloat16 [1536], P('fsdp'), may hold values from 0.099609375 to 1.8984375
- w_gate: bfloat16 [1536, 8960], P('fsdp'), may hold values from -0.15625 to 0.15625
- w_up: bfloat16 [1536, 8960], P('fsdp'), may hold values from -0.15625 to 0.15625
- w_down: bfloat16 [8960, 1536], P('fsdp'), may hold values from -0.0625 to 0.0625
- cotangent: bfloat16 [8192, 1536], P(('fsdp', 'ctx')), may hold values from -6 to 6
Outputs:
- out_tokens: bfloat16 [8192, 1536], P(('fsdp', 'ctx'))
- grad_tokens: bfloat16 [8192, 1536], P(('fsdp', 'ctx'))
- grad_norm_attn: float32 [1536], P('fsdp')
- grad_w_qkv: float32 [1536, 2048], P('fsdp')
- grad_b_qkv: float32 [2048], P('fsdp')
- grad_w_out: float32 [1536, 1536], P('fsdp')
- grad_norm_mlp: float32 [1536], P('fsdp')
- grad_w_gate: float32 [1536, 8960], P('fsdp')
- grad_w_up: float32 [1536, 8960], P('fsdp')
- grad_w_down: float32 [8960, 1536], P('fsdp')
The draws below stay inside these ranges and needn't reach their ends.
Inputs may be any that keep to these rules, and one draw needn't show every extreme that they name: Each row holds every block number of its sequence once: ctx index c holds block block_order[s, c], tokens block_order[s, c] * 256 to that plus 256 - 1.
All inputs are finite; a program needn't handle non-finite values.
Results may differ from the reference program's by a relative error of at most 0.02.
Values may be sent and summed in bfloat16 or wider, within the bound.
No kernel may reach another device: no remote copies, remote signals or barrier semaphores. Data moves between devices by JAX's collectives and lax.ppermute only.
A program may use at most 704 MiB of HBM per device.

```python
import math
import jax
import jax.numpy as jnp
from jax import lax

D = 1536
HEADS = 12
KV_HEADS = 2
HEAD = 128
FF = 8960
BLK = 256
QKV = 2048
SEQS = 8
LEN = 1024
TOKENS = 8192
N_CTX = 4


def shard_levels(rng, extent, shards, low, high):
    level, own = 1.0, jax.random.fold_in(rng, 6)
    for dim, shards_of in shards:
        steps = jnp.exp(jax.random.uniform(jax.random.fold_in(own, dim), (shards_of,), jnp.float32, low / len(shards), high / len(shards)))
        level = level * jnp.repeat(steps, extent[dim] // shards_of).reshape([-1 if axis == dim else 1 for axis in range(len(extent))])
    return level


def bell_draw(stream_key, shape, deviation, reach, shards=(), kind=jnp.bfloat16):
    level = shard_levels(stream_key, shape, shards, -0.22, 0.18) if shards else 1.0
    values = jax.random.normal(stream_key, shape, jnp.float32) * deviation * level
    return jnp.minimum(jnp.maximum(values, -reach), reach).astype(kind)


def setup_inputs(seed: int = 0) -> dict:
    seeds = jax.random.split(jax.random.key(seed), 12)
    return {
        "tokens_in": bell_draw(seeds[0], (TOKENS, D), 1.0, 6.0, ((0, 32),)),
        "block_order": jax.vmap(lambda own: jax.random.permutation(own, N_CTX))(jax.random.split(seeds[1], SEQS)).reshape((SEQS, N_CTX)).astype(jnp.int32),
        "norm_attn": jnp.clip(1.0 + 0.18 * jax.random.normal(seeds[2], (D,), jnp.float32), 0.099609375, 1.8984375).astype(jnp.bfloat16),
        "w_qkv": bell_draw(seeds[3], (D, QKV), D ** -0.5, 0.15625, ((0, 8),)),
        "b_qkv": bell_draw(seeds[4], (QKV,), 0.5, 3.0, ((0, 8),)),
        "w_out": bell_draw(seeds[5], (HEADS * HEAD, D), (HEADS * HEAD // 16) ** -0.5, 0.625, ((0, 8),)),
        "norm_mlp": jnp.clip(1.0 + 0.18 * jax.random.normal(seeds[6], (D,), jnp.float32), 0.099609375, 1.8984375).astype(jnp.bfloat16),
        "w_gate": bell_draw(seeds[7], (D, FF), D ** -0.5, 0.15625, ((0, 8),)),
        "w_up": bell_draw(seeds[8], (D, FF), D ** -0.5, 0.15625, ((0, 8),)),
        "w_down": bell_draw(seeds[9], (FF, D), FF ** -0.5, 0.0625, ((0, 8),)),
        "cotangent": bell_draw(seeds[10], (TOKENS, D), 1.0, 6.0, ((0, 32),)),
    }


@jax.custom_vjp
def low(v):
    return lax.optimization_barrier(v.astype(jnp.bfloat16)).astype(jnp.float32)

@jax.custom_vjp
def low_back(v):
    return v

def low_keep(v):
    return (low(v), None)

def low_pass(kept, grad):
    return (grad,)

def back_keep(v):
    return (v, None)

def back_low(kept, grad):
    return (low(grad),)
low.defvjp(low_keep, low_pass)
low_back.defvjp(back_keep, back_low)
norm_eps = 1e-06
rope_base = 1000000.0
masked_score = -1e+30

def matmul(left_side, right_side):
    return jnp.dot(left_side, right_side, precision=lax.Precision.HIGHEST, preferred_element_type=jnp.float32)

def rotary(positions):
    half_width = HEAD // 2
    frequency = rope_base ** (-(jnp.arange(half_width, dtype=jnp.float32) * 2.0) / HEAD)
    angles = positions.astype(jnp.float32)[:, None] * frequency[None, :]
    angles = jnp.concatenate([angles, angles], 1)
    return (jnp.cos(angles)[:, None, :], jnp.sin(angles)[:, None, :])

def turned(tensor):
    half_width = tensor.shape[-1] // 2
    return jnp.concatenate([-tensor[..., half_width:], tensor[..., :half_width]], -1)

def forward(params, source, positions):
    norm_attn, w_qkv, b_qkv, w_out, norm_mlp, w_gate, w_up, w_down = params
    cosine, sine_part = rotary(positions)
    q_width = HEADS * HEAD
    k_width = KV_HEADS * HEAD
    group_size = HEADS // KV_HEADS
    score_scale = HEAD ** (-0.5)
    scale_one = lax.rsqrt(lax.optimization_barrier(jnp.mean(source * source, axis=-1, keepdims=True)) + norm_eps)
    normed = low(source * scale_one * norm_attn)
    projected = low_back(matmul(normed, w_qkv) + b_qkv)
    query = projected[:, :q_width].reshape(LEN, HEADS, HEAD)
    key_heads = projected[:, q_width:q_width + k_width].reshape(LEN, KV_HEADS, HEAD)
    value_heads = low(projected[:, q_width + k_width:].reshape(LEN, KV_HEADS, HEAD))
    query = low(query * cosine + turned(query) * sine_part)
    key_heads = low(key_heads * cosine + turned(key_heads) * sine_part)
    query = query.reshape(LEN, KV_HEADS, group_size, HEAD)
    block_rows = math.gcd(LEN, 512)
    blocks = LEN // block_rows

    def attend_block(items):
        query_block, query_pos = items
        raw_scores = jnp.einsum('qhgd,khd->qhgk', query_block, key_heads, precision=lax.Precision.HIGHEST)
        scores = low_back(raw_scores) * score_scale
        visible = positions[None, None, None, :] <= query_pos[:, None, None, None]
        scores = jnp.where(visible, scores, masked_score)
        top_score = lax.optimization_barrier(jnp.max(scores, -1, keepdims=True))
        weights = jnp.exp(scores - top_score)
        probability = low(weights / lax.optimization_barrier(jnp.sum(weights, -1, keepdims=True)))
        return jnp.einsum('qhgk,khd->qhgd', probability, value_heads, precision=lax.Precision.HIGHEST)
    mixed = lax.map(jax.checkpoint(attend_block), (query.reshape(blocks, block_rows, KV_HEADS, group_size, HEAD), positions.reshape(blocks, block_rows)))
    mixed = low(low_back(mixed.reshape(LEN, q_width)))
    hidden = source + low_back(matmul(mixed, w_out))
    scale_two = lax.rsqrt(lax.optimization_barrier(jnp.mean(hidden * hidden, axis=-1, keepdims=True)) + norm_eps)
    normed_two = low(hidden * scale_two * norm_mlp)
    gate_value = low_back(matmul(normed_two, w_gate))
    up_value = low_back(matmul(normed_two, w_up))
    activation = low(jax.nn.silu(gate_value) * up_value)
    return hidden + matmul(activation, w_down)

def reference(tokens_in, block_order, norm_attn, w_qkv, b_qkv, w_out, norm_mlp, w_gate, w_up, w_down, cotangent):
    params = tuple((weight.astype(jnp.float32) for weight in (norm_attn, w_qkv, b_qkv, w_out, norm_mlp, w_gate, w_up, w_down)))
    positions = (block_order[:, :, None] * BLK + jnp.arange(BLK, dtype=jnp.int32)[None, None, :]).reshape(SEQS, LEN).astype(jnp.int32)
    sources = tokens_in.astype(jnp.float32).reshape(SEQS, LEN, D)
    cotangents = cotangent.astype(jnp.float32).reshape(SEQS, LEN, D)

    def one_sequence(running, items):
        source, grad_out, seq_pos = items
        result, pullback = jax.vjp(lambda weights, inputs: forward(weights, inputs, seq_pos), params, source)
        grads, grad_in = pullback(grad_out)
        running = jax.tree.map(lambda first_term, second_term: first_term + second_term, running, grads)
        return (running, (result, grad_in))
    zeros_all = jax.tree.map(jnp.zeros_like, params)
    grads, (results, grad_inputs) = lax.scan(one_sequence, zeros_all, (sources, cotangents, positions))
    return (results.reshape(TOKENS, D).astype(jnp.bfloat16), grad_inputs.reshape(TOKENS, D).astype(jnp.bfloat16), grads[0], grads[1], grads[2], grads[3], grads[4], grads[5], grads[6], grads[7])
```

```python
import jax
import jax.numpy as jnp
from jax import lax
from jax.sharding import PartitionSpec as P

HEADS = 12
KV_HEADS = 2
HEAD = 128


norm_eps = 1e-06
rope_base = 1000000.0
masked_score = -1e30


def rotary(positions, width):
    half_width = width // 2
    frequency = rope_base ** (-(jnp.arange(half_width, dtype=jnp.float32) * 2.0) / width)
    angles = positions.astype(jnp.float32)[:, None] * frequency[None, :]
    angles = jnp.concatenate([angles, angles], 1)
    return (jnp.cos(angles)[:, None, :], jnp.sin(angles)[:, None, :])


def turned(tensor):
    half_width = tensor.shape[-1] // 2
    return jnp.concatenate([-tensor[..., half_width:], tensor[..., :half_width]], -1)


def turned_back(tensor):
    half_width = tensor.shape[-1] // 2
    return jnp.concatenate([tensor[..., half_width:], -tensor[..., :half_width]], -1)


def key_positions(orders, start_row, count, block_rows):
    row_ids = start_row + jnp.arange(count, dtype=jnp.int32)
    owner_dev = row_ids // block_rows
    device_ids = jnp.arange(orders.shape[0], dtype=jnp.int32)
    chosen = jnp.sum(jnp.where(owner_dev[:, None] == device_ids[None, :], orders[None, :], 0), 1)
    return chosen * block_rows + row_ids % block_rows


def contract_rows(left_side, right_side):
    return lax.dot_general(
        left_side, right_side, (((0,), (0,)), ((), ())), preferred_element_type=jnp.float32
    )


def contract_cols(left_side, right_side):
    return lax.dot_general(
        left_side, right_side, (((1,), (1,)), ((), ())), preferred_element_type=jnp.float32
    )


def plus(left_side, right_side):
    return (left_side.astype(jnp.float32) + right_side.astype(jnp.float32)).astype(jnp.bfloat16)


def ctx_sums(chunks):
    if lax.axis_size("ctx") != 4:
        return [lax.psum(chunk, "ctx") for chunk in chunks]
    place = lax.axis_index("ctx")
    outer = (place == 0) | (place == 3)
    depth = 2
    count = len(chunks)
    totals, results = [], []
    for step in range(count + depth):
        coming = chunks[step] if step < count else None
        going = totals[step - depth] if step >= depth else None
        if coming is None or going is None or coming.shape == going.shape:
            if going is None:
                payload = coming
            elif coming is None:
                payload = going
            else:
                payload = jnp.where(outer, coming, going)
            swapped = lax.ppermute(payload, "ctx", [(0, 1), (1, 0), (2, 3), (3, 2)])
            inward = outward = swapped
        else:
            inward = lax.ppermute(coming, "ctx", [(0, 1), (3, 2)])
            outward = lax.ppermute(going, "ctx", [(1, 0), (2, 3)])
        if going is not None:
            results.append(jnp.where(outer, outward, going))
        if coming is not None:
            pair_sum = plus(coming, inward)
            across = lax.ppermute(pair_sum, "ctx", [(1, 2), (2, 1)])
            totals.append(plus(pair_sum, across))
    return results


def local(
    tokens_in,
    block_order,
    norm_attn,
    w_qkv,
    b_qkv,
    w_out,
    norm_mlp,
    w_gate,
    w_up,
    w_down,
    cotangent,
):
    block_rows, width = tokens_in.shape
    shard_count = lax.axis_size("fsdp")
    context_count = lax.axis_size("ctx")
    seq_length = block_rows * context_count
    orders = block_order[0]
    context_index = lax.axis_index("ctx")
    shard_index = lax.axis_index("fsdp")
    own_block = jnp.sum(
        jnp.where(jnp.arange(context_count, dtype=jnp.int32) == context_index, orders, 0)
    )
    query_pos = own_block * block_rows + jnp.arange(block_rows, dtype=jnp.int32)
    query_top = own_block * block_rows + block_rows - 1
    cosine, sine_part = rotary(query_pos, HEAD)
    group_size = HEADS // KV_HEADS
    q_width = HEADS * HEAD
    k_width = KV_HEADS * HEAD
    score_scale = HEAD ** (-0.5)
    source = tokens_in.astype(jnp.float32)
    shard_rows = w_gate.shape[0]
    ff_cols = w_gate.shape[1] // shard_count

    qkv_all = lax.all_gather(w_qkv, "fsdp", axis=0, tiled=True)
    vectors = lax.all_gather(jnp.concatenate([norm_attn, norm_mlp, b_qkv]), "fsdp", axis=0)
    gain_attn = vectors[:, :shard_rows].reshape(-1).astype(jnp.float32)
    gain_mlp = vectors[:, shard_rows : 2 * shard_rows].reshape(-1).astype(jnp.float32)
    bias_all = vectors[:, 2 * shard_rows :].reshape(-1).astype(jnp.float32)

    def to_columns(weight):
        parts = weight.reshape(shard_rows, shard_count, ff_cols).transpose(1, 0, 2)
        return lax.all_to_all(parts, "fsdp", 0, 0).reshape(width, ff_cols)

    gate_cols = to_columns(w_gate)
    up_cols = to_columns(w_up)
    out_all = lax.all_gather(w_out, "fsdp", axis=0, tiled=True)
    cot_all = lax.all_gather(cotangent, "fsdp", axis=0, tiled=True)

    scale_one = lax.rsqrt(jnp.mean(source * source, -1, keepdims=True) + norm_eps)
    normed = (source * scale_one * gain_attn).astype(jnp.bfloat16)
    projected = jnp.dot(normed, qkv_all, preferred_element_type=jnp.float32) + bias_all
    query = projected[:, :q_width].reshape(block_rows, HEADS, HEAD)
    key_heads = projected[:, q_width : q_width + k_width].reshape(block_rows, KV_HEADS, HEAD)
    query = (
        (query * cosine + turned(query) * sine_part)
        .astype(jnp.bfloat16)
        .reshape(block_rows, KV_HEADS, group_size, HEAD)
    )
    key_heads = (
        (key_heads * cosine + turned(key_heads) * sine_part)
        .astype(jnp.bfloat16)
        .reshape(block_rows, k_width)
    )
    keys_values = jnp.concatenate(
        [key_heads, projected[:, q_width + k_width :].astype(jnp.bfloat16)], 1
    )

    def scores_of(key_rows, key_pos):
        raw_scores = (
            jnp.einsum("qhgd,khd->qhgk", query, key_rows, preferred_element_type=jnp.float32)
            * score_scale
        )
        visible = key_pos[None, None, None, :] <= query_pos[:, None, None, None]
        return (jnp.where(visible, raw_scores, masked_score), visible)

    start_state = (
        jnp.full((block_rows, KV_HEADS, group_size), masked_score, jnp.float32),
        jnp.zeros((block_rows, KV_HEADS, group_size), jnp.float32),
        jnp.zeros((block_rows, KV_HEADS, group_size, HEAD), jnp.float32),
    )
    carry_state = start_state
    shard_piece = lax.all_gather(keys_values, "ctx", axis=0, tiled=True)
    count = shard_piece.shape[0]
    sub_rows = min(count, 512)
    for offset in range(0, count, sub_rows):
        subpiece = shard_piece[offset : offset + sub_rows]
        key_pos = key_positions(orders, jnp.int32(offset), subpiece.shape[0], block_rows)

        def update(state_now):
            run_max, run_sum, accum = state_now
            key_rows = subpiece[:, :k_width].reshape(-1, KV_HEADS, HEAD)
            value_rows = subpiece[:, k_width:].reshape(-1, KV_HEADS, HEAD)
            scores, visible = scores_of(key_rows, key_pos)
            new_max = jnp.maximum(run_max, jnp.max(scores, -1))
            factor = jnp.exp(run_max - new_max)
            weights = jnp.where(visible, jnp.exp(scores - new_max[..., None]), 0.0)
            run_sum = run_sum * factor + jnp.sum(weights, -1)
            accum = accum * factor[..., None] + jnp.einsum(
                "qhgk,khd->qhgd",
                weights.astype(jnp.bfloat16),
                value_rows,
                preferred_element_type=jnp.float32,
            )
            return (new_max, run_sum, accum)

        carry_state = lax.cond(
            jnp.min(key_pos) <= query_top, update, lambda same_state: same_state, carry_state
        )
    run_max, run_sum, accum = carry_state
    log_total = run_max + jnp.log(run_sum)
    mixed_full = (accum / run_sum[..., None]).reshape(block_rows, q_width)
    mixed = mixed_full.astype(jnp.bfloat16)
    hidden = source + jnp.dot(mixed, out_all, preferred_element_type=jnp.float32)
    scale_two = lax.rsqrt(jnp.mean(hidden * hidden, -1, keepdims=True) + norm_eps)
    normed_two = (hidden * scale_two * gain_mlp).astype(jnp.bfloat16)

    normed_all = lax.all_gather(normed_two, "fsdp", axis=0, tiled=True)
    gate_value = jnp.dot(normed_all, gate_cols, preferred_element_type=jnp.float32)
    up_value = jnp.dot(normed_all, up_cols, preferred_element_type=jnp.float32)
    sigmoid_gate = jax.nn.sigmoid(gate_value)
    swished = gate_value * sigmoid_gate
    activation = (swished * up_value).astype(jnp.bfloat16)
    grad_act = contract_cols(cot_all, w_down)
    slope = sigmoid_gate * (1.0 + gate_value * (1.0 - sigmoid_gate))
    grad_gate = (grad_act * up_value * slope).astype(jnp.bfloat16)
    grad_up = (grad_act * swished).astype(jnp.bfloat16)
    grad_terms = contract_cols(grad_gate, gate_cols) + contract_cols(grad_up, up_cols)
    part_grad = lax.psum_scatter(
        grad_terms.astype(jnp.bfloat16), "fsdp", scatter_dimension=0, tiled=True
    ).astype(jnp.float32)
    down_terms = contract_rows(activation, cot_all).astype(jnp.bfloat16)

    def to_rows(terms):
        parts = terms.astype(jnp.bfloat16).reshape(shard_count, shard_rows, ff_cols)
        return lax.all_to_all(parts, "fsdp", 0, 0)

    gate_terms = to_rows(contract_rows(normed_all, grad_gate))
    up_terms = to_rows(contract_rows(normed_all, grad_up))
    mlp_terms = jnp.dot(activation, w_down, preferred_element_type=jnp.float32)
    mlp_out = lax.psum_scatter(
        mlp_terms.astype(jnp.bfloat16), "fsdp", scatter_dimension=0, tiled=True
    ).astype(jnp.float32)
    out_tokens = (hidden + mlp_out).astype(jnp.bfloat16)

    grad_out = cotangent.astype(jnp.float32)
    scaled_two = part_grad * gain_mlp
    grad_hidden = (
        grad_out
        + scale_two * scaled_two
        - hidden * scale_two**3 * jnp.mean(hidden * scaled_two, -1, keepdims=True)
    )
    gain_mlp_local = jnp.sum(part_grad * hidden * scale_two, 0)
    grad_branch = grad_hidden.astype(jnp.bfloat16)
    grad_mixed = contract_cols(grad_branch, out_all).astype(jnp.bfloat16)
    grad_heads = grad_mixed.reshape(block_rows, KV_HEADS, group_size, HEAD)
    row_delta = jnp.sum(
        grad_heads.astype(jnp.float32) * mixed_full.reshape(block_rows, KV_HEADS, group_size, HEAD),
        -1,
    )
    start_back = (
        jnp.zeros((block_rows, KV_HEADS, group_size, HEAD), jnp.float32),
        jnp.zeros((seq_length, 2 * k_width), jnp.float32),
    )
    carry_state = start_back
    for offset in range(0, count, sub_rows):
        attend_subpiece = shard_piece[offset : offset + sub_rows]
        attend_key_pos = key_positions(
            orders, jnp.int32(offset), attend_subpiece.shape[0], block_rows
        )

        def update(state_now):
            grad_query, kv_terms = state_now
            key_rows = attend_subpiece[:, :k_width].reshape(-1, KV_HEADS, HEAD)
            value_rows = attend_subpiece[:, k_width:].reshape(-1, KV_HEADS, HEAD)
            scores, visible = scores_of(key_rows, attend_key_pos)
            probability = jnp.where(visible, jnp.exp(scores - log_total[..., None]), 0.0)
            grad_probs = jnp.einsum(
                "qhgd,khd->qhgk", grad_heads, value_rows, preferred_element_type=jnp.float32
            )
            grad_scores = (probability * (grad_probs - row_delta[..., None]) * score_scale).astype(
                jnp.bfloat16
            )
            grad_query = grad_query + jnp.einsum(
                "qhgk,khd->qhgd", grad_scores, key_rows, preferred_element_type=jnp.float32
            )
            grad_keys = jnp.einsum(
                "qhgk,qhgd->khd", grad_scores, query, preferred_element_type=jnp.float32
            )
            grad_values = jnp.einsum(
                "qhgk,qhgd->khd",
                probability.astype(jnp.bfloat16),
                grad_heads,
                preferred_element_type=jnp.float32,
            )
            new_terms = jnp.concatenate(
                [grad_keys.reshape(-1, k_width), grad_values.reshape(-1, k_width)], 1
            )
            earlier = kv_terms[offset : offset + new_terms.shape[0]]
            kv_terms = lax.dynamic_update_slice_in_dim(kv_terms, earlier + new_terms, offset, 0)
            return (grad_query, kv_terms)

        carry_state = lax.cond(
            jnp.min(attend_key_pos) <= query_top, update, lambda same_state: same_state, carry_state
        )
    grad_query, kv_terms = carry_state
    grad_kv = lax.psum_scatter(
        kv_terms.astype(jnp.bfloat16), "ctx", scatter_dimension=0, tiled=True
    ).astype(jnp.float32)
    grad_query = grad_query.reshape(block_rows, HEADS, HEAD)
    grad_query = grad_query * cosine + turned_back(grad_query * sine_part)
    grad_key = grad_kv[:, :k_width].reshape(block_rows, KV_HEADS, HEAD)
    grad_key = grad_key * cosine + turned_back(grad_key * sine_part)
    grad_projected = jnp.concatenate(
        [
            grad_query.reshape(block_rows, q_width),
            grad_key.reshape(block_rows, k_width),
            grad_kv[:, k_width:],
        ],
        1,
    ).astype(jnp.bfloat16)
    bias_local = jnp.sum(grad_projected.astype(jnp.float32), 0)
    grad_normed = contract_cols(grad_projected, qkv_all)
    scaled_one = grad_normed * gain_attn
    grad_tokens = (
        grad_hidden
        + scale_one * scaled_one
        - source * scale_one**3 * jnp.mean(source * scaled_one, -1, keepdims=True)
    ).astype(jnp.bfloat16)
    gain_attn_local = jnp.sum(grad_normed * source * scale_one, 0)

    def to_owner(terms):
        return lax.psum_scatter(
            terms.astype(jnp.bfloat16), "fsdp", scatter_dimension=0, tiled=True
        )

    out_terms = to_owner(contract_rows(mixed, grad_branch))
    qkv_terms = to_owner(contract_rows(normed, grad_projected))

    down_cuts, col_cuts = 5, 4
    down_step, col_step = down_terms.shape[0] // down_cuts, shard_count // col_cuts
    chunks = [down_terms[i * down_step : (i + 1) * down_step] for i in range(down_cuts)]
    chunks += [gate_terms[i * col_step : (i + 1) * col_step] for i in range(col_cuts)]
    chunks += [up_terms[i * col_step : (i + 1) * col_step] for i in range(col_cuts)]
    chunks += [out_terms, qkv_terms]
    sums = ctx_sums(chunks)

    def to_output(parts):
        whole = jnp.concatenate(parts).astype(jnp.float32)
        return whole.transpose(1, 0, 2).reshape(shard_rows, shard_count * ff_cols)

    grad_down = jnp.concatenate(sums[:down_cuts]).astype(jnp.float32)
    grad_gate_w = to_output(sums[down_cuts : down_cuts + col_cuts])
    grad_up_w = to_output(sums[down_cuts + col_cuts : down_cuts + 2 * col_cuts])
    grad_out_w = sums[-2].astype(jnp.float32)
    grad_qkv_w = sums[-1].astype(jnp.float32)

    small = lax.psum(
        jnp.concatenate([gain_attn_local, gain_mlp_local, bias_local]), ("fsdp", "ctx")
    )

    def own_part(start, size):
        part = size // shard_count
        return lax.dynamic_slice_in_dim(small, start + shard_index * part, part, 0)

    return (
        out_tokens,
        grad_tokens,
        own_part(0, width),
        grad_qkv_w,
        own_part(2 * width, bias_all.shape[0]),
        grad_out_w,
        own_part(width, width),
        grad_gate_w,
        grad_up_w,
        grad_down,
    )


def solution(mesh):
    in_specs = (
        P(("fsdp", "ctx"), None),
        P("fsdp", None),
        P("fsdp"),
        P("fsdp", None),
        P("fsdp"),
        P("fsdp", None),
        P("fsdp"),
        P("fsdp", None),
        P("fsdp", None),
        P("fsdp", None),
        P(("fsdp", "ctx"), None),
    )
    out_specs = (
        P(("fsdp", "ctx"), None),
        P(("fsdp", "ctx"), None),
        P("fsdp"),
        P("fsdp", None),
        P("fsdp"),
        P("fsdp", None),
        P("fsdp"),
        P("fsdp", None),
        P("fsdp", None),
        P("fsdp", None),
    )
    return jax.shard_map(local, mesh=mesh, in_specs=in_specs, out_specs=out_specs, check_vma=False)
```

```python
import jax
import jax.numpy as jnp
from jax import lax
from jax.experimental import pallas as pl
from jax.experimental.pallas import tpu as pltpu
from jax.sharding import PartitionSpec as P

HEADS = 12
KV_HEADS = 2
HEAD = 128
GROUP = HEADS // KV_HEADS
Q_WIDTH = HEADS * HEAD
K_WIDTH = KV_HEADS * HEAD

norm_eps = 1e-06
rope_base = 1000000.0
masked_score = -1e30
score_scale = HEAD ** (-0.5)
score_scale_two = score_scale * 1.4426950408889634
bf16 = jnp.bfloat16
f32 = jnp.float32
light = pl.CostEstimate(flops=1 << 20, bytes_accessed=1 << 16, transcendentals=0)


def dot(left_side, right_side, left_dim, right_dim):
    return lax.dot_general(
        left_side,
        right_side,
        (((left_dim,), (right_dim,)), ((), ())),
        preferred_element_type=f32,
    )


def kernel_params(mib):
    return pltpu.CompilerParams(vmem_limit_bytes=mib * 1024 * 1024)


def padded(size):
    return (size + 127) // 128 * 128


def whole(shape):
    return pl.BlockSpec(shape, lambda *_: (0,) * len(shape))


def split_columns(weight, shard_count):
    rows, width = weight.shape
    cols = width // shard_count
    full = padded(cols)
    step = 48 if rows % 48 == 0 else rows

    def kernel(in_ref, out_ref):
        for shard in range(shard_count):
            out_ref[shard, :, :cols] = in_ref[:, shard * cols : (shard + 1) * cols]
            if full > cols:
                out_ref[shard, :, cols:] = jnp.zeros((step, full - cols), weight.dtype)

    return pl.pallas_call(
        kernel,
        grid=(rows // step,),
        in_specs=[pl.BlockSpec((step, width), lambda i: (i, 0))],
        out_specs=pl.BlockSpec((shard_count, step, full), lambda i: (0, i, 0)),
        out_shape=jax.ShapeDtypeStruct((shard_count, rows, full), weight.dtype),
        compiler_params=kernel_params(32),
        cost_estimate=light,
    )(weight)


def merge_columns(parts, cols):
    shards, rows, full = parts.shape
    width = shards * cols
    step = 48 if rows % 48 == 0 else rows

    def kernel(in_ref, out_ref):
        for shard in range(shards):
            part = in_ref[shard, :, :cols]
            out_ref[:, shard * cols : (shard + 1) * cols] = part.astype(f32)

    return pl.pallas_call(
        kernel,
        grid=(rows // step,),
        in_specs=[pl.BlockSpec((shards, step, full), lambda i: (0, i, 0))],
        out_specs=pl.BlockSpec((step, width), lambda i: (i, 0)),
        out_shape=jax.ShapeDtypeStruct((rows, width), f32),
        compiler_params=kernel_params(40),
        cost_estimate=light,
    )(parts)


def project(tokens_in, gain, weights, bias, cosine, sine):
    rows, width = tokens_in.shape
    tile = K_WIDTH
    query_steps = Q_WIDTH // tile

    def kernel(x_ref, gain_ref, w_ref, bias_ref, cos_ref, sin_ref, normed_ref, q_ref, kv_ref):
        step = pl.program_id(0)

        @pl.when(step == 0)
        def _():
            source = x_ref[...].astype(f32)
            scale = lax.rsqrt(jnp.mean(source * source, -1, keepdims=True) + norm_eps)
            normed_ref[...] = (source * scale * gain_ref[...]).astype(bf16)

        out = dot(normed_ref[...], w_ref[...], 1, 0) + bias_ref[...]
        heads = []
        for head in range(tile // HEAD):
            part = out[:, head * HEAD : (head + 1) * HEAD]
            turned = part * cos_ref[...] + pltpu.roll(part, HEAD // 2, 1) * sin_ref[...]
            heads.append(jnp.where(step <= query_steps, turned, part).astype(bf16))

        @pl.when(step < query_steps)
        def _():
            for head, value in enumerate(heads):
                q_ref[:, head * HEAD : (head + 1) * HEAD] = value

        @pl.when(step >= query_steps)
        def _():
            for head, value in enumerate(heads):
                kv_ref[:, head * HEAD : (head + 1) * HEAD] = value

    return pl.pallas_call(
        kernel,
        grid=(query_steps + 2,),
        in_specs=[
            whole((rows, width)),
            whole((1, width)),
            pl.BlockSpec((width, tile), lambda i: (0, i)),
            pl.BlockSpec((1, tile), lambda i: (0, i)),
            whole((rows, HEAD)),
            whole((rows, HEAD)),
        ],
        out_specs=[
            whole((rows, width)),
            pl.BlockSpec((rows, tile), lambda i: (0, jnp.minimum(i, query_steps - 1))),
            pl.BlockSpec((rows, tile), lambda i: (0, jnp.maximum(i - query_steps, 0))),
        ],
        out_shape=[
            jax.ShapeDtypeStruct((rows, width), bf16),
            jax.ShapeDtypeStruct((rows, Q_WIDTH), bf16),
            jax.ShapeDtypeStruct((rows, 2 * K_WIDTH), bf16),
        ],
        compiler_params=kernel_params(32),
        cost_estimate=light,
    )(tokens_in, gain, weights, bias, cosine, sine)


def fill_bias(info_ref, bias_ref, count, rows):
    query_pos = info_ref[0] * rows + lax.broadcasted_iota(jnp.int32, (rows, rows), 1)
    for piece in range(count):
        key_pos = info_ref[1 + piece] * rows + lax.broadcasted_iota(jnp.int32, (rows, rows), 0)
        bias_ref[piece * rows : (piece + 1) * rows, :] = jnp.where(
            key_pos <= query_pos, 0.0, masked_score
        )


def attend(info, query, kv_pieces):
    rows = query.shape[0]
    count = len(kv_pieces)

    def kernel(info_ref, q_ref, *refs):
        keys, values = refs[:count], refs[count : 2 * count]
        mixed_ref, total_ref, bias_ref, score_ref = refs[2 * count :]

        @pl.when(pl.program_id(0) == 0)
        def _():
            fill_bias(info_ref, bias_ref, count, rows)

        q = q_ref[...]
        top = None
        for piece in range(count):
            at = slice(piece * rows, (piece + 1) * rows)
            score = dot(keys[piece][...], q, 1, 1) * score_scale_two + bias_ref[at, :]
            score_ref[at, :] = score
            peak = jnp.max(score, 0, keepdims=True)
            top = peak if top is None else jnp.maximum(top, peak)
        total = jnp.zeros((1, rows), f32)
        mixed = jnp.zeros((HEAD, rows), f32)
        for piece in range(count):
            weight = jnp.exp2(score_ref[piece * rows : (piece + 1) * rows, :] - top)
            total += jnp.sum(weight, 0, keepdims=True)
            mixed += dot(values[piece][...], weight.astype(bf16), 0, 0)
        mixed_ref[...] = (mixed / total).T.astype(bf16)
        total_ref[0] = top + jnp.log2(total)

    key_spec = pl.BlockSpec((rows, HEAD), lambda h: (0, h // GROUP))
    value_spec = pl.BlockSpec((rows, HEAD), lambda h: (0, KV_HEADS + h // GROUP))
    head_spec = pl.BlockSpec((rows, HEAD), lambda h: (0, h))
    return pl.pallas_call(
        kernel,
        grid=(HEADS,),
        in_specs=[pl.BlockSpec(memory_space=pltpu.SMEM), head_spec]
        + [key_spec] * count
        + [value_spec] * count,
        out_specs=[head_spec, pl.BlockSpec((1, 1, rows), lambda h: (h, 0, 0))],
        out_shape=[
            jax.ShapeDtypeStruct((rows, Q_WIDTH), bf16),
            jax.ShapeDtypeStruct((HEADS, 1, rows), f32),
        ],
        scratch_shapes=[pltpu.VMEM((count * rows, rows), f32)] * 2,
        compiler_params=kernel_params(32),
        cost_estimate=light,
    )(info, query, *kv_pieces, *kv_pieces)


def attend_back(info, query, grad_mixed, totals, cosine, sine, kv_pieces):
    rows = query.shape[0]
    count = len(kv_pieces)

    def kernel(info_ref, q_ref, g_ref, total_ref, cos_ref, sin_ref, *refs):
        keys, values = refs[:count], refs[count : 2 * count]
        dq_ref = refs[2 * count]
        kv_refs = refs[2 * count + 1 : 3 * count + 1]
        bias_ref, p_ref, dp_ref, sum_ref = refs[3 * count + 1 :]
        head = pl.program_id(0)

        @pl.when(head == 0)
        def _():
            fill_bias(info_ref, bias_ref, count, rows)

        @pl.when(head % GROUP == 0)
        def _():
            sum_ref[...] = jnp.zeros_like(sum_ref)

        q, g, total = q_ref[...], g_ref[...], total_ref[0]
        delta = jnp.zeros((1, rows), f32)
        for piece in range(count):
            at = slice(piece * rows, (piece + 1) * rows)
            score = dot(keys[piece][...], q, 1, 1) * score_scale_two + bias_ref[at, :]
            p = jnp.exp2(score - total)
            dp = dot(values[piece][...], g, 1, 1)
            p_ref[at, :] = p
            dp_ref[at, :] = dp
            delta += jnp.sum(p * dp, 0, keepdims=True)
        dq = jnp.zeros((HEAD, rows), f32)
        for piece in range(count):
            at = slice(piece * rows, (piece + 1) * rows)
            p = p_ref[at, :]
            ds = (p * (dp_ref[at, :] - delta) * score_scale).astype(bf16)
            dq += dot(keys[piece][...], ds, 0, 0)
            sum_ref[piece, 0] += dot(ds, q, 1, 0)
            sum_ref[piece, 1] += dot(p.astype(bf16), g, 1, 0)
        dq = dq.T
        dq_ref[...] = (dq * cos_ref[...] - pltpu.roll(dq, HEAD // 2, 1) * sin_ref[...]).astype(bf16)

        @pl.when(head % GROUP == GROUP - 1)
        def _():
            for piece in range(count):
                kv_refs[piece][...] = sum_ref[piece].astype(bf16)

    key_spec = pl.BlockSpec((rows, HEAD), lambda h: (0, h // GROUP))
    value_spec = pl.BlockSpec((rows, HEAD), lambda h: (0, KV_HEADS + h // GROUP))
    head_spec = pl.BlockSpec((rows, HEAD), lambda h: (0, h))
    return pl.pallas_call(
        kernel,
        grid=(HEADS,),
        in_specs=[
            pl.BlockSpec(memory_space=pltpu.SMEM),
            head_spec,
            head_spec,
            pl.BlockSpec((1, 1, rows), lambda h: (h, 0, 0)),
            whole((rows, HEAD)),
            whole((rows, HEAD)),
        ]
        + [key_spec] * count
        + [value_spec] * count,
        out_specs=[head_spec]
        + [pl.BlockSpec((2, rows, HEAD), lambda h: (0, 0, h // GROUP))] * count,
        out_shape=[jax.ShapeDtypeStruct((rows, Q_WIDTH), bf16)]
        + [jax.ShapeDtypeStruct((2, rows, K_WIDTH), bf16)] * count,
        scratch_shapes=[pltpu.VMEM((count * rows, rows), f32)] * 3
        + [pltpu.VMEM((count, 2, rows, HEAD), f32)],
        compiler_params=kernel_params(32),
        cost_estimate=light,
    )(info, query, grad_mixed, totals, cosine, sine, *kv_pieces, *kv_pieces)


def once(shape):
    return pl.BlockSpec(shape, lambda *_: (0,) * len(shape), pipeline_mode=pl.Buffered(1))


def token_rows(count, rows):
    return 2 * rows if count % (2 * rows) == 0 else rows


def feed_forward(normed, cotangent, gate_cols, up_cols, units_here, rows, cuts):
    count, width = normed.shape
    units = gate_cols.shape[1]
    rows = token_rows(count, rows)
    steps, part, tile = count // rows, units_here // cuts, 256

    def kernel(x_ref, c_ref, wg_ref, wu_ref, act_ref, to_gate_ref, to_up_ref, *refs):
        down_refs, turned_ref = refs[:cuts], refs[cuts]
        step = pl.program_id(0)

        @pl.when(step < steps)
        def _():
            x = x_ref[...]
            gate = dot(x, wg_ref[...], 1, 0)
            up = dot(x, wu_ref[...], 1, 0)
            sigmoid = jax.nn.sigmoid(gate)
            swished = gate * sigmoid
            act = (swished * up).astype(bf16)
            act_ref[...] = act
            turned_ref[:, pl.ds(pl.multiple_of(step * rows, rows), rows)] = act.T
            to_up_ref[...] = swished.astype(bf16)
            to_gate_ref[...] = (up * sigmoid * (1.0 + gate * (1.0 - sigmoid))).astype(bf16)

        @pl.when(step >= steps)
        def _():
            for cut, down_ref in enumerate(down_refs):
                turned = turned_ref[cut * part : (cut + 1) * part, :]
                down_ref[...] = dot(turned, c_ref[...], 1, 0).astype(bf16)

    def early(i):
        return (jnp.minimum(i, steps - 1), 0)

    def late(i):
        return (0, jnp.maximum(i - steps, 0))

    return pl.pallas_call(
        kernel,
        grid=(steps + width // tile,),
        in_specs=[
            pl.BlockSpec((rows, width), early),
            pl.BlockSpec((count, tile), late),
            once((width, units)),
            once((width, units)),
        ],
        out_specs=[pl.BlockSpec((rows, units), early)] * 3 + [pl.BlockSpec((part, tile), late)] * cuts,
        out_shape=[jax.ShapeDtypeStruct((count, units), bf16)] * 3
        + [jax.ShapeDtypeStruct((part, width), bf16)] * cuts,
        scratch_shapes=[pltpu.VMEM((units, count), bf16)],
        compiler_params=kernel_params(58),
        cost_estimate=light,
    )(normed, cotangent, gate_cols, up_cols)


def unit_grads(cotangent, down_rows, to_gate, to_up, rows):
    count, width = cotangent.shape
    units = down_rows.shape[0]
    rows = token_rows(count, rows)

    def kernel(c_ref, wd_ref, tg_ref, tu_ref, dg_ref, du_ref):
        grad_act = dot(c_ref[...], wd_ref[...], 1, 1)
        dg_ref[...] = (grad_act * tg_ref[...].astype(f32)).astype(bf16)
        du_ref[...] = (grad_act * tu_ref[...].astype(f32)).astype(bf16)

    unit_spec = pl.BlockSpec((rows, units), lambda i: (i, 0))
    return pl.pallas_call(
        kernel,
        grid=(count // rows,),
        in_specs=[
            pl.BlockSpec((rows, width), lambda i: (i, 0)),
            once((units, width)),
            unit_spec,
            unit_spec,
        ],
        out_specs=[unit_spec] * 2,
        out_shape=[jax.ShapeDtypeStruct((count, units), bf16)] * 2,
        compiler_params=kernel_params(58),
        cost_estimate=light,
    )(cotangent, down_rows, to_gate, to_up)


def through_columns(grad_gate, grad_up, gate_cols, up_cols, rows):
    count, units = grad_gate.shape
    width = gate_cols.shape[0]
    rows = token_rows(count, rows)

    def kernel(dg_ref, du_ref, wg_ref, wu_ref, out_ref):
        out = dot(dg_ref[...], wg_ref[...], 1, 1) + dot(du_ref[...], wu_ref[...], 1, 1)
        out_ref[...] = out.astype(bf16)

    unit_spec = pl.BlockSpec((rows, units), lambda i: (i, 0))
    return pl.pallas_call(
        kernel,
        grid=(count // rows,),
        in_specs=[unit_spec, unit_spec, once((width, units)), once((width, units))],
        out_specs=pl.BlockSpec((rows, width), lambda i: (i, 0)),
        out_shape=jax.ShapeDtypeStruct((count, width), bf16),
        compiler_params=kernel_params(58),
        cost_estimate=light,
    )(grad_gate, grad_up, gate_cols, up_cols)


def column_grad(normed, grad, cuts):
    count, width = normed.shape
    units = grad.shape[1]
    tile = 256
    each = width // tile // cuts

    def kernel(x_ref, g_ref, *out_refs):
        step = pl.program_id(0)
        out = dot(x_ref[...].T, g_ref[...], 1, 0).astype(bf16)
        for cut, out_ref in enumerate(out_refs):

            @pl.when(step // each == cut)
            def _():
                out_ref[...] = out

    def cut_spec(cut):
        return pl.BlockSpec((tile, units), lambda i: (jnp.clip(i - cut * each, 0, each - 1), 0))

    return pl.pallas_call(
        kernel,
        grid=(width // tile,),
        in_specs=[pl.BlockSpec((count, tile), lambda i: (0, i)), once((count, units))],
        out_specs=[cut_spec(cut) for cut in range(cuts)],
        out_shape=[jax.ShapeDtypeStruct((width // cuts, units), bf16)] * cuts,
        compiler_params=kernel_params(58),
        cost_estimate=light,
    )(normed, grad)


def through_rows(activation, down_rows, rows):
    count, units = activation.shape
    width = down_rows.shape[1]
    rows = token_rows(count, rows)

    def kernel(act_ref, wd_ref, out_ref):
        out_ref[...] = dot(act_ref[...], wd_ref[...], 1, 0).astype(bf16)

    return pl.pallas_call(
        kernel,
        grid=(count // rows,),
        in_specs=[pl.BlockSpec((rows, units), lambda i: (i, 0)), once((units, width))],
        out_specs=pl.BlockSpec((rows, width), lambda i: (i, 0)),
        out_shape=jax.ShapeDtypeStruct((count, width), bf16),
        compiler_params=kernel_params(58),
        cost_estimate=light,
    )(activation, down_rows)


def rotary(positions):
    half = HEAD // 2
    frequency = rope_base ** (-(jnp.arange(half, dtype=f32) * 2.0) / HEAD)
    angles = positions.astype(f32)[:, None] * frequency[None, :]
    cosine, sine = jnp.cos(angles), jnp.sin(angles)
    return jnp.concatenate([cosine, cosine], 1), jnp.concatenate([-sine, sine], 1)


def fence(*values):
    return lax.optimization_barrier(values)


def added(left_side, right_side):
    def kernel(a_ref, b_ref, out_ref):
        out_ref[...] = (a_ref[...].astype(f32) + b_ref[...].astype(f32)).astype(out_ref.dtype)

    def one(a, b):
        steps = [n for n in (4, 5, 3, 2) if a.ndim == 2 and a.shape[0] % (16 * n) == 0]
        if not steps:
            return (a.astype(f32) + b.astype(f32)).astype(a.dtype)
        block = pl.BlockSpec((a.shape[0] // steps[0], a.shape[1]), lambda i: (i, 0))
        return pl.pallas_call(
            kernel,
            grid=(steps[0],),
            in_specs=[block] * 2,
            out_specs=block,
            out_shape=jax.ShapeDtypeStruct(a.shape, a.dtype),
            compiler_params=kernel_params(16),
            cost_estimate=light,
        )(a, b)

    return jax.tree.map(one, left_side, right_side)


class CtxLine:
    lead = 2

    def __init__(self):
        place = lax.axis_index("ctx")
        self.outer = (place == 0) | (place == 3)
        self.waiting = []
        self.chunks, self.inward, self.across, self.pair_sums = [], [], [], []
        self.totals, self.outward = [], []

    def add(self, chunks):
        self.waiting += list(chunks)
        self.send()

    def send(self):
        while self.waiting and len(self.chunks) < len(self.pair_sums) + self.lead:
            chunk = self.waiting.pop(0)
            self.chunks.append(chunk)
            self.inward.append(lax.ppermute(chunk, "ctx", [(0, 1), (3, 2)]))

    def round(self, *values):
        step = len(self.pair_sums)
        more = step < len(self.chunks)
        if more:
            self.inward[step], values = fence(self.inward[step], values)
            self.pair_sums.append(added(self.chunks[step], self.inward[step]))
        last = step - 1
        held = [
            (array, slice(max(at, 0), max(at + 1, 0)))
            for array, at in ((self.across, last), (self.outward, last - 1), (self.pair_sums, step))
        ]
        fenced, self.waiting, values = fence([array[at] for array, at in held], self.waiting, values)
        for (array, at), value in zip(held, fenced):
            array[at] = value
        if more:
            self.across.append(lax.ppermute(self.pair_sums[step], "ctx", [(1, 2), (2, 1)]))
        if step:
            total = added(self.pair_sums[last], self.across[last])
            self.totals.append(total)
            self.outward.append(lax.ppermute(total, "ctx", [(1, 0), (2, 3)]))
        self.send()
        return values

    def rest(self):
        while len(self.totals) < len(self.chunks):
            self.round()

    def sums(self, first, last):
        return jax.tree.map(
            lambda back, total: jnp.where(self.outer, back, total),
            self.outward[first:last],
            self.totals[first:last],
        )


def summed_in_plane(vector):
    size = lax.axis_size("fsdp")
    bit = 1
    while bit < size:
        vector = vector + lax.ppermute(vector, "fsdp", [(j, j ^ bit) for j in range(size)])
        bit *= 2
    return vector


def local(
    tokens_in,
    block_order,
    norm_attn,
    w_qkv,
    b_qkv,
    w_out,
    norm_mlp,
    w_gate,
    w_up,
    w_down,
    cotangent,
):
    rows, width = tokens_in.shape
    shards = lax.axis_size("fsdp")
    blocks = lax.axis_size("ctx")
    shard = lax.axis_index("fsdp")
    place = lax.axis_index("ctx")
    shard_rows = w_gate.shape[0]
    units = w_down.shape[0]
    orders = block_order[0]
    owners = jnp.concatenate([place[None], (place - jnp.arange(blocks)) % blocks])
    info = jnp.sum(
        jnp.where(owners[:, None] == jnp.arange(blocks)[None, :], orders[None, :], 0), 1
    ).astype(jnp.int32)
    cosine, sine = rotary(info[0] * rows + jnp.arange(rows, dtype=jnp.int32))

    def turn(parts):
        return lax.all_to_all(parts, "fsdp", 0, 0)

    qkv_all = lax.all_gather(w_qkv, "fsdp", axis=0, tiled=True)
    vectors = lax.all_gather(jnp.concatenate([norm_attn, norm_mlp, b_qkv]), "fsdp", axis=0)
    part = 2 * shard_rows // 3 // blocks
    shared = part * blocks
    weights = (w_gate, w_up)
    parts = jnp.concatenate(
        [lax.dynamic_slice_in_dim(weight, place * part, part, 0) for weight in weights]
    )
    vectors, parts = fence(vectors, split_columns(parts, shards))
    pieces = [turn(parts)]

    def ring(piece):
        return lax.ppermute(piece, "ctx", [(j, (j + 1) % blocks) for j in range(blocks)])

    pieces.append(ring(pieces[0]))
    full = padded(units)
    down_rows = jnp.concatenate([w_down, jnp.zeros((full - units, width), bf16)])
    direct = split_columns(jnp.concatenate([weight[shared:] for weight in weights]), shards)
    gain_attn = vectors[:, :shard_rows].reshape(1, -1).astype(f32)
    gain_mlp = vectors[:, shard_rows : 2 * shard_rows].reshape(1, -1).astype(f32)
    bias_all = vectors[:, 2 * shard_rows :].reshape(1, -1).astype(f32)
    qkv_all, pieces, direct, down_rows = fence(qkv_all, pieces, direct, down_rows)
    direct = turn(direct)
    out_all = lax.all_gather(w_out, "fsdp", axis=0, tiled=True)

    normed, query, keys_values = project(tokens_in, gain_attn, qkv_all, bias_all, cosine, sine)
    kv_pieces = [keys_values] + [
        lax.ppermute(keys_values, "ctx", [(j, (j + s) % blocks) for j in range(blocks)])
        for s in range(1, blocks)
    ]
    kv_pieces, pieces, own_cot = fence(kv_pieces, pieces, cotangent)
    for _ in range(2, blocks - 1):
        pieces.append(ring(pieces[-1]))
    mixed, totals = attend(info, query, kv_pieces)
    mixed, direct = fence(mixed, direct)
    source = tokens_in.astype(f32)
    hidden = source + dot(mixed, out_all, 1, 0)
    scale_two = lax.rsqrt(jnp.mean(hidden * hidden, -1, keepdims=True) + norm_eps)
    normed_two = (hidden * scale_two * gain_mlp).astype(bf16)

    normed_two, pieces = fence(normed_two, pieces)
    pieces.append(ring(pieces[-1]))
    normed_all = lax.all_gather(normed_two, "fsdp", axis=0, tiled=True)
    chips = range(0, shards, 2)
    own_pieces = [own_cot] + [
        lax.ppermute(own_cot, "fsdp", [(j, j ^ chip) for j in range(shards)]) for chip in chips[1:]
    ]
    own_pieces[1], pieces = fence(own_pieces[1], pieces)
    cot_pieces = []
    for chip, piece in zip(chips, own_pieces):
        other = lax.ppermute(piece, "fsdp", [(j, j ^ 1) for j in range(shards)])
        cot_pieces += [(chip, piece), (chip ^ 1, other)]
    cot_all = jnp.zeros((shards * rows, width), bf16)
    for bits, piece in cot_pieces:
        cot_all = lax.dynamic_update_slice_in_dim(cot_all, piece, (shard ^ bits) * rows, 0)
    columns = []
    for k in range(2):
        array = jnp.zeros((shards, shard_rows // part, part, full), bf16)
        rest = direct[:, k * (shard_rows - shared) : (k + 1) * (shard_rows - shared)]
        rest = rest.reshape(shards, -1, part, full)
        array = lax.dynamic_update_slice_in_dim(array, rest, blocks, 1)
        for s, piece in enumerate(pieces):
            piece = piece[:, None, k * part : (k + 1) * part]
            array = lax.dynamic_update_slice_in_dim(array, piece, (place - s) % blocks, 1)
        columns.append(array.reshape(width, full))
    gate_cols, up_cols = columns
    cuts = 2
    activation, to_gate, to_up, *down_terms = feed_forward(
        normed_all, cot_all, gate_cols, up_cols, units, rows, cuts
    )

    def to_rows(terms):
        return turn(terms.reshape(shards, shard_rows, full)).reshape(width, full)

    def merged(terms):
        return merge_columns(terms.reshape(shards, shard_rows, full), units)

    def to_owner(terms):
        return lax.psum_scatter(terms, "fsdp", scatter_dimension=0, tiled=True)

    def through_attention(part_grad):
        part_grad = part_grad.astype(f32)
        scaled = part_grad * gain_mlp
        grad_hidden = (
            cotangent.astype(f32)
            + scale_two * scaled
            - hidden * scale_two**3 * jnp.mean(hidden * scaled, -1, keepdims=True)
        )
        gain_terms = jnp.sum(part_grad * hidden * scale_two, 0)
        grad_branch = grad_hidden.astype(bf16)
        grad_mixed = dot(grad_branch, out_all, 1, 1).astype(bf16)
        grad_query, *kv_terms = attend_back(
            info, query, grad_mixed, totals, cosine, sine, kv_pieces
        )
        return grad_hidden, gain_terms, grad_branch, grad_query, *kv_terms

    def kv_exchange(kv_terms):
        return [
            lax.ppermute(kv_terms[s], "ctx", [(j, (j - s) % blocks) for j in range(blocks)])
            for s in range(1, blocks)
        ]

    def projected_grad(grad_query, own_terms, other_terms):
        grad_kv = own_terms.astype(f32)
        for terms in other_terms:
            grad_kv = grad_kv + terms.astype(f32)
        grad_key = grad_kv[0].reshape(rows, KV_HEADS, HEAD)
        rolled = jnp.concatenate([grad_key[..., HEAD // 2 :], grad_key[..., : HEAD // 2]], -1)
        grad_key = grad_key * cosine[:, None, :] - rolled * sine[:, None, :]
        return jnp.concatenate(
            [grad_query, grad_key.reshape(rows, K_WIDTH).astype(bf16), grad_kv[1].astype(bf16)], 1
        )

    def to_tokens(grad_projected, grad_hidden):
        scale_one = lax.rsqrt(jnp.mean(source * source, -1, keepdims=True) + norm_eps)
        grad_normed = dot(grad_projected, qkv_all, 1, 1)
        scaled = grad_normed * gain_attn
        grad_tokens = (
            grad_hidden
            + scale_one * scaled
            - source * scale_one**3 * jnp.mean(source * scaled, -1, keepdims=True)
        ).astype(bf16)
        bias_terms = jnp.sum(grad_projected.astype(f32), 0)
        return grad_tokens, jnp.sum(grad_normed * source * scale_one, 0), bias_terms

    def out_grad(mixed, grad_branch):
        return dot(mixed, grad_branch, 0, 0).astype(bf16)

    def own_sums(*terms):
        total = summed_in_plane(jnp.concatenate([t.reshape(shards, -1) for t in terms], 1))
        return lax.dynamic_index_in_dim(total, shard, 0, False)

    grad_gate, grad_up = unit_grads(cot_all, down_rows, to_gate, to_up, rows)
    mlp_grad = through_columns(grad_gate, grad_up, gate_cols, up_cols, rows)
    if blocks == 4:
        line = CtxLine()
        line.add(down_terms)
        mlp_grad, grad_gate, grad_up, act = line.round(
            mlp_grad, grad_gate, grad_up, activation
        )
        part_grad = to_owner(mlp_grad)
        gate_terms = column_grad(normed_all, grad_gate, cuts)
        (up_terms,) = column_grad(normed_all, grad_up, 1)
        mlp_terms = through_rows(act, down_rows, rows)
        gate_terms, up_terms, mlp_terms = line.round(gate_terms, up_terms, mlp_terms)
        line.add(gate_terms)
        up_terms = to_rows(up_terms)
        part_grad, mlp_terms = fence(part_grad, mlp_terms)
        mlp_out = to_owner(mlp_terms)
        grad_hidden, gain_mlp_terms, grad_branch, grad_query, *kv_terms = through_attention(
            part_grad
        )
        others = kv_exchange(kv_terms)
        out_terms = to_owner(out_grad(mixed, grad_branch))
        line.round()
        grad_query, up_terms = line.round(grad_query, up_terms)
        line.add([up_terms[: width // 2], up_terms[width // 2 :]])
        grad_projected = projected_grad(grad_query, kv_terms[0], others)
        qkv_terms = to_owner(dot(normed, grad_projected, 0, 0).astype(bf16))
        grad_projected, out_terms = line.round(grad_projected, out_terms)
        line.add([out_terms])
        grad_tokens, gain_attn_terms, bias_terms = to_tokens(grad_projected, grad_hidden)
        small = own_sums(gain_attn_terms, gain_mlp_terms, bias_terms)
        grad_tokens, small = line.round(grad_tokens, small)
        gate_terms = to_rows(jnp.concatenate(line.sums(cuts, 2 * cuts)))
        qkv_terms, mlp_out, hidden = line.round(qkv_terms, mlp_out, hidden)
        half = shard_rows // 2
        line.add([[qkv_terms[:half], small], [qkv_terms[half:]]])
        line.rest()
        down_sums = line.sums(0, cuts)
        up_terms = jnp.concatenate(line.sums(2 * cuts, 2 * cuts + 2))
        out_sum, (qkv_sum, small), (qkv_more,) = line.sums(2 * cuts + 2, 2 * cuts + 5)
        qkv_sum = jnp.concatenate([qkv_sum, qkv_more])
    else:
        part_grad = to_owner(mlp_grad)
        gate_terms = column_grad(normed_all, grad_gate, cuts)
        up_terms = column_grad(normed_all, grad_up, cuts)
        gate_terms, up_terms = (to_rows(jnp.concatenate(t)) for t in (gate_terms, up_terms))
        mlp_out = to_owner(through_rows(activation, down_rows, rows))
        grad_hidden, gain_mlp_terms, grad_branch, grad_query, *kv_terms = through_attention(
            part_grad
        )
        others = kv_exchange(kv_terms)
        out_terms = to_owner(out_grad(mixed, grad_branch))
        grad_projected = projected_grad(grad_query, kv_terms[0], others)
        qkv_terms = to_owner(dot(normed, grad_projected, 0, 0).astype(bf16))
        grad_tokens, gain_attn_terms, bias_terms = to_tokens(grad_projected, grad_hidden)
        small = own_sums(gain_attn_terms, gain_mlp_terms, bias_terms)
        down_sums, gate_terms, up_terms, out_sum, qkv_sum, small = lax.psum(
            (down_terms, gate_terms, up_terms, out_terms, qkv_terms, small), "ctx"
        )

    grad_down_w = jnp.concatenate(down_sums).astype(f32)
    grad_out_w = out_sum.astype(f32)
    grad_qkv_w = qkv_sum.astype(f32)
    out_tokens = (hidden + mlp_out.astype(f32)).astype(bf16)

    return (
        out_tokens,
        grad_tokens,
        small[:shard_rows],
        grad_qkv_w,
        small[2 * shard_rows :],
        grad_out_w,
        small[shard_rows : 2 * shard_rows],
        merged(gate_terms),
        merged(up_terms),
        grad_down_w,
    )


def solution(mesh):
    in_specs = (
        P(("fsdp", "ctx"), None),
        P("fsdp", None),
        P("fsdp"),
        P("fsdp", None),
        P("fsdp"),
        P("fsdp", None),
        P("fsdp"),
        P("fsdp", None),
        P("fsdp", None),
        P("fsdp", None),
        P(("fsdp", "ctx"), None),
    )
    out_specs = (
        P(("fsdp", "ctx"), None),
        P(("fsdp", "ctx"), None),
        P("fsdp"),
        P("fsdp", None),
        P("fsdp"),
        P("fsdp", None),
        P("fsdp"),
        P("fsdp", None),
        P("fsdp", None),
        P("fsdp", None),
    )
    return jax.shard_map(local, mesh=mesh, in_specs=in_specs, out_specs=out_specs, check_vma=False)
```

```python
import jax
import jax.numpy as jnp
from jax import lax
from jax.experimental import pallas as pl
from jax.experimental.pallas import tpu as pltpu
from jax.sharding import PartitionSpec as P

HEADS = 12
KV_HEADS = 2
HEAD = 128
GROUP = HEADS // KV_HEADS
Q_WIDTH = HEADS * HEAD
K_WIDTH = KV_HEADS * HEAD

norm_eps = 1e-06
rope_base = 1000000.0
masked_score = -1e30
score_scale = HEAD ** (-0.5)
score_scale_two = score_scale * 1.4426950408889634
bf16 = jnp.bfloat16
f32 = jnp.float32
light = pl.CostEstimate(flops=1 << 20, bytes_accessed=1 << 16, transcendentals=0)


def dot(left_side, right_side, left_dim, right_dim):
    return lax.dot_general(
        left_side,
        right_side,
        (((left_dim,), (right_dim,)), ((), ())),
        preferred_element_type=f32,
    )


def kernel_params(mib):
    return pltpu.CompilerParams(vmem_limit_bytes=mib * 1024 * 1024)


def padded(size):
    return (size + 127) // 128 * 128


def whole(shape):
    return pl.BlockSpec(shape, lambda *_: (0,) * len(shape))


def split_columns(weight, shard_count):
    rows, width = weight.shape
    cols = width // shard_count
    full = padded(cols)
    step = 48 if rows % 48 == 0 else rows

    def kernel(in_ref, out_ref):
        for shard in range(shard_count):
            out_ref[shard, :, :cols] = in_ref[:, shard * cols : (shard + 1) * cols]
            if full > cols:
                out_ref[shard, :, cols:] = jnp.zeros((step, full - cols), weight.dtype)

    return pl.pallas_call(
        kernel,
        grid=(rows // step,),
        in_specs=[pl.BlockSpec((step, width), lambda i: (i, 0))],
        out_specs=pl.BlockSpec((shard_count, step, full), lambda i: (0, i, 0)),
        out_shape=jax.ShapeDtypeStruct((shard_count, rows, full), weight.dtype),
        compiler_params=kernel_params(32),
        cost_estimate=light,
    )(weight)


def merge_columns(parts, cols):
    shards, rows, full = parts.shape
    width = shards * cols
    step = 48 if rows % 48 == 0 else rows

    def kernel(in_ref, out_ref):
        for shard in range(shards):
            part = in_ref[shard, :, :cols]
            out_ref[:, shard * cols : (shard + 1) * cols] = part.astype(f32)

    return pl.pallas_call(
        kernel,
        grid=(rows // step,),
        in_specs=[pl.BlockSpec((shards, step, full), lambda i: (0, i, 0))],
        out_specs=pl.BlockSpec((step, width), lambda i: (i, 0)),
        out_shape=jax.ShapeDtypeStruct((rows, width), f32),
        compiler_params=kernel_params(40),
        cost_estimate=light,
    )(parts)


def moved(moves, arrays, shapes):
    def kernel(at_ref, *refs):
        sources, targets, sems = refs[: len(arrays)], refs[len(arrays) : -1], refs[-1]
        copies = [
            pltpu.make_async_copy(
                sources[source].at[where], targets[target].at[there], sems.at[i]
            )
            for i, (source, where, target, there) in enumerate(moves(at_ref[0], at_ref[1]))
        ]
        for copy in copies:
            copy.start()
        for copy in copies:
            copy.wait()

    anywhere = pl.BlockSpec(memory_space=pl.ANY)
    at = jnp.stack([lax.axis_index("ctx"), lax.axis_index("fsdp")]).astype(jnp.int32)
    return pl.pallas_call(
        kernel,
        in_specs=[pl.BlockSpec(memory_space=pltpu.SMEM)] + [anywhere] * len(arrays),
        out_specs=[anywhere] * len(shapes),
        out_shape=[jax.ShapeDtypeStruct(shape, bf16) for shape in shapes],
        scratch_shapes=[pltpu.SemaphoreType.DMA((len(moves(0, 0)),))],
        compiler_params=kernel_params(16),
        cost_estimate=light,
    )(at, *arrays)


def project(tokens_in, gain, weights, bias, cosine, sine):
    rows, width = tokens_in.shape
    tile = K_WIDTH
    query_steps = Q_WIDTH // tile

    def kernel(x_ref, gain_ref, w_ref, bias_ref, cos_ref, sin_ref, normed_ref, q_ref, kv_ref):
        step = pl.program_id(0)

        @pl.when(step == 0)
        def _():
            source = x_ref[...].astype(f32)
            scale = lax.rsqrt(jnp.mean(source * source, -1, keepdims=True) + norm_eps)
            normed_ref[...] = (source * scale * gain_ref[...]).astype(bf16)

        out = dot(normed_ref[...], w_ref[...], 1, 0) + bias_ref[...]
        heads = []
        for head in range(tile // HEAD):
            part = out[:, head * HEAD : (head + 1) * HEAD]
            turned = part * cos_ref[...] + pltpu.roll(part, HEAD // 2, 1) * sin_ref[...]
            heads.append(jnp.where(step <= query_steps, turned, part).astype(bf16))

        @pl.when(step < query_steps)
        def _():
            for head, value in enumerate(heads):
                q_ref[:, head * HEAD : (head + 1) * HEAD] = value

        @pl.when(step >= query_steps)
        def _():
            for head, value in enumerate(heads):
                kv_ref[:, head * HEAD : (head + 1) * HEAD] = value

    return pl.pallas_call(
        kernel,
        grid=(query_steps + 2,),
        in_specs=[
            whole((rows, width)),
            whole((1, width)),
            pl.BlockSpec((width, tile), lambda i: (0, i)),
            pl.BlockSpec((1, tile), lambda i: (0, i)),
            whole((rows, HEAD)),
            whole((rows, HEAD)),
        ],
        out_specs=[
            whole((rows, width)),
            pl.BlockSpec((rows, tile), lambda i: (0, jnp.minimum(i, query_steps - 1))),
            pl.BlockSpec((rows, tile), lambda i: (0, jnp.maximum(i - query_steps, 0))),
        ],
        out_shape=[
            jax.ShapeDtypeStruct((rows, width), bf16),
            jax.ShapeDtypeStruct((rows, Q_WIDTH), bf16),
            jax.ShapeDtypeStruct((rows, 2 * K_WIDTH), bf16),
        ],
        compiler_params=kernel_params(32),
        cost_estimate=light,
    )(tokens_in, gain, weights, bias, cosine, sine)


def fill_bias(info_ref, bias_ref, count, rows):
    query_pos = info_ref[0] * rows + lax.broadcasted_iota(jnp.int32, (rows, rows), 1)
    for piece in range(count):
        key_pos = info_ref[1 + piece] * rows + lax.broadcasted_iota(jnp.int32, (rows, rows), 0)
        bias_ref[piece * rows : (piece + 1) * rows, :] = jnp.where(
            key_pos <= query_pos, 0.0, masked_score
        )


def attend(info, query, kv_pieces):
    rows = query.shape[0]
    count = len(kv_pieces)

    def kernel(info_ref, q_ref, *refs):
        keys, values = refs[:count], refs[count : 2 * count]
        mixed_ref, total_ref, bias_ref, score_ref = refs[2 * count :]

        @pl.when(pl.program_id(0) == 0)
        def _():
            fill_bias(info_ref, bias_ref, count, rows)

        q = q_ref[...]
        top = None
        for piece in range(count):
            at = slice(piece * rows, (piece + 1) * rows)
            score = dot(keys[piece][...], q, 1, 1) * score_scale_two + bias_ref[at, :]
            score_ref[at, :] = score
            peak = jnp.max(score, 0, keepdims=True)
            top = peak if top is None else jnp.maximum(top, peak)
        total = jnp.zeros((1, rows), f32)
        mixed = jnp.zeros((HEAD, rows), f32)
        for piece in range(count):
            weight = jnp.exp2(score_ref[piece * rows : (piece + 1) * rows, :] - top)
            total += jnp.sum(weight, 0, keepdims=True)
            mixed += dot(values[piece][...], weight.astype(bf16), 0, 0)
        mixed_ref[...] = (mixed / total).T.astype(bf16)
        total_ref[0] = top + jnp.log2(total)

    key_spec = pl.BlockSpec((rows, HEAD), lambda h: (0, h // GROUP))
    value_spec = pl.BlockSpec((rows, HEAD), lambda h: (0, KV_HEADS + h // GROUP))
    head_spec = pl.BlockSpec((rows, HEAD), lambda h: (0, h))
    return pl.pallas_call(
        kernel,
        grid=(HEADS,),
        in_specs=[pl.BlockSpec(memory_space=pltpu.SMEM), head_spec]
        + [key_spec] * count
        + [value_spec] * count,
        out_specs=[head_spec, pl.BlockSpec((1, 1, rows), lambda h: (h, 0, 0))],
        out_shape=[
            jax.ShapeDtypeStruct((rows, Q_WIDTH), bf16),
            jax.ShapeDtypeStruct((HEADS, 1, rows), f32),
        ],
        scratch_shapes=[pltpu.VMEM((count * rows, rows), f32)] * 2,
        compiler_params=kernel_params(32),
        cost_estimate=light,
    )(info, query, *kv_pieces, *kv_pieces)


def attend_back(info, query, grad_mixed, totals, cosine, sine, kv_pieces):
    rows = query.shape[0]
    count = len(kv_pieces)

    def kernel(info_ref, q_ref, g_ref, total_ref, cos_ref, sin_ref, *refs):
        keys, values = refs[:count], refs[count : 2 * count]
        dq_ref = refs[2 * count]
        kv_ref, bias_ref, p_ref, dp_ref, sum_ref = refs[2 * count + 1 :]
        head = pl.program_id(0)

        @pl.when(head == 0)
        def _():
            fill_bias(info_ref, bias_ref, count, rows)

        @pl.when(head % GROUP == 0)
        def _():
            sum_ref[...] = jnp.zeros_like(sum_ref)

        q, g, total = q_ref[...], g_ref[...], total_ref[0]
        delta = jnp.zeros((1, rows), f32)
        for piece in range(count):
            at = slice(piece * rows, (piece + 1) * rows)
            score = dot(keys[piece][...], q, 1, 1) * score_scale_two + bias_ref[at, :]
            p = jnp.exp2(score - total)
            dp = dot(values[piece][...], g, 1, 1)
            p_ref[at, :] = p
            dp_ref[at, :] = dp
            delta += jnp.sum(p * dp, 0, keepdims=True)
        dq = jnp.zeros((HEAD, rows), f32)
        for piece in range(count):
            at = slice(piece * rows, (piece + 1) * rows)
            p = p_ref[at, :]
            ds = (p * (dp_ref[at, :] - delta) * score_scale).astype(bf16)
            dq += dot(keys[piece][...], ds, 0, 0)
            sum_ref[piece, 0] += dot(ds, q, 1, 0)
            sum_ref[piece, 1] += dot(p.astype(bf16), g, 1, 0)
        dq = dq.T
        dq_ref[...] = (dq * cos_ref[...] - pltpu.roll(dq, HEAD // 2, 1) * sin_ref[...]).astype(bf16)

        @pl.when(head % GROUP == GROUP - 1)
        def _():
            for piece in range(count):
                kv_ref[info_ref[1 + count + piece]] = sum_ref[piece].astype(bf16)

    key_spec = pl.BlockSpec((rows, HEAD), lambda h: (0, h // GROUP))
    value_spec = pl.BlockSpec((rows, HEAD), lambda h: (0, KV_HEADS + h // GROUP))
    head_spec = pl.BlockSpec((rows, HEAD), lambda h: (0, h))
    return pl.pallas_call(
        kernel,
        grid=(HEADS,),
        in_specs=[
            pl.BlockSpec(memory_space=pltpu.SMEM),
            head_spec,
            head_spec,
            pl.BlockSpec((1, 1, rows), lambda h: (h, 0, 0)),
            whole((rows, HEAD)),
            whole((rows, HEAD)),
        ]
        + [key_spec] * count
        + [value_spec] * count,
        out_specs=[head_spec]
        + [pl.BlockSpec((count, 2, rows, HEAD), lambda h: (0, 0, 0, h // GROUP))],
        out_shape=[jax.ShapeDtypeStruct((rows, Q_WIDTH), bf16)]
        + [jax.ShapeDtypeStruct((count, 2, rows, K_WIDTH), bf16)],
        scratch_shapes=[pltpu.VMEM((count * rows, rows), f32)] * 3
        + [pltpu.VMEM((count, 2, rows, HEAD), f32)],
        compiler_params=kernel_params(32),
        cost_estimate=light,
    )(info, query, grad_mixed, totals, cosine, sine, *kv_pieces, *kv_pieces)


def once(shape):
    return pl.BlockSpec(shape, lambda *_: (0,) * len(shape), pipeline_mode=pl.Buffered(1))


def token_rows(count, rows):
    return 2 * rows if count % (2 * rows) == 0 else rows


def feed_forward(normed, cotangent, gate_cols, up_cols, units_here, rows, cuts):
    count, width = normed.shape
    units = gate_cols.shape[1]
    rows = token_rows(count, rows)
    steps, part, tile = count // rows, units_here // cuts, 256

    def kernel(x_ref, c_ref, wg_ref, wu_ref, act_ref, to_gate_ref, to_up_ref, *refs):
        down_refs, turned_ref = refs[:cuts], refs[cuts]
        step = pl.program_id(0)

        @pl.when(step < steps)
        def _():
            x = x_ref[...]
            gate = dot(x, wg_ref[...], 1, 0)
            up = dot(x, wu_ref[...], 1, 0)
            sigmoid = jax.nn.sigmoid(gate)
            swished = gate * sigmoid
            act = (swished * up).astype(bf16)
            act_ref[...] = act
            turned_ref[:, pl.ds(pl.multiple_of(step * rows, rows), rows)] = act.T
            to_up_ref[...] = swished.astype(bf16)
            to_gate_ref[...] = (up * sigmoid * (1.0 + gate * (1.0 - sigmoid))).astype(bf16)

        @pl.when(step >= steps)
        def _():
            for cut, down_ref in enumerate(down_refs):
                turned = turned_ref[cut * part : (cut + 1) * part, :]
                down_ref[...] = dot(turned, c_ref[...], 1, 0).astype(bf16)

    def early(i):
        return (jnp.minimum(i, steps - 1), 0)

    def late(i):
        return (0, jnp.maximum(i - steps, 0))

    return pl.pallas_call(
        kernel,
        grid=(steps + width // tile,),
        in_specs=[
            pl.BlockSpec((rows, width), early),
            pl.BlockSpec((count, tile), late),
            once((width, units)),
            once((width, units)),
        ],
        out_specs=[pl.BlockSpec((rows, units), early)] * 3 + [pl.BlockSpec((part, tile), late)] * cuts,
        out_shape=[jax.ShapeDtypeStruct((count, units), bf16)] * 3
        + [jax.ShapeDtypeStruct((part, width), bf16)] * cuts,
        scratch_shapes=[pltpu.VMEM((units, count), bf16)],
        compiler_params=kernel_params(58),
        cost_estimate=light,
    )(normed, cotangent, gate_cols, up_cols)


def unit_grads(cotangent, down_rows, to_gate, to_up, rows):
    count, width = cotangent.shape
    units = down_rows.shape[0]
    rows = token_rows(count, rows)

    def kernel(c_ref, wd_ref, tg_ref, tu_ref, dg_ref, du_ref):
        grad_act = dot(c_ref[...], wd_ref[...], 1, 1)
        dg_ref[...] = (grad_act * tg_ref[...].astype(f32)).astype(bf16)
        du_ref[...] = (grad_act * tu_ref[...].astype(f32)).astype(bf16)

    unit_spec = pl.BlockSpec((rows, units), lambda i: (i, 0))
    return pl.pallas_call(
        kernel,
        grid=(count // rows,),
        in_specs=[
            pl.BlockSpec((rows, width), lambda i: (i, 0)),
            once((units, width)),
            unit_spec,
            unit_spec,
        ],
        out_specs=[unit_spec] * 2,
        out_shape=[jax.ShapeDtypeStruct((count, units), bf16)] * 2,
        compiler_params=kernel_params(58),
        cost_estimate=light,
    )(cotangent, down_rows, to_gate, to_up)


def through_columns(grad_gate, grad_up, gate_cols, up_cols, rows):
    count, units = grad_gate.shape
    width = gate_cols.shape[0]
    rows = token_rows(count, rows)

    def kernel(dg_ref, du_ref, wg_ref, wu_ref, out_ref):
        out = dot(dg_ref[...], wg_ref[...], 1, 1) + dot(du_ref[...], wu_ref[...], 1, 1)
        out_ref[...] = out.astype(bf16)

    unit_spec = pl.BlockSpec((rows, units), lambda i: (i, 0))
    return pl.pallas_call(
        kernel,
        grid=(count // rows,),
        in_specs=[unit_spec, unit_spec, once((width, units)), once((width, units))],
        out_specs=pl.BlockSpec((rows, width), lambda i: (i, 0)),
        out_shape=jax.ShapeDtypeStruct((count, width), bf16),
        compiler_params=kernel_params(58),
        cost_estimate=light,
    )(grad_gate, grad_up, gate_cols, up_cols)


def column_grad(normed, grad, cuts):
    count, width = normed.shape
    units = grad.shape[1]
    tile = 256
    each = width // tile // cuts

    def kernel(x_ref, g_ref, *out_refs):
        step = pl.program_id(0)
        out = dot(x_ref[...].T, g_ref[...], 1, 0).astype(bf16)
        for cut, out_ref in enumerate(out_refs):

            @pl.when(step // each == cut)
            def _():
                out_ref[...] = out

    def cut_spec(cut):
        return pl.BlockSpec((tile, units), lambda i: (jnp.clip(i - cut * each, 0, each - 1), 0))

    return pl.pallas_call(
        kernel,
        grid=(width // tile,),
        in_specs=[pl.BlockSpec((count, tile), lambda i: (0, i)), once((count, units))],
        out_specs=[cut_spec(cut) for cut in range(cuts)],
        out_shape=[jax.ShapeDtypeStruct((width // cuts, units), bf16)] * cuts,
        compiler_params=kernel_params(58),
        cost_estimate=light,
    )(normed, grad)


def through_rows(activation, down_rows, rows):
    count, units = activation.shape
    width = down_rows.shape[1]
    rows = token_rows(count, rows)

    def kernel(act_ref, wd_ref, out_ref):
        out_ref[...] = dot(act_ref[...], wd_ref[...], 1, 0).astype(bf16)

    return pl.pallas_call(
        kernel,
        grid=(count // rows,),
        in_specs=[pl.BlockSpec((rows, units), lambda i: (i, 0)), once((units, width))],
        out_specs=pl.BlockSpec((rows, width), lambda i: (i, 0)),
        out_shape=jax.ShapeDtypeStruct((count, width), bf16),
        compiler_params=kernel_params(58),
        cost_estimate=light,
    )(activation, down_rows)


def rotary(positions):
    half = HEAD // 2
    frequency = rope_base ** (-(jnp.arange(half, dtype=f32) * 2.0) / HEAD)
    angles = positions.astype(f32)[:, None] * frequency[None, :]
    cosine, sine = jnp.cos(angles), jnp.sin(angles)
    return jnp.concatenate([cosine, cosine], 1), jnp.concatenate([-sine, sine], 1)


def fence(*values):
    return lax.optimization_barrier(values)


def added(left_side, right_side):
    def kernel(a_ref, b_ref, out_ref):
        out_ref[...] = (a_ref[...].astype(f32) + b_ref[...].astype(f32)).astype(out_ref.dtype)

    def one(a, b):
        steps = [n for n in (4, 5, 3, 2) if a.ndim == 2 and a.shape[0] % (16 * n) == 0]
        if not steps:
            return (a.astype(f32) + b.astype(f32)).astype(a.dtype)
        block = pl.BlockSpec((a.shape[0] // steps[0], a.shape[1]), lambda i: (i, 0))
        return pl.pallas_call(
            kernel,
            grid=(steps[0],),
            in_specs=[block] * 2,
            out_specs=block,
            out_shape=jax.ShapeDtypeStruct(a.shape, a.dtype),
            compiler_params=kernel_params(16),
            cost_estimate=light,
        )(a, b)

    return jax.tree.map(one, left_side, right_side)


class CtxLine:
    lead = 1

    def __init__(self):
        place = lax.axis_index("ctx")
        self.outer = (place == 0) | (place == 3)
        self.waiting = []
        self.chunks, self.inward, self.across, self.pair_sums = [], [], [], []
        self.totals, self.outward = [], []

    def add(self, chunks):
        self.waiting += list(chunks)
        self.send()

    def send(self):
        while self.waiting and len(self.chunks) < len(self.pair_sums) + self.lead:
            chunk = self.waiting.pop(0)
            self.chunks.append(chunk)
            self.inward.append(lax.ppermute(chunk, "ctx", [(0, 1), (3, 2)]))

    def round(self, *values):
        step = len(self.pair_sums)
        more = step < len(self.chunks)
        last = len(self.totals)
        if more:
            self.inward[step], values = fence(self.inward[step], values)
            self.pair_sums.append(added(self.chunks[step], self.inward[step]))
        ahead = slice(step + 1, step + 2 if step > 2 else step)
        held = [
            (self.across, slice(last, None)),
            (self.pair_sums, slice(last + 1, None)),
            (self.outward, slice(last - 1, None) if last else slice(0, 0)),
            (self.inward, ahead),
        ]
        fenced, self.waiting, values = fence([array[at] for array, at in held], self.waiting, values)
        for (array, at), value in zip(held, fenced):
            array[at] = value
        self.send()
        if len(self.across) > last:
            self.totals.append(added(self.pair_sums[last], self.across[last]))
            self.outward.append(lax.ppermute(self.totals[-1], "ctx", [(1, 0), (2, 3)]))
        if more:
            self.across.append(lax.ppermute(self.pair_sums[step], "ctx", [(1, 2), (2, 1)]))
        return values

    def sums(self, first, last):
        return jax.tree.map(
            lambda back, total: jnp.where(self.outer, back, total),
            self.outward[first:last],
            self.totals[first:last],
        )


def summed_in_plane(vector):
    size = lax.axis_size("fsdp")
    bit = 1
    while bit < size:
        vector = vector + lax.ppermute(vector, "fsdp", [(j, j ^ bit) for j in range(size)])
        bit *= 2
    return vector


def local(
    tokens_in,
    block_order,
    norm_attn,
    w_qkv,
    b_qkv,
    w_out,
    norm_mlp,
    w_gate,
    w_up,
    w_down,
    cotangent,
):
    rows, width = tokens_in.shape
    shards = lax.axis_size("fsdp")
    blocks = lax.axis_size("ctx")
    shard = lax.axis_index("fsdp")
    place = lax.axis_index("ctx")
    shard_rows = w_gate.shape[0]
    units = w_down.shape[0]
    orders = block_order[0]
    owners = jnp.concatenate([place[None], (place - jnp.arange(blocks)) % blocks])
    info = jnp.sum(
        jnp.where(owners[:, None] == jnp.arange(blocks)[None, :], orders[None, :], 0), 1
    )
    info = jnp.concatenate([info, owners[1:]]).astype(jnp.int32)
    cosine, sine = rotary(info[0] * rows + jnp.arange(rows, dtype=jnp.int32))

    def turn(parts):
        return lax.all_to_all(parts, "fsdp", 0, 0)

    qkv_all = lax.all_gather(w_qkv, "fsdp", axis=0, tiled=True)
    vectors = lax.all_gather(jnp.concatenate([norm_attn, norm_mlp, b_qkv]), "fsdp", axis=0)
    part = 2 * shard_rows // 3 // blocks
    shared = part * blocks
    weights = (w_gate, w_up)
    parts = jnp.concatenate(
        [lax.dynamic_slice_in_dim(weight, place * part, part, 0) for weight in weights]
    )
    vectors, parts = fence(vectors, split_columns(parts, shards))
    pieces = [turn(parts)]

    def ring(piece):
        return lax.ppermute(piece, "ctx", [(j, (j + 1) % blocks) for j in range(blocks)])

    pieces.append(ring(pieces[0]))
    full = padded(units)
    down_rows = jnp.concatenate([w_down, jnp.zeros((full - units, width), bf16)])
    direct = split_columns(jnp.concatenate([weight[shared:] for weight in weights]), shards)
    gain_attn = vectors[:, :shard_rows].reshape(1, -1).astype(f32)
    gain_mlp = vectors[:, shard_rows : 2 * shard_rows].reshape(1, -1).astype(f32)
    bias_all = vectors[:, 2 * shard_rows :].reshape(1, -1).astype(f32)
    qkv_all, pieces, down_rows = fence(qkv_all, pieces, down_rows)
    out_all = lax.all_gather(w_out, "fsdp", axis=0, tiled=True)

    normed, query, keys_values = project(tokens_in, gain_attn, qkv_all, bias_all, cosine, sine)
    keys_values, direct = fence(keys_values, direct)
    direct = turn(direct)
    kv_pieces = [keys_values] + [
        lax.ppermute(keys_values, "ctx", [(j, (j + s) % blocks) for j in range(blocks)])
        for s in range(1, blocks)
    ]
    kv_pieces, pieces, own_cot = fence(kv_pieces, pieces, cotangent)
    for _ in range(2, blocks - 1):
        pieces.append(ring(pieces[-1]))

    def from_chip(chip):
        return lax.ppermute(own_cot, "fsdp", [(j, j ^ chip) for j in range(shards)])

    chips = [chip for chip in range(2, shards, 2) if chip & (chip - 1) == 0]
    cot_pieces = {chip: from_chip(chip) for chip in chips}
    mixed, totals = attend(info, query, kv_pieces)
    mixed, direct = fence(mixed, direct)
    source = tokens_in.astype(f32)
    hidden = source + dot(mixed, out_all, 1, 0)
    scale_two = lax.rsqrt(jnp.mean(hidden * hidden, -1, keepdims=True) + norm_eps)
    normed_two = (hidden * scale_two * gain_mlp).astype(bf16)

    normed_two, pieces, cot_pieces = fence(normed_two, pieces, cot_pieces)
    pieces.append(ring(pieces[-1]))
    normed_all = lax.all_gather(normed_two, "fsdp", axis=0, tiled=True)
    cot_pieces[0] = own_cot
    for chip in range(2, shards, 2):
        if chip not in cot_pieces:
            cot_pieces[chip] = from_chip(chip)
            cot_pieces[chip], pieces = fence(cot_pieces[chip], pieces)
    for chip in range(0, shards, 2):
        cot_pieces[chip ^ 1] = lax.ppermute(
            cot_pieces[chip], "fsdp", [(j, j ^ 1) for j in range(shards)]
        )
    order = list(cot_pieces)

    def cot_moves(place, shard):
        return [
            (i, pl.ds(0, rows), 0, pl.ds((shard ^ bits) * rows, rows))
            for i, bits in enumerate(order)
        ]

    (cot_all,) = moved(cot_moves, [cot_pieces[bits] for bits in order], [(shards * rows, width)])

    groups = shard_rows // part
    grouped = (shards, groups, part, full)
    rest = groups - blocks

    def column_moves(place, shard):
        every = pl.ds(0, shards)
        listed = []
        for k in range(2):
            for s in range(blocks):
                group = lax.rem(place - s + blocks, blocks)
                listed.append((s, (every, k), k, (every, group)))
            listed.append((blocks, (every, pl.ds(k * rest, rest)), k, (every, pl.ds(blocks, rest))))
        return listed

    sources = [piece.reshape(shards, 2, part, full) for piece in pieces]
    sources.append(direct.reshape(shards, 2 * rest, part, full))
    columns = moved(column_moves, sources, [grouped] * 2)
    gate_cols, up_cols = (array.reshape(width, full) for array in columns)
    cuts = 2
    activation, to_gate, to_up, *down_terms = feed_forward(
        normed_all, cot_all, gate_cols, up_cols, units, rows, cuts
    )

    def to_rows(terms):
        return turn(terms.reshape(shards, shard_rows, full)).reshape(width, full)

    def merged(terms):
        return merge_columns(terms.reshape(shards, shard_rows, full), units)

    def to_owner(terms):
        return lax.psum_scatter(terms, "fsdp", scatter_dimension=0, tiled=True)

    def through_attention(part_grad):
        part_grad = part_grad.astype(f32)
        scaled = part_grad * gain_mlp
        grad_hidden = (
            cotangent.astype(f32)
            + scale_two * scaled
            - hidden * scale_two**3 * jnp.mean(hidden * scaled, -1, keepdims=True)
        )
        gain_terms = jnp.sum(part_grad * hidden * scale_two, 0)
        grad_branch = grad_hidden.astype(bf16)
        grad_mixed = dot(grad_branch, out_all, 1, 1).astype(bf16)
        grad_query, kv_terms = attend_back(
            info, query, grad_mixed, totals, cosine, sine, kv_pieces
        )
        return grad_hidden, gain_terms, grad_branch, grad_query, kv_terms

    def kv_owner(kv_terms):
        return lax.psum_scatter(kv_terms, "ctx", scatter_dimension=0)

    def projected_grad(grad_query, kv_terms):
        grad_kv = kv_terms.astype(f32)
        grad_key = grad_kv[0].reshape(rows, KV_HEADS, HEAD)
        rolled = jnp.concatenate([grad_key[..., HEAD // 2 :], grad_key[..., : HEAD // 2]], -1)
        grad_key = grad_key * cosine[:, None, :] - rolled * sine[:, None, :]
        return jnp.concatenate(
            [grad_query, grad_key.reshape(rows, K_WIDTH).astype(bf16), grad_kv[1].astype(bf16)], 1
        )

    def to_tokens(grad_projected, grad_hidden):
        scale_one = lax.rsqrt(jnp.mean(source * source, -1, keepdims=True) + norm_eps)
        grad_normed = dot(grad_projected, qkv_all, 1, 1)
        scaled = grad_normed * gain_attn
        grad_tokens = (
            grad_hidden
            + scale_one * scaled
            - source * scale_one**3 * jnp.mean(source * scaled, -1, keepdims=True)
        ).astype(bf16)
        bias_terms = jnp.sum(grad_projected.astype(f32), 0)
        return grad_tokens, jnp.sum(grad_normed * source * scale_one, 0), bias_terms

    def out_grad(mixed, grad_branch):
        return dot(mixed, grad_branch, 0, 0).astype(bf16)

    def own_sums(*terms):
        total = summed_in_plane(jnp.concatenate([t.reshape(shards, -1) for t in terms], 1))
        return lax.dynamic_index_in_dim(total, shard, 0, False)

    grad_gate, grad_up = unit_grads(cot_all, down_rows, to_gate, to_up, rows)
    mlp_grad = through_columns(grad_gate, grad_up, gate_cols, up_cols, rows)
    if blocks == 4:
        line = CtxLine()
        line.add(down_terms)
        mlp_grad, grad_gate, grad_up, act = line.round(
            mlp_grad, grad_gate, grad_up, activation
        )
        part_grad = to_owner(mlp_grad)
        gate_terms = column_grad(normed_all, grad_gate, cuts)
        (up_terms,) = column_grad(normed_all, grad_up, 1)
        gate_terms, up_terms, act = line.round(gate_terms, up_terms, act)
        line.add(gate_terms)
        up_terms = to_rows(up_terms)
        grad_hidden, gain_mlp_terms, grad_branch, grad_query, kv_terms = through_attention(
            part_grad
        )
        grad_hidden, grad_branch, grad_query, mixed_now, kv_terms, up_terms = line.round(
            grad_hidden, grad_branch, grad_query, mixed, kv_terms, up_terms
        )
        kv_terms = kv_owner(kv_terms)
        out_terms = out_grad(mixed_now, grad_branch)
        split = width // 2
        line.add([up_terms[:split], up_terms[split:]])
        grad_query, out_terms = line.round(grad_query, out_terms)
        out_terms = to_owner(out_terms)
        grad_projected = projected_grad(grad_query, kv_terms)
        qkv_terms = dot(normed, grad_projected, 0, 0).astype(bf16)
        grad_tokens, gain_attn_terms, bias_terms = to_tokens(grad_projected, grad_hidden)
        qkv_terms, grad_tokens, gain_attn_terms, bias_terms, act = line.round(
            qkv_terms, grad_tokens, gain_attn_terms, bias_terms, act
        )
        qkv_terms = to_owner(qkv_terms)
        small = own_sums(gain_attn_terms, gain_mlp_terms, bias_terms)
        mlp_terms = through_rows(act, down_rows, rows)
        small, mlp_terms, out_terms = line.round(small, mlp_terms, out_terms)
        mlp_out = to_owner(mlp_terms)
        line.add([out_terms])
        gate_terms = to_rows(jnp.concatenate(line.sums(cuts, 2 * cuts)))
        (qkv_terms,) = line.round(qkv_terms)
        line.add([[qkv_terms, small]])
        line.round()
        (gate_terms,) = line.round(gate_terms)
        down_sums = line.sums(0, cuts)
        up_sum, up_more, out_sum, (qkv_sum, small) = line.sums(2 * cuts, 2 * cuts + 4)
        up_terms = jnp.concatenate([up_sum, up_more])
    else:
        part_grad = to_owner(mlp_grad)
        gate_terms = column_grad(normed_all, grad_gate, cuts)
        up_terms = column_grad(normed_all, grad_up, cuts)
        gate_terms, up_terms = (to_rows(jnp.concatenate(t)) for t in (gate_terms, up_terms))
        mlp_out = to_owner(through_rows(activation, down_rows, rows))
        grad_hidden, gain_mlp_terms, grad_branch, grad_query, kv_terms = through_attention(
            part_grad
        )
        kv_terms = kv_owner(kv_terms)
        out_terms = to_owner(out_grad(mixed, grad_branch))
        grad_projected = projected_grad(grad_query, kv_terms)
        qkv_terms = to_owner(dot(normed, grad_projected, 0, 0).astype(bf16))
        grad_tokens, gain_attn_terms, bias_terms = to_tokens(grad_projected, grad_hidden)
        small = own_sums(gain_attn_terms, gain_mlp_terms, bias_terms)
        down_sums, gate_terms, up_terms, out_sum, qkv_sum, small = lax.psum(
            (down_terms, gate_terms, up_terms, out_terms, qkv_terms, small), "ctx"
        )

    grad_down_w = jnp.concatenate(down_sums).astype(f32)
    grad_out_w = out_sum.astype(f32)
    grad_qkv_w = qkv_sum.astype(f32)
    out_tokens = (hidden + mlp_out.astype(f32)).astype(bf16)

    return (
        out_tokens,
        grad_tokens,
        small[:shard_rows],
        grad_qkv_w,
        small[2 * shard_rows :],
        grad_out_w,
        small[shard_rows : 2 * shard_rows],
        merged(gate_terms),
        merged(up_terms),
        grad_down_w,
    )


def solution(mesh):
    in_specs = (
        P(("fsdp", "ctx"), None),
        P("fsdp", None),
        P("fsdp"),
        P("fsdp", None),
        P("fsdp"),
        P("fsdp", None),
        P("fsdp"),
        P("fsdp", None),
        P("fsdp", None),
        P("fsdp", None),
        P(("fsdp", "ctx"), None),
    )
    out_specs = (
        P(("fsdp", "ctx"), None),
        P(("fsdp", "ctx"), None),
        P("fsdp"),
        P("fsdp", None),
        P("fsdp"),
        P("fsdp", None),
        P("fsdp"),
        P("fsdp", None),
        P("fsdp", None),
        P("fsdp", None),
    )
    return jax.shard_map(local, mesh=mesh, in_specs=in_specs, out_specs=out_specs, check_vma=False)
```

```python
import jax
import jax.numpy as jnp
from jax import lax
from jax.experimental import pallas as pl
from jax.experimental.pallas import tpu as pltpu
from jax.sharding import PartitionSpec as P

HEADS = 12
KV_HEADS = 2
HEAD = 128
GROUP = HEADS // KV_HEADS
Q_WIDTH = HEADS * HEAD
K_WIDTH = KV_HEADS * HEAD

norm_eps = 1e-06
rope_base = 1000000.0
masked_score = -1e30
score_scale = HEAD ** (-0.5)
score_scale_two = score_scale * 1.4426950408889634
bf16 = jnp.bfloat16
f32 = jnp.float32
light = pl.CostEstimate(flops=1 << 20, bytes_accessed=1 << 16, transcendentals=0)


def dot(left_side, right_side, left_dim, right_dim):
    return lax.dot_general(
        left_side,
        right_side,
        (((left_dim,), (right_dim,)), ((), ())),
        preferred_element_type=f32,
    )


def kernel_params(mib):
    return pltpu.CompilerParams(vmem_limit_bytes=mib * 1024 * 1024)


def padded(size):
    return (size + 127) // 128 * 128


def whole(shape):
    return pl.BlockSpec(shape, lambda *_: (0,) * len(shape))


def split_columns(weight, shard_count):
    rows, width = weight.shape
    cols = width // shard_count
    full = padded(cols)
    step = 48 if rows % 48 == 0 else rows

    def kernel(in_ref, out_ref):
        for shard in range(shard_count):
            out_ref[shard, :, :cols] = in_ref[:, shard * cols : (shard + 1) * cols]
            if full > cols:
                out_ref[shard, :, cols:] = jnp.zeros((step, full - cols), weight.dtype)

    return pl.pallas_call(
        kernel,
        grid=(rows // step,),
        in_specs=[pl.BlockSpec((step, width), lambda i: (i, 0))],
        out_specs=pl.BlockSpec((shard_count, step, full), lambda i: (0, i, 0)),
        out_shape=jax.ShapeDtypeStruct((shard_count, rows, full), weight.dtype),
        compiler_params=kernel_params(32),
        cost_estimate=light,
    )(weight)


def merge_columns(parts, cols):
    shards, rows, full = parts.shape
    width = shards * cols
    step = 48 if rows % 48 == 0 else rows

    def kernel(in_ref, out_ref):
        for shard in range(shards):
            part = in_ref[shard, :, :cols]
            out_ref[:, shard * cols : (shard + 1) * cols] = part.astype(f32)

    return pl.pallas_call(
        kernel,
        grid=(rows // step,),
        in_specs=[pl.BlockSpec((shards, step, full), lambda i: (0, i, 0))],
        out_specs=pl.BlockSpec((step, width), lambda i: (i, 0)),
        out_shape=jax.ShapeDtypeStruct((rows, width), f32),
        compiler_params=kernel_params(40),
        cost_estimate=light,
    )(parts)


def moved(moves, arrays, shapes):
    def kernel(at_ref, *refs):
        sources, targets, sems = refs[: len(arrays)], refs[len(arrays) : -1], refs[-1]
        copies = [
            pltpu.make_async_copy(
                sources[source].at[where], targets[target].at[there], sems.at[i]
            )
            for i, (source, where, target, there) in enumerate(moves(at_ref[0], at_ref[1]))
        ]
        for copy in copies:
            copy.start()
        for copy in copies:
            copy.wait()

    anywhere = pl.BlockSpec(memory_space=pl.ANY)
    at = jnp.stack([lax.axis_index("ctx"), lax.axis_index("fsdp")]).astype(jnp.int32)
    return pl.pallas_call(
        kernel,
        in_specs=[pl.BlockSpec(memory_space=pltpu.SMEM)] + [anywhere] * len(arrays),
        out_specs=[anywhere] * len(shapes),
        out_shape=[jax.ShapeDtypeStruct(shape, bf16) for shape in shapes],
        scratch_shapes=[pltpu.SemaphoreType.DMA((len(moves(0, 0)),))],
        compiler_params=kernel_params(16),
        cost_estimate=light,
    )(at, *arrays)


def project(tokens_in, gain, weights, bias, cosine, sine):
    rows, width = tokens_in.shape
    tile = K_WIDTH
    query_steps = Q_WIDTH // tile

    def kernel(x_ref, gain_ref, w_ref, bias_ref, cos_ref, sin_ref, normed_ref, q_ref, kv_ref):
        step = pl.program_id(0)

        @pl.when(step == 0)
        def _():
            source = x_ref[...].astype(f32)
            scale = lax.rsqrt(jnp.mean(source * source, -1, keepdims=True) + norm_eps)
            normed_ref[...] = (source * scale * gain_ref[...]).astype(bf16)

        out = dot(normed_ref[...], w_ref[...], 1, 0) + bias_ref[...]
        heads = []
        for head in range(tile // HEAD):
            part = out[:, head * HEAD : (head + 1) * HEAD]
            turned = part * cos_ref[...] + pltpu.roll(part, HEAD // 2, 1) * sin_ref[...]
            heads.append(jnp.where(step <= query_steps, turned, part).astype(bf16))

        @pl.when(step < query_steps)
        def _():
            for head, value in enumerate(heads):
                q_ref[:, head * HEAD : (head + 1) * HEAD] = value

        @pl.when(step >= query_steps)
        def _():
            for head, value in enumerate(heads):
                kv_ref[:, head * HEAD : (head + 1) * HEAD] = value

    return pl.pallas_call(
        kernel,
        grid=(query_steps + 2,),
        in_specs=[
            whole((rows, width)),
            whole((1, width)),
            pl.BlockSpec((width, tile), lambda i: (0, i)),
            pl.BlockSpec((1, tile), lambda i: (0, i)),
            whole((rows, HEAD)),
            whole((rows, HEAD)),
        ],
        out_specs=[
            whole((rows, width)),
            pl.BlockSpec((rows, tile), lambda i: (0, jnp.minimum(i, query_steps - 1))),
            pl.BlockSpec((rows, tile), lambda i: (0, jnp.maximum(i - query_steps, 0))),
        ],
        out_shape=[
            jax.ShapeDtypeStruct((rows, width), bf16),
            jax.ShapeDtypeStruct((rows, Q_WIDTH), bf16),
            jax.ShapeDtypeStruct((rows, 2 * K_WIDTH), bf16),
        ],
        compiler_params=kernel_params(32),
        cost_estimate=light,
    )(tokens_in, gain, weights, bias, cosine, sine)


def fill_bias(info_ref, bias_ref, count, rows):
    query_pos = info_ref[0] * rows + lax.broadcasted_iota(jnp.int32, (rows, rows), 1)
    for piece in range(count):
        key_pos = info_ref[1 + piece] * rows + lax.broadcasted_iota(jnp.int32, (rows, rows), 0)
        bias_ref[piece * rows : (piece + 1) * rows, :] = jnp.where(
            key_pos <= query_pos, 0.0, masked_score
        )


def attend(info, query, kv_pieces):
    rows = query.shape[0]
    count = len(kv_pieces)

    def kernel(info_ref, q_ref, *refs):
        keys, values = refs[:count], refs[count : 2 * count]
        mixed_ref, total_ref, bias_ref, score_ref = refs[2 * count :]

        @pl.when(pl.program_id(0) == 0)
        def _():
            fill_bias(info_ref, bias_ref, count, rows)

        q = q_ref[...]
        top = None
        for piece in range(count):
            at = slice(piece * rows, (piece + 1) * rows)
            score = dot(keys[piece][...], q, 1, 1) * score_scale_two + bias_ref[at, :]
            score_ref[at, :] = score
            peak = jnp.max(score, 0, keepdims=True)
            top = peak if top is None else jnp.maximum(top, peak)
        total = jnp.zeros((1, rows), f32)
        mixed = jnp.zeros((HEAD, rows), f32)
        for piece in range(count):
            weight = jnp.exp2(score_ref[piece * rows : (piece + 1) * rows, :] - top)
            total += jnp.sum(weight, 0, keepdims=True)
            mixed += dot(values[piece][...], weight.astype(bf16), 0, 0)
        mixed_ref[...] = (mixed / total).T.astype(bf16)
        total_ref[0] = top + jnp.log2(total)

    key_spec = pl.BlockSpec((rows, HEAD), lambda h: (0, h // GROUP))
    value_spec = pl.BlockSpec((rows, HEAD), lambda h: (0, KV_HEADS + h // GROUP))
    head_spec = pl.BlockSpec((rows, HEAD), lambda h: (0, h))
    return pl.pallas_call(
        kernel,
        grid=(HEADS,),
        in_specs=[pl.BlockSpec(memory_space=pltpu.SMEM), head_spec]
        + [key_spec] * count
        + [value_spec] * count,
        out_specs=[head_spec, pl.BlockSpec((1, 1, rows), lambda h: (h, 0, 0))],
        out_shape=[
            jax.ShapeDtypeStruct((rows, Q_WIDTH), bf16),
            jax.ShapeDtypeStruct((HEADS, 1, rows), f32),
        ],
        scratch_shapes=[pltpu.VMEM((count * rows, rows), f32)] * 2,
        compiler_params=kernel_params(32),
        cost_estimate=light,
    )(info, query, *kv_pieces, *kv_pieces)


def attend_back(info, query, grad_mixed, totals, cosine, sine, kv_pieces):
    rows = query.shape[0]
    count = len(kv_pieces)

    def kernel(info_ref, q_ref, g_ref, total_ref, cos_ref, sin_ref, *refs):
        keys, values = refs[:count], refs[count : 2 * count]
        dq_ref = refs[2 * count]
        kv_ref, bias_ref, p_ref, dp_ref, sum_ref = refs[2 * count + 1 :]
        head = pl.program_id(0)

        @pl.when(head == 0)
        def _():
            fill_bias(info_ref, bias_ref, count, rows)

        @pl.when(head % GROUP == 0)
        def _():
            sum_ref[...] = jnp.zeros_like(sum_ref)

        q, g, total = q_ref[...], g_ref[...], total_ref[0]
        delta = jnp.zeros((1, rows), f32)
        for piece in range(count):
            at = slice(piece * rows, (piece + 1) * rows)
            score = dot(keys[piece][...], q, 1, 1) * score_scale_two + bias_ref[at, :]
            p = jnp.exp2(score - total)
            dp = dot(values[piece][...], g, 1, 1)
            p_ref[at, :] = p
            dp_ref[at, :] = dp
            delta += jnp.sum(p * dp, 0, keepdims=True)
        dq = jnp.zeros((HEAD, rows), f32)
        for piece in range(count):
            at = slice(piece * rows, (piece + 1) * rows)
            p = p_ref[at, :]
            ds = (p * (dp_ref[at, :] - delta) * score_scale).astype(bf16)
            dq += dot(keys[piece][...], ds, 0, 0)
            sum_ref[piece, 0] += dot(ds, q, 1, 0)
            sum_ref[piece, 1] += dot(p.astype(bf16), g, 1, 0)
        dq = dq.T
        dq_ref[...] = (dq * cos_ref[...] - pltpu.roll(dq, HEAD // 2, 1) * sin_ref[...]).astype(bf16)

        @pl.when(head % GROUP == GROUP - 1)
        def _():
            for piece in range(count):
                kv_ref[info_ref[1 + count + piece]] = sum_ref[piece].astype(bf16)

    key_spec = pl.BlockSpec((rows, HEAD), lambda h: (0, h // GROUP))
    value_spec = pl.BlockSpec((rows, HEAD), lambda h: (0, KV_HEADS + h // GROUP))
    head_spec = pl.BlockSpec((rows, HEAD), lambda h: (0, h))
    return pl.pallas_call(
        kernel,
        grid=(HEADS,),
        in_specs=[
            pl.BlockSpec(memory_space=pltpu.SMEM),
            head_spec,
            head_spec,
            pl.BlockSpec((1, 1, rows), lambda h: (h, 0, 0)),
            whole((rows, HEAD)),
            whole((rows, HEAD)),
        ]
        + [key_spec] * count
        + [value_spec] * count,
        out_specs=[head_spec]
        + [pl.BlockSpec((count, 2, rows, HEAD), lambda h: (0, 0, 0, h // GROUP))],
        out_shape=[jax.ShapeDtypeStruct((rows, Q_WIDTH), bf16)]
        + [jax.ShapeDtypeStruct((count, 2, rows, K_WIDTH), bf16)],
        scratch_shapes=[pltpu.VMEM((count * rows, rows), f32)] * 3
        + [pltpu.VMEM((count, 2, rows, HEAD), f32)],
        compiler_params=kernel_params(32),
        cost_estimate=light,
    )(info, query, grad_mixed, totals, cosine, sine, *kv_pieces, *kv_pieces)


def once(shape):
    return pl.BlockSpec(shape, lambda *_: (0,) * len(shape), pipeline_mode=pl.Buffered(1))


def token_rows(count, rows):
    return 2 * rows if count % (2 * rows) == 0 else rows


def feed_forward(normed, cotangent, gate_cols, up_cols, units_here, rows, cuts):
    count, width = normed.shape
    units = gate_cols.shape[1]
    rows = token_rows(count, rows)
    steps, part, tile = count // rows, units_here // cuts, 256

    def kernel(x_ref, c_ref, wg_ref, wu_ref, act_ref, to_gate_ref, to_up_ref, *refs):
        down_refs, turned_ref = refs[:cuts], refs[cuts]
        step = pl.program_id(0)

        @pl.when(step < steps)
        def _():
            x = x_ref[...]
            gate = dot(x, wg_ref[...], 1, 0)
            up = dot(x, wu_ref[...], 1, 0)
            sigmoid = jax.nn.sigmoid(gate)
            swished = gate * sigmoid
            act = (swished * up).astype(bf16)
            act_ref[...] = act
            turned_ref[:, pl.ds(pl.multiple_of(step * rows, rows), rows)] = act.T
            to_up_ref[...] = swished.astype(bf16)
            to_gate_ref[...] = (up * sigmoid * (1.0 + gate * (1.0 - sigmoid))).astype(bf16)

        @pl.when(step >= steps)
        def _():
            for cut, down_ref in enumerate(down_refs):
                turned = turned_ref[cut * part : (cut + 1) * part, :]
                down_ref[...] = dot(turned, c_ref[...], 1, 0).astype(bf16)

    def early(i):
        return (jnp.minimum(i, steps - 1), 0)

    def late(i):
        return (0, jnp.maximum(i - steps, 0))

    return pl.pallas_call(
        kernel,
        grid=(steps + width // tile,),
        in_specs=[
            pl.BlockSpec((rows, width), early),
            pl.BlockSpec((count, tile), late),
            once((width, units)),
            once((width, units)),
        ],
        out_specs=[pl.BlockSpec((rows, units), early)] * 3 + [pl.BlockSpec((part, tile), late)] * cuts,
        out_shape=[jax.ShapeDtypeStruct((count, units), bf16)] * 3
        + [jax.ShapeDtypeStruct((part, width), bf16)] * cuts,
        scratch_shapes=[pltpu.VMEM((units, count), bf16)],
        compiler_params=kernel_params(58),
        cost_estimate=light,
    )(normed, cotangent, gate_cols, up_cols)


def unit_grads(cotangent, down_rows, to_gate, to_up, rows):
    count, width = cotangent.shape
    units = down_rows.shape[0]
    rows = token_rows(count, rows)

    def kernel(c_ref, wd_ref, tg_ref, tu_ref, dg_ref, du_ref):
        grad_act = dot(c_ref[...], wd_ref[...], 1, 1)
        dg_ref[...] = (grad_act * tg_ref[...].astype(f32)).astype(bf16)
        du_ref[...] = (grad_act * tu_ref[...].astype(f32)).astype(bf16)

    unit_spec = pl.BlockSpec((rows, units), lambda i: (i, 0))
    return pl.pallas_call(
        kernel,
        grid=(count // rows,),
        in_specs=[
            pl.BlockSpec((rows, width), lambda i: (i, 0)),
            once((units, width)),
            unit_spec,
            unit_spec,
        ],
        out_specs=[unit_spec] * 2,
        out_shape=[jax.ShapeDtypeStruct((count, units), bf16)] * 2,
        compiler_params=kernel_params(58),
        cost_estimate=light,
    )(cotangent, down_rows, to_gate, to_up)


def through_columns(grad_gate, grad_up, gate_cols, up_cols, rows):
    count, units = grad_gate.shape
    width = gate_cols.shape[0]
    rows = token_rows(count, rows)

    def kernel(dg_ref, du_ref, wg_ref, wu_ref, out_ref):
        out = dot(dg_ref[...], wg_ref[...], 1, 1) + dot(du_ref[...], wu_ref[...], 1, 1)
        out_ref[...] = out.astype(bf16)

    unit_spec = pl.BlockSpec((rows, units), lambda i: (i, 0))
    return pl.pallas_call(
        kernel,
        grid=(count // rows,),
        in_specs=[unit_spec, unit_spec, once((width, units)), once((width, units))],
        out_specs=pl.BlockSpec((rows, width), lambda i: (i, 0)),
        out_shape=jax.ShapeDtypeStruct((count, width), bf16),
        compiler_params=kernel_params(58),
        cost_estimate=light,
    )(grad_gate, grad_up, gate_cols, up_cols)


def column_grad(normed, grad, cuts):
    count, width = normed.shape
    units = grad.shape[1]
    tile = 256
    each = width // tile // cuts

    def kernel(x_ref, g_ref, *out_refs):
        step = pl.program_id(0)
        out = dot(x_ref[...].T, g_ref[...], 1, 0).astype(bf16)
        for cut, out_ref in enumerate(out_refs):

            @pl.when(step // each == cut)
            def _():
                out_ref[...] = out

    def cut_spec(cut):
        return pl.BlockSpec((tile, units), lambda i: (jnp.clip(i - cut * each, 0, each - 1), 0))

    return pl.pallas_call(
        kernel,
        grid=(width // tile,),
        in_specs=[pl.BlockSpec((count, tile), lambda i: (0, i)), once((count, units))],
        out_specs=[cut_spec(cut) for cut in range(cuts)],
        out_shape=[jax.ShapeDtypeStruct((width // cuts, units), bf16)] * cuts,
        compiler_params=kernel_params(58),
        cost_estimate=light,
    )(normed, grad)


def through_rows(activation, down_rows, rows):
    count, units = activation.shape
    width = down_rows.shape[1]
    rows = token_rows(count, rows)

    def kernel(act_ref, wd_ref, out_ref):
        out_ref[...] = dot(act_ref[...], wd_ref[...], 1, 0).astype(bf16)

    return pl.pallas_call(
        kernel,
        grid=(count // rows,),
        in_specs=[pl.BlockSpec((rows, units), lambda i: (i, 0)), once((units, width))],
        out_specs=pl.BlockSpec((rows, width), lambda i: (i, 0)),
        out_shape=jax.ShapeDtypeStruct((count, width), bf16),
        compiler_params=kernel_params(58),
        cost_estimate=light,
    )(activation, down_rows)


def rotary(positions):
    half = HEAD // 2
    frequency = rope_base ** (-(jnp.arange(half, dtype=f32) * 2.0) / HEAD)
    angles = positions.astype(f32)[:, None] * frequency[None, :]
    cosine, sine = jnp.cos(angles), jnp.sin(angles)
    return jnp.concatenate([cosine, cosine], 1), jnp.concatenate([-sine, sine], 1)


def fence(*values):
    return lax.optimization_barrier(values)


def added(left_side, right_side):
    def kernel(a_ref, b_ref, out_ref):
        out_ref[...] = (a_ref[...].astype(f32) + b_ref[...].astype(f32)).astype(out_ref.dtype)

    def one(a, b):
        steps = [n for n in (2, 3, 5) if a.ndim == 2 and a.shape[0] % (16 * n) == 0]
        if not steps:
            return (a.astype(f32) + b.astype(f32)).astype(a.dtype)
        block = pl.BlockSpec((a.shape[0] // steps[0], a.shape[1]), lambda i: (i, 0))
        return pl.pallas_call(
            kernel,
            grid=(steps[0],),
            in_specs=[block] * 2,
            out_specs=block,
            out_shape=jax.ShapeDtypeStruct(a.shape, a.dtype),
            compiler_params=kernel_params(16),
            cost_estimate=light,
        )(a, b)

    return jax.tree.map(one, left_side, right_side)


class CtxLine:
    def __init__(self):
        place = lax.axis_index("ctx")
        self.outer = (place == 0) | (place == 3)
        self.waiting = []
        self.chunks, self.inward, self.across, self.pair_sums = [], [], [], []
        self.totals, self.outward = [], []

    def add(self, chunks):
        self.waiting += list(chunks)
        self.send()

    def send(self):
        ready = len(self.pair_sums)
        while self.waiting and len(self.chunks) < ready + (2 if ready > 2 else 1):
            chunk = self.waiting.pop(0)
            if ready > 2:
                self.inward[-1], chunk = fence(self.inward[-1], chunk)
            self.chunks.append(chunk)
            self.inward.append(lax.ppermute(chunk, "ctx", [(0, 1), (3, 2)]))

    def round(self, *values):
        step = len(self.pair_sums)
        more = step < len(self.chunks)
        last = len(self.totals)
        if more:
            self.inward[step], values = fence(self.inward[step], values)
            self.pair_sums.append(added(self.chunks[step], self.inward[step]))
        held = [
            (self.across, slice(last, None)),
            (self.pair_sums, slice(last + 1, None)),
            (self.outward, slice(last - 1, None) if last else slice(0, 0)),
        ]
        fenced, self.waiting, values = fence([array[at] for array, at in held], self.waiting, values)
        for (array, at), value in zip(held, fenced):
            array[at] = value
        self.send()
        if len(self.across) > last:
            self.totals.append(added(self.pair_sums[last], self.across[last]))
            self.outward.append(lax.ppermute(self.totals[-1], "ctx", [(1, 0), (2, 3)]))
        if more:
            self.across.append(lax.ppermute(self.pair_sums[step], "ctx", [(1, 2), (2, 1)]))
        return values

    def sums(self, first, last):
        return jax.tree.map(
            lambda back, total: jnp.where(self.outer, back, total),
            self.outward[first:last],
            self.totals[first:last],
        )


def summed_in_plane(vector):
    size = lax.axis_size("fsdp")
    bit = 1
    while bit < size:
        vector = vector + lax.ppermute(vector, "fsdp", [(j, j ^ bit) for j in range(size)])
        bit *= 2
    return vector


def local(
    tokens_in,
    block_order,
    norm_attn,
    w_qkv,
    b_qkv,
    w_out,
    norm_mlp,
    w_gate,
    w_up,
    w_down,
    cotangent,
):
    rows, width = tokens_in.shape
    shards = lax.axis_size("fsdp")
    blocks = lax.axis_size("ctx")
    shard = lax.axis_index("fsdp")
    place = lax.axis_index("ctx")
    shard_rows = w_gate.shape[0]
    units = w_down.shape[0]
    orders = block_order[0]
    owners = jnp.concatenate([place[None], (place - jnp.arange(blocks)) % blocks])
    info = jnp.sum(
        jnp.where(owners[:, None] == jnp.arange(blocks)[None, :], orders[None, :], 0), 1
    )
    info = jnp.concatenate([info, owners[1:]]).astype(jnp.int32)
    cosine, sine = rotary(info[0] * rows + jnp.arange(rows, dtype=jnp.int32))

    def turn(parts):
        return lax.all_to_all(parts, "fsdp", 0, 0)

    qkv_all = lax.all_gather(w_qkv, "fsdp", axis=0, tiled=True)
    vectors = lax.all_gather(jnp.concatenate([norm_attn, norm_mlp, b_qkv]), "fsdp", axis=0)
    part = 2 * shard_rows // 3 // blocks
    shared = part * blocks
    weights = (w_gate, w_up)
    parts = jnp.concatenate(
        [lax.dynamic_slice_in_dim(weight, place * part, part, 0) for weight in weights]
    )
    vectors, parts = fence(vectors, split_columns(parts, shards))
    pieces = [turn(parts)]

    def ring(piece):
        return lax.ppermute(piece, "ctx", [(j, (j + 1) % blocks) for j in range(blocks)])

    pieces.append(ring(pieces[0]))
    full = padded(units)
    down_rows = jnp.concatenate([w_down, jnp.zeros((full - units, width), bf16)])
    direct = split_columns(jnp.concatenate([weight[shared:] for weight in weights]), shards)
    gain_attn = vectors[:, :shard_rows].reshape(1, -1).astype(f32)
    gain_mlp = vectors[:, shard_rows : 2 * shard_rows].reshape(1, -1).astype(f32)
    bias_all = vectors[:, 2 * shard_rows :].reshape(1, -1).astype(f32)
    qkv_all, pieces, down_rows = fence(qkv_all, pieces, down_rows)
    out_all = lax.all_gather(w_out, "fsdp", axis=0, tiled=True)

    normed, query, keys_values = project(tokens_in, gain_attn, qkv_all, bias_all, cosine, sine)
    keys_values, direct = fence(keys_values, direct)
    direct = turn(direct)
    kv_pieces = [keys_values] + [
        lax.ppermute(keys_values, "ctx", [(j, (j + s) % blocks) for j in range(blocks)])
        for s in range(1, blocks)
    ]
    kv_pieces, pieces, own_cot = fence(kv_pieces, pieces, cotangent)
    for _ in range(2, blocks - 1):
        pieces.append(ring(pieces[-1]))

    def from_chip(chip):
        return lax.ppermute(own_cot, "fsdp", [(j, j ^ chip) for j in range(shards)])

    chips = [chip for chip in range(2, shards, 2) if chip & (chip - 1) == 0]
    cot_pieces = {chip: from_chip(chip) for chip in chips}
    mixed, totals = attend(info, query, kv_pieces)
    mixed, direct = fence(mixed, direct)
    source = tokens_in.astype(f32)
    hidden = source + dot(mixed, out_all, 1, 0)
    scale_two = lax.rsqrt(jnp.mean(hidden * hidden, -1, keepdims=True) + norm_eps)
    normed_two = (hidden * scale_two * gain_mlp).astype(bf16)

    normed_two, pieces, cot_pieces = fence(normed_two, pieces, cot_pieces)
    pieces.append(ring(pieces[-1]))
    normed_all = lax.all_gather(normed_two, "fsdp", axis=0, tiled=True)
    cot_pieces[0] = own_cot
    for chip in range(2, shards, 2):
        if chip not in cot_pieces:
            cot_pieces[chip] = from_chip(chip)
            cot_pieces[chip], pieces = fence(cot_pieces[chip], pieces)
    for chip in range(0, shards, 2):
        cot_pieces[chip ^ 1] = lax.ppermute(
            cot_pieces[chip], "fsdp", [(j, j ^ 1) for j in range(shards)]
        )
    order = list(cot_pieces)

    def cot_moves(place, shard):
        return [
            (i, pl.ds(0, rows), 0, pl.ds((shard ^ bits) * rows, rows))
            for i, bits in enumerate(order)
        ]

    (cot_all,) = moved(cot_moves, [cot_pieces[bits] for bits in order], [(shards * rows, width)])

    groups = shard_rows // part
    grouped = (shards, groups, part, full)
    rest = groups - blocks

    def column_moves(place, shard):
        every = pl.ds(0, shards)
        listed = []
        for k in range(2):
            for s in range(blocks):
                group = lax.rem(place - s + blocks, blocks)
                listed.append((s, (every, k), k, (every, group)))
            listed.append((blocks, (every, pl.ds(k * rest, rest)), k, (every, pl.ds(blocks, rest))))
        return listed

    sources = [piece.reshape(shards, 2, part, full) for piece in pieces]
    sources.append(direct.reshape(shards, 2 * rest, part, full))
    columns = moved(column_moves, sources, [grouped] * 2)
    gate_cols, up_cols = (array.reshape(width, full) for array in columns)
    cuts = 2
    activation, to_gate, to_up, *down_terms = feed_forward(
        normed_all, cot_all, gate_cols, up_cols, units, rows, cuts
    )

    def to_rows(terms):
        return turn(terms.reshape(shards, shard_rows, full)).reshape(width, full)

    def merged(terms):
        return merge_columns(terms.reshape(shards, shard_rows, full), units)

    def to_owner(terms):
        return lax.psum_scatter(terms, "fsdp", scatter_dimension=0, tiled=True)

    def through_attention(part_grad):
        part_grad = part_grad.astype(f32)
        scaled = part_grad * gain_mlp
        grad_hidden = (
            cotangent.astype(f32)
            + scale_two * scaled
            - hidden * scale_two**3 * jnp.mean(hidden * scaled, -1, keepdims=True)
        )
        gain_terms = jnp.sum(part_grad * hidden * scale_two, 0)
        grad_branch = grad_hidden.astype(bf16)
        grad_mixed = dot(grad_branch, out_all, 1, 1).astype(bf16)
        grad_query, kv_terms = attend_back(
            info, query, grad_mixed, totals, cosine, sine, kv_pieces
        )
        return grad_hidden, gain_terms, grad_branch, grad_query, kv_terms

    def kv_owner(kv_terms):
        return lax.psum_scatter(kv_terms, "ctx", scatter_dimension=0)

    def projected_grad(grad_query, kv_terms):
        grad_kv = kv_terms.astype(f32)
        grad_key = grad_kv[0].reshape(rows, KV_HEADS, HEAD)
        rolled = jnp.concatenate([grad_key[..., HEAD // 2 :], grad_key[..., : HEAD // 2]], -1)
        grad_key = grad_key * cosine[:, None, :] - rolled * sine[:, None, :]
        return jnp.concatenate(
            [grad_query, grad_key.reshape(rows, K_WIDTH).astype(bf16), grad_kv[1].astype(bf16)], 1
        )

    def to_tokens(grad_projected, grad_hidden):
        scale_one = lax.rsqrt(jnp.mean(source * source, -1, keepdims=True) + norm_eps)
        grad_normed = dot(grad_projected, qkv_all, 1, 1)
        scaled = grad_normed * gain_attn
        grad_tokens = (
            grad_hidden
            + scale_one * scaled
            - source * scale_one**3 * jnp.mean(source * scaled, -1, keepdims=True)
        ).astype(bf16)
        bias_terms = jnp.sum(grad_projected.astype(f32), 0)
        return grad_tokens, jnp.sum(grad_normed * source * scale_one, 0), bias_terms

    def out_grad(mixed, grad_branch):
        return dot(mixed, grad_branch, 0, 0).astype(bf16)

    def own_sums(*terms):
        total = summed_in_plane(jnp.concatenate([t.reshape(shards, -1) for t in terms], 1))
        return lax.dynamic_index_in_dim(total, shard, 0, False)

    grad_gate, grad_up = unit_grads(cot_all, down_rows, to_gate, to_up, rows)
    mlp_grad = through_columns(grad_gate, grad_up, gate_cols, up_cols, rows)
    if blocks == 4:
        line = CtxLine()
        line.add(down_terms)
        mlp_grad, grad_gate, grad_up, act = line.round(
            mlp_grad, grad_gate, grad_up, activation
        )
        part_grad = to_owner(mlp_grad)
        gate_terms = column_grad(normed_all, grad_gate, cuts)
        (up_terms,) = column_grad(normed_all, grad_up, 1)
        gate_terms, up_terms, act = line.round(gate_terms, up_terms, act)
        line.add(gate_terms)
        up_terms = to_rows(up_terms)
        grad_hidden, gain_mlp_terms, grad_branch, grad_query, kv_terms = through_attention(
            part_grad
        )
        kv_sums = kv_owner(kv_terms)
        grad_hidden, grad_branch, grad_query, mixed_now, kv_terms, up_terms = line.round(
            grad_hidden, grad_branch, grad_query, mixed, kv_terms, up_terms
        )
        out_terms = out_grad(mixed_now, grad_branch)
        split = width // 2
        line.add([up_terms[:split], up_terms[split:]])
        grad_query, out_terms = line.round(grad_query, out_terms)
        out_terms = to_owner(out_terms)
        grad_projected = projected_grad(grad_query, kv_sums)
        qkv_terms = dot(normed, grad_projected, 0, 0).astype(bf16)
        grad_tokens, gain_attn_terms, bias_terms = to_tokens(grad_projected, grad_hidden)
        qkv_terms, grad_tokens, gain_attn_terms, bias_terms, act = line.round(
            qkv_terms, grad_tokens, gain_attn_terms, bias_terms, act
        )
        qkv_terms = to_owner(qkv_terms)
        small = own_sums(gain_attn_terms, gain_mlp_terms, bias_terms)
        mlp_terms = through_rows(act, down_rows, rows)
        small, mlp_terms, out_terms = line.round(small, mlp_terms, out_terms)
        mlp_out = to_owner(mlp_terms)
        line.add([out_terms])
        gate_terms = to_rows(jnp.concatenate(line.sums(cuts, 2 * cuts)))
        (qkv_terms,) = line.round(qkv_terms)
        line.add([[qkv_terms, small]])
        line.round()
        (gate_terms,) = line.round(gate_terms)
        down_sums = line.sums(0, cuts)
        up_sum, up_more, out_sum, (qkv_sum, small) = line.sums(2 * cuts, 2 * cuts + 4)
        up_terms = jnp.concatenate([up_sum, up_more])
    else:
        part_grad = to_owner(mlp_grad)
        gate_terms = column_grad(normed_all, grad_gate, cuts)
        up_terms = column_grad(normed_all, grad_up, cuts)
        gate_terms, up_terms = (to_rows(jnp.concatenate(t)) for t in (gate_terms, up_terms))
        mlp_out = to_owner(through_rows(activation, down_rows, rows))
        grad_hidden, gain_mlp_terms, grad_branch, grad_query, kv_terms = through_attention(
            part_grad
        )
        kv_terms = kv_owner(kv_terms)
        out_terms = to_owner(out_grad(mixed, grad_branch))
        grad_projected = projected_grad(grad_query, kv_terms)
        qkv_terms = to_owner(dot(normed, grad_projected, 0, 0).astype(bf16))
        grad_tokens, gain_attn_terms, bias_terms = to_tokens(grad_projected, grad_hidden)
        small = own_sums(gain_attn_terms, gain_mlp_terms, bias_terms)
        down_sums, gate_terms, up_terms, out_sum, qkv_sum, small = lax.psum(
            (down_terms, gate_terms, up_terms, out_terms, qkv_terms, small), "ctx"
        )

    grad_down_w = jnp.concatenate(down_sums).astype(f32)
    grad_out_w = out_sum.astype(f32)
    grad_qkv_w = qkv_sum.astype(f32)
    out_tokens = (hidden + mlp_out.astype(f32)).astype(bf16)

    return (
        out_tokens,
        grad_tokens,
        small[:shard_rows],
        grad_qkv_w,
        small[2 * shard_rows :],
        grad_out_w,
        small[shard_rows : 2 * shard_rows],
        merged(gate_terms),
        merged(up_terms),
        grad_down_w,
    )


def solution(mesh):
    in_specs = (
        P(("fsdp", "ctx"), None),
        P("fsdp", None),
        P("fsdp"),
        P("fsdp", None),
        P("fsdp"),
        P("fsdp", None),
        P("fsdp"),
        P("fsdp", None),
        P("fsdp", None),
        P("fsdp", None),
        P(("fsdp", "ctx"), None),
    )
    out_specs = (
        P(("fsdp", "ctx"), None),
        P(("fsdp", "ctx"), None),
        P("fsdp"),
        P("fsdp", None),
        P("fsdp"),
        P("fsdp", None),
        P("fsdp"),
        P("fsdp", None),
        P("fsdp", None),
        P("fsdp", None),
    )
    return jax.shard_map(local, mesh=mesh, in_specs=in_specs, out_specs=out_specs, check_vma=False)
```

```python
import jax
import jax.numpy as jnp
from jax import lax
from jax.experimental import pallas as pl
from jax.experimental.pallas import tpu as pltpu
from jax.sharding import PartitionSpec as P

HEADS = 12
KV_HEADS = 2
HEAD = 128
GROUP = HEADS // KV_HEADS
Q_WIDTH = HEADS * HEAD
K_WIDTH = KV_HEADS * HEAD

norm_eps = 1e-06
rope_base = 1000000.0
masked_score = -1e30
score_scale = HEAD ** (-0.5)
score_scale_two = score_scale * 1.4426950408889634
bf16 = jnp.bfloat16
f32 = jnp.float32
light = pl.CostEstimate(flops=1 << 20, bytes_accessed=1 << 16, transcendentals=0)


def dot(left_side, right_side, left_dim, right_dim):
    return lax.dot_general(
        left_side,
        right_side,
        (((left_dim,), (right_dim,)), ((), ())),
        preferred_element_type=f32,
    )


def kernel_params(mib):
    return pltpu.CompilerParams(vmem_limit_bytes=mib * 1024 * 1024)


def padded(size):
    return (size + 127) // 128 * 128


def whole(shape):
    return pl.BlockSpec(shape, lambda *_: (0,) * len(shape))


def split_columns(weight, shard_count):
    rows, width = weight.shape
    cols = width // shard_count
    full = padded(cols)
    step = 48 if rows % 48 == 0 else rows

    def kernel(in_ref, out_ref):
        for shard in range(shard_count):
            out_ref[shard, :, :cols] = in_ref[:, shard * cols : (shard + 1) * cols]
            if full > cols:
                out_ref[shard, :, cols:] = jnp.zeros((step, full - cols), weight.dtype)

    return pl.pallas_call(
        kernel,
        grid=(rows // step,),
        in_specs=[pl.BlockSpec((step, width), lambda i: (i, 0))],
        out_specs=pl.BlockSpec((shard_count, step, full), lambda i: (0, i, 0)),
        out_shape=jax.ShapeDtypeStruct((shard_count, rows, full), weight.dtype),
        compiler_params=kernel_params(32),
        cost_estimate=light,
    )(weight)


def merge_columns(parts, cols):
    shards, rows, full = parts.shape
    width = shards * cols
    step = 48 if rows % 48 == 0 else rows

    def kernel(in_ref, out_ref):
        for shard in range(shards):
            part = in_ref[shard, :, :cols]
            out_ref[:, shard * cols : (shard + 1) * cols] = part.astype(f32)

    return pl.pallas_call(
        kernel,
        grid=(rows // step,),
        in_specs=[pl.BlockSpec((shards, step, full), lambda i: (0, i, 0))],
        out_specs=pl.BlockSpec((step, width), lambda i: (i, 0)),
        out_shape=jax.ShapeDtypeStruct((rows, width), f32),
        compiler_params=kernel_params(40),
        cost_estimate=light,
    )(parts)


def moved(moves, arrays, shapes):
    def kernel(at_ref, *refs):
        sources, targets, sems = refs[: len(arrays)], refs[len(arrays) : -1], refs[-1]
        copies = [
            pltpu.make_async_copy(
                sources[source].at[where], targets[target].at[there], sems.at[i]
            )
            for i, (source, where, target, there) in enumerate(moves(at_ref[0], at_ref[1]))
        ]
        for copy in copies:
            copy.start()
        for copy in copies:
            copy.wait()

    anywhere = pl.BlockSpec(memory_space=pl.ANY)
    at = jnp.stack([lax.axis_index("ctx"), lax.axis_index("fsdp")]).astype(jnp.int32)
    return pl.pallas_call(
        kernel,
        in_specs=[pl.BlockSpec(memory_space=pltpu.SMEM)] + [anywhere] * len(arrays),
        out_specs=[anywhere] * len(shapes),
        out_shape=[jax.ShapeDtypeStruct(shape, bf16) for shape in shapes],
        scratch_shapes=[pltpu.SemaphoreType.DMA((len(moves(0, 0)),))],
        compiler_params=kernel_params(16),
        cost_estimate=light,
    )(at, *arrays)


def project(tokens_in, gain, weights, bias, cosine, sine):
    rows, width = tokens_in.shape
    tile = K_WIDTH
    query_steps = Q_WIDTH // tile

    def kernel(x_ref, gain_ref, w_ref, bias_ref, cos_ref, sin_ref, normed_ref, q_ref, kv_ref):
        step = pl.program_id(0)

        @pl.when(step == 0)
        def _():
            source = x_ref[...].astype(f32)
            scale = lax.rsqrt(jnp.mean(source * source, -1, keepdims=True) + norm_eps)
            normed_ref[...] = (source * scale * gain_ref[...]).astype(bf16)

        out = dot(normed_ref[...], w_ref[...], 1, 0) + bias_ref[...]
        heads = []
        for head in range(tile // HEAD):
            part = out[:, head * HEAD : (head + 1) * HEAD]
            turned = part * cos_ref[...] + pltpu.roll(part, HEAD // 2, 1) * sin_ref[...]
            heads.append(jnp.where(step <= query_steps, turned, part).astype(bf16))

        @pl.when(step < query_steps)
        def _():
            for head, value in enumerate(heads):
                q_ref[:, head * HEAD : (head + 1) * HEAD] = value

        @pl.when(step >= query_steps)
        def _():
            for head, value in enumerate(heads):
                kv_ref[:, head * HEAD : (head + 1) * HEAD] = value

    return pl.pallas_call(
        kernel,
        grid=(query_steps + 2,),
        in_specs=[
            whole((rows, width)),
            whole((1, width)),
            pl.BlockSpec((width, tile), lambda i: (0, i)),
            pl.BlockSpec((1, tile), lambda i: (0, i)),
            whole((rows, HEAD)),
            whole((rows, HEAD)),
        ],
        out_specs=[
            whole((rows, width)),
            pl.BlockSpec((rows, tile), lambda i: (0, jnp.minimum(i, query_steps - 1))),
            pl.BlockSpec((rows, tile), lambda i: (0, jnp.maximum(i - query_steps, 0))),
        ],
        out_shape=[
            jax.ShapeDtypeStruct((rows, width), bf16),
            jax.ShapeDtypeStruct((rows, Q_WIDTH), bf16),
            jax.ShapeDtypeStruct((rows, 2 * K_WIDTH), bf16),
        ],
        compiler_params=kernel_params(32),
        cost_estimate=light,
    )(tokens_in, gain, weights, bias, cosine, sine)


def fill_bias(info_ref, bias_ref, count, rows):
    query_pos = info_ref[0] * rows + lax.broadcasted_iota(jnp.int32, (rows, rows), 1)
    for piece in range(count):
        key_pos = info_ref[1 + piece] * rows + lax.broadcasted_iota(jnp.int32, (rows, rows), 0)
        bias_ref[piece * rows : (piece + 1) * rows, :] = jnp.where(
            key_pos <= query_pos, 0.0, masked_score
        )


def attend(info, query, kv_pieces):
    rows = query.shape[0]
    count = len(kv_pieces)

    def kernel(info_ref, q_ref, *refs):
        keys, values = refs[:count], refs[count : 2 * count]
        mixed_ref, total_ref, bias_ref, score_ref = refs[2 * count :]

        @pl.when(pl.program_id(0) == 0)
        def _():
            fill_bias(info_ref, bias_ref, count, rows)

        q = q_ref[...]
        top = None
        for piece in range(count):
            at = slice(piece * rows, (piece + 1) * rows)
            score = dot(keys[piece][...], q, 1, 1) * score_scale_two + bias_ref[at, :]
            score_ref[at, :] = score
            peak = jnp.max(score, 0, keepdims=True)
            top = peak if top is None else jnp.maximum(top, peak)
        total = jnp.zeros((1, rows), f32)
        mixed = jnp.zeros((HEAD, rows), f32)
        for piece in range(count):
            weight = jnp.exp2(score_ref[piece * rows : (piece + 1) * rows, :] - top)
            total += jnp.sum(weight, 0, keepdims=True)
            mixed += dot(values[piece][...], weight.astype(bf16), 0, 0)
        mixed_ref[...] = (mixed / total).T.astype(bf16)
        total_ref[0] = top + jnp.log2(total)

    key_spec = pl.BlockSpec((rows, HEAD), lambda h: (0, h // GROUP))
    value_spec = pl.BlockSpec((rows, HEAD), lambda h: (0, KV_HEADS + h // GROUP))
    head_spec = pl.BlockSpec((rows, HEAD), lambda h: (0, h))
    return pl.pallas_call(
        kernel,
        grid=(HEADS,),
        in_specs=[pl.BlockSpec(memory_space=pltpu.SMEM), head_spec]
        + [key_spec] * count
        + [value_spec] * count,
        out_specs=[head_spec, pl.BlockSpec((1, 1, rows), lambda h: (h, 0, 0))],
        out_shape=[
            jax.ShapeDtypeStruct((rows, Q_WIDTH), bf16),
            jax.ShapeDtypeStruct((HEADS, 1, rows), f32),
        ],
        scratch_shapes=[pltpu.VMEM((count * rows, rows), f32)] * 2,
        compiler_params=kernel_params(32),
        cost_estimate=light,
    )(info, query, *kv_pieces, *kv_pieces)


def norm_back(part_grad, cotangent, hidden, gain, out_all):
    rows, width = hidden.shape
    tile = 256

    def kernel(p_ref, c_ref, h_ref, gain_ref, w_ref, gh_ref, gain_out_ref, branch_ref, mixed_ref):
        @pl.when(pl.program_id(0) == 0)
        def _():
            part, h = p_ref[...].astype(f32), h_ref[...]
            scale = lax.rsqrt(jnp.mean(h * h, -1, keepdims=True) + norm_eps)
            scaled = part * gain_ref[...]
            grad = (
                c_ref[...].astype(f32)
                + scale * scaled
                - h * (scale * scale * scale) * jnp.mean(h * scaled, -1, keepdims=True)
            )
            gh_ref[...] = grad
            gain_out_ref[...] = jnp.sum(part * h * scale, 0, keepdims=True)
            branch_ref[...] = grad.astype(bf16)

        mixed_ref[...] = dot(branch_ref[...], w_ref[...], 1, 1).astype(bf16)

    return pl.pallas_call(
        kernel,
        grid=(out_all.shape[0] // tile,),
        in_specs=[whole((rows, width))] * 3
        + [whole((1, width)), pl.BlockSpec((tile, width), lambda i: (i, 0))],
        out_specs=[whole((rows, width)), whole((1, width)), whole((rows, width))]
        + [pl.BlockSpec((rows, tile), lambda i: (0, i))],
        out_shape=[
            jax.ShapeDtypeStruct((rows, width), f32),
            jax.ShapeDtypeStruct((1, width), f32),
            jax.ShapeDtypeStruct((rows, width), bf16),
            jax.ShapeDtypeStruct((rows, out_all.shape[0]), bf16),
        ],
        compiler_params=kernel_params(32),
        cost_estimate=light,
    )(part_grad, cotangent, hidden, gain, out_all)


def attend_back(info, query, grad_mixed, totals, cosine, sine, kv_pieces):
    rows = query.shape[0]
    count = len(kv_pieces)

    def kernel(info_ref, q_ref, g_ref, total_ref, cos_ref, sin_ref, *refs):
        keys, values = refs[:count], refs[count : 2 * count]
        dq_ref = refs[2 * count]
        kv_ref, bias_ref, p_ref, dp_ref, sum_ref = refs[2 * count + 1 :]
        head = pl.program_id(0)

        @pl.when(head == 0)
        def _():
            fill_bias(info_ref, bias_ref, count, rows)

        @pl.when(head % GROUP == 0)
        def _():
            sum_ref[...] = jnp.zeros_like(sum_ref)

        q, g, total = q_ref[...], g_ref[...], total_ref[0]
        delta = jnp.zeros((1, rows), f32)
        for piece in range(count):
            at = slice(piece * rows, (piece + 1) * rows)
            score = dot(keys[piece][...], q, 1, 1) * score_scale_two + bias_ref[at, :]
            p = jnp.exp2(score - total)
            dp = dot(values[piece][...], g, 1, 1)
            p_ref[at, :] = p
            dp_ref[at, :] = dp
            delta += jnp.sum(p * dp, 0, keepdims=True)
        dq = jnp.zeros((HEAD, rows), f32)
        for piece in range(count):
            at = slice(piece * rows, (piece + 1) * rows)
            p = p_ref[at, :]
            ds = (p * (dp_ref[at, :] - delta) * score_scale).astype(bf16)
            dq += dot(keys[piece][...], ds, 0, 0)
            sum_ref[piece, 0] += dot(ds, q, 1, 0)
            sum_ref[piece, 1] += dot(p.astype(bf16), g, 1, 0)
        dq = dq.T
        dq_ref[...] = (dq * cos_ref[...] - pltpu.roll(dq, HEAD // 2, 1) * sin_ref[...]).astype(bf16)

        @pl.when(head % GROUP == GROUP - 1)
        def _():
            for piece in range(count):
                kv_ref[info_ref[1 + count + piece]] = sum_ref[piece].astype(bf16)

    key_spec = pl.BlockSpec((rows, HEAD), lambda h: (0, h // GROUP))
    value_spec = pl.BlockSpec((rows, HEAD), lambda h: (0, KV_HEADS + h // GROUP))
    head_spec = pl.BlockSpec((rows, HEAD), lambda h: (0, h))
    return pl.pallas_call(
        kernel,
        grid=(HEADS,),
        in_specs=[
            pl.BlockSpec(memory_space=pltpu.SMEM),
            head_spec,
            head_spec,
            pl.BlockSpec((1, 1, rows), lambda h: (h, 0, 0)),
            whole((rows, HEAD)),
            whole((rows, HEAD)),
        ]
        + [key_spec] * count
        + [value_spec] * count,
        out_specs=[head_spec]
        + [pl.BlockSpec((count, 2, rows, HEAD), lambda h: (0, 0, 0, h // GROUP))],
        out_shape=[jax.ShapeDtypeStruct((rows, Q_WIDTH), bf16)]
        + [jax.ShapeDtypeStruct((count, 2, rows, K_WIDTH), bf16)],
        scratch_shapes=[pltpu.VMEM((count * rows, rows), f32)] * 3
        + [pltpu.VMEM((count, 2, rows, HEAD), f32)],
        compiler_params=kernel_params(32),
        cost_estimate=light,
    )(info, query, grad_mixed, totals, cosine, sine, *kv_pieces, *kv_pieces)


def once(shape):
    return pl.BlockSpec(shape, lambda *_: (0,) * len(shape), pipeline_mode=pl.Buffered(1))


def token_rows(count, rows):
    return 2 * rows if count % (2 * rows) == 0 else rows


def feed_forward(normed, cotangent, gate_cols, up_cols, units_here, rows, cuts):
    count, width = normed.shape
    units = gate_cols.shape[1]
    rows = token_rows(count, rows)
    steps, part, tile = count // rows, units_here // cuts, 256

    def kernel(x_ref, c_ref, wg_ref, wu_ref, act_ref, to_gate_ref, to_up_ref, *refs):
        down_refs, turned_ref = refs[:cuts], refs[cuts]
        step = pl.program_id(0)

        @pl.when(step < steps)
        def _():
            x = x_ref[...]
            gate = dot(x, wg_ref[...], 1, 0)
            up = dot(x, wu_ref[...], 1, 0)
            sigmoid = jax.nn.sigmoid(gate)
            swished = gate * sigmoid
            act = (swished * up).astype(bf16)
            act_ref[...] = act
            turned_ref[:, pl.ds(pl.multiple_of(step * rows, rows), rows)] = act.T
            to_up_ref[...] = swished.astype(bf16)
            to_gate_ref[...] = (up * sigmoid * (1.0 + gate * (1.0 - sigmoid))).astype(bf16)

        @pl.when(step >= steps)
        def _():
            for cut, down_ref in enumerate(down_refs):
                turned = turned_ref[cut * part : (cut + 1) * part, :]
                down_ref[...] = dot(turned, c_ref[...], 1, 0).astype(bf16)

    def early(i):
        return (jnp.minimum(i, steps - 1), 0)

    def late(i):
        return (0, jnp.maximum(i - steps, 0))

    return pl.pallas_call(
        kernel,
        grid=(steps + width // tile,),
        in_specs=[
            pl.BlockSpec((rows, width), early),
            pl.BlockSpec((count, tile), late),
            once((width, units)),
            once((width, units)),
        ],
        out_specs=[pl.BlockSpec((rows, units), early)] * 3 + [pl.BlockSpec((part, tile), late)] * cuts,
        out_shape=[jax.ShapeDtypeStruct((count, units), bf16)] * 3
        + [jax.ShapeDtypeStruct((part, width), bf16)] * cuts,
        scratch_shapes=[pltpu.VMEM((units, count), bf16)],
        compiler_params=kernel_params(58),
        cost_estimate=light,
    )(normed, cotangent, gate_cols, up_cols)


def unit_grads(cotangent, down_rows, to_gate, to_up, rows):
    count, width = cotangent.shape
    units = down_rows.shape[0]
    rows = token_rows(count, rows)

    def kernel(c_ref, wd_ref, tg_ref, tu_ref, dg_ref, du_ref):
        grad_act = dot(c_ref[...], wd_ref[...], 1, 1)
        dg_ref[...] = (grad_act * tg_ref[...].astype(f32)).astype(bf16)
        du_ref[...] = (grad_act * tu_ref[...].astype(f32)).astype(bf16)

    unit_spec = pl.BlockSpec((rows, units), lambda i: (i, 0))
    return pl.pallas_call(
        kernel,
        grid=(count // rows,),
        in_specs=[
            pl.BlockSpec((rows, width), lambda i: (i, 0)),
            once((units, width)),
            unit_spec,
            unit_spec,
        ],
        out_specs=[unit_spec] * 2,
        out_shape=[jax.ShapeDtypeStruct((count, units), bf16)] * 2,
        compiler_params=kernel_params(58),
        cost_estimate=light,
    )(cotangent, down_rows, to_gate, to_up)


def through_columns(grad_gate, grad_up, gate_cols, up_cols, rows):
    count, units = grad_gate.shape
    width = gate_cols.shape[0]
    rows = token_rows(count, rows)

    def kernel(dg_ref, du_ref, wg_ref, wu_ref, out_ref):
        out = dot(dg_ref[...], wg_ref[...], 1, 1) + dot(du_ref[...], wu_ref[...], 1, 1)
        out_ref[...] = out.astype(bf16)

    unit_spec = pl.BlockSpec((rows, units), lambda i: (i, 0))
    return pl.pallas_call(
        kernel,
        grid=(count // rows,),
        in_specs=[unit_spec, unit_spec, once((width, units)), once((width, units))],
        out_specs=pl.BlockSpec((rows, width), lambda i: (i, 0)),
        out_shape=jax.ShapeDtypeStruct((count, width), bf16),
        compiler_params=kernel_params(58),
        cost_estimate=light,
    )(grad_gate, grad_up, gate_cols, up_cols)


def column_grad(normed, grad, cuts):
    count, width = normed.shape
    units = grad.shape[1]
    tile = 256
    each = width // tile // cuts

    def kernel(x_ref, g_ref, *out_refs):
        step = pl.program_id(0)
        out = dot(x_ref[...].T, g_ref[...], 1, 0).astype(bf16)
        for cut, out_ref in enumerate(out_refs):

            @pl.when(step // each == cut)
            def _():
                out_ref[...] = out

    def cut_spec(cut):
        return pl.BlockSpec((tile, units), lambda i: (jnp.clip(i - cut * each, 0, each - 1), 0))

    return pl.pallas_call(
        kernel,
        grid=(width // tile,),
        in_specs=[pl.BlockSpec((count, tile), lambda i: (0, i)), once((count, units))],
        out_specs=[cut_spec(cut) for cut in range(cuts)],
        out_shape=[jax.ShapeDtypeStruct((width // cuts, units), bf16)] * cuts,
        compiler_params=kernel_params(58),
        cost_estimate=light,
    )(normed, grad)


def through_rows(activation, down_rows, rows):
    count, units = activation.shape
    width = down_rows.shape[1]
    rows = token_rows(count, rows)

    def kernel(act_ref, wd_ref, out_ref):
        out_ref[...] = dot(act_ref[...], wd_ref[...], 1, 0).astype(bf16)

    return pl.pallas_call(
        kernel,
        grid=(count // rows,),
        in_specs=[pl.BlockSpec((rows, units), lambda i: (i, 0)), once((units, width))],
        out_specs=pl.BlockSpec((rows, width), lambda i: (i, 0)),
        out_shape=jax.ShapeDtypeStruct((count, width), bf16),
        compiler_params=kernel_params(58),
        cost_estimate=light,
    )(activation, down_rows)


def rotary(positions):
    half = HEAD // 2
    frequency = rope_base ** (-(jnp.arange(half, dtype=f32) * 2.0) / HEAD)
    angles = positions.astype(f32)[:, None] * frequency[None, :]
    cosine, sine = jnp.cos(angles), jnp.sin(angles)
    return jnp.concatenate([cosine, cosine], 1), jnp.concatenate([-sine, sine], 1)


def fence(*values):
    return lax.optimization_barrier(values)


def added(left_side, right_side):
    def kernel(a_ref, b_ref, out_ref):
        out_ref[...] = (a_ref[...].astype(f32) + b_ref[...].astype(f32)).astype(out_ref.dtype)

    def one(a, b):
        steps = [n for n in (2, 3, 5) if a.ndim == 2 and a.shape[0] % (16 * n) == 0]
        if not steps:
            return (a.astype(f32) + b.astype(f32)).astype(a.dtype)
        block = pl.BlockSpec((a.shape[0] // steps[0], a.shape[1]), lambda i: (i, 0))
        return pl.pallas_call(
            kernel,
            grid=(steps[0],),
            in_specs=[block] * 2,
            out_specs=block,
            out_shape=jax.ShapeDtypeStruct(a.shape, a.dtype),
            compiler_params=kernel_params(16),
            cost_estimate=light,
        )(a, b)

    return jax.tree.map(one, left_side, right_side)


class CtxLine:
    def __init__(self):
        place = lax.axis_index("ctx")
        self.outer = (place == 0) | (place == 3)
        self.waiting = []
        self.chunks, self.inward, self.across, self.pair_sums = [], [], [], []
        self.totals, self.outward = [], []

    def add(self, chunks):
        self.waiting += list(chunks)
        self.send()

    def send(self):
        ready = len(self.pair_sums)
        while self.waiting and len(self.chunks) < ready + (2 if ready > 2 else 1):
            chunk = self.waiting.pop(0)
            if ready > 2:
                self.inward[-1], chunk = fence(self.inward[-1], chunk)
            self.chunks.append(chunk)
            self.inward.append(lax.ppermute(chunk, "ctx", [(0, 1), (3, 2)]))

    def round(self, *values):
        step = len(self.pair_sums)
        more = step < len(self.chunks)
        last = len(self.totals)
        if more:
            self.inward[step], values = fence(self.inward[step], values)
            self.pair_sums.append(added(self.chunks[step], self.inward[step]))
        held = [
            (self.across, slice(last, None)),
            (self.pair_sums, slice(last + 1, None)),
            (self.outward, slice(last - 1, None) if last else slice(0, 0)),
        ]
        fenced, self.waiting, values = fence([array[at] for array, at in held], self.waiting, values)
        for (array, at), value in zip(held, fenced):
            array[at] = value
        self.send()
        if len(self.across) > last:
            self.totals.append(added(self.pair_sums[last], self.across[last]))
            self.outward.append(lax.ppermute(self.totals[-1], "ctx", [(1, 0), (2, 3)]))
        if more:
            self.across.append(lax.ppermute(self.pair_sums[step], "ctx", [(1, 2), (2, 1)]))
        return values

    def sums(self, first, last):
        return jax.tree.map(
            lambda back, total: jnp.where(self.outer, back, total),
            self.outward[first:last],
            self.totals[first:last],
        )


def summed_in_plane(vector):
    size = lax.axis_size("fsdp")
    bit = 1
    while bit < size:
        vector = vector + lax.ppermute(vector, "fsdp", [(j, j ^ bit) for j in range(size)])
        bit *= 2
    return vector


def local(
    tokens_in,
    block_order,
    norm_attn,
    w_qkv,
    b_qkv,
    w_out,
    norm_mlp,
    w_gate,
    w_up,
    w_down,
    cotangent,
):
    rows, width = tokens_in.shape
    shards = lax.axis_size("fsdp")
    blocks = lax.axis_size("ctx")
    shard = lax.axis_index("fsdp")
    place = lax.axis_index("ctx")
    shard_rows = w_gate.shape[0]
    units = w_down.shape[0]
    orders = block_order[0]
    owners = jnp.concatenate([place[None], (place - jnp.arange(blocks)) % blocks])
    info = jnp.sum(
        jnp.where(owners[:, None] == jnp.arange(blocks)[None, :], orders[None, :], 0), 1
    )
    info = jnp.concatenate([info, owners[1:]]).astype(jnp.int32)
    cosine, sine = rotary(info[0] * rows + jnp.arange(rows, dtype=jnp.int32))

    def turn(parts):
        return lax.all_to_all(parts, "fsdp", 0, 0)

    qkv_all = lax.all_gather(w_qkv, "fsdp", axis=0, tiled=True)
    vectors = lax.all_gather(jnp.concatenate([norm_attn, norm_mlp, b_qkv]), "fsdp", axis=0)
    part = 2 * shard_rows // 3 // blocks
    shared = part * blocks
    weights = (w_gate, w_up)
    parts = jnp.concatenate(
        [lax.dynamic_slice_in_dim(weight, place * part, part, 0) for weight in weights]
    )
    vectors, parts = fence(vectors, split_columns(parts, shards))
    pieces = [turn(parts)]

    def ring(piece):
        return lax.ppermute(piece, "ctx", [(j, (j + 1) % blocks) for j in range(blocks)])

    pieces.append(ring(pieces[0]))
    full = padded(units)
    down_rows = jnp.concatenate([w_down, jnp.zeros((full - units, width), bf16)])
    direct = split_columns(jnp.concatenate([weight[shared:] for weight in weights]), shards)
    gain_attn = vectors[:, :shard_rows].reshape(1, -1).astype(f32)
    gain_mlp = vectors[:, shard_rows : 2 * shard_rows].reshape(1, -1).astype(f32)
    bias_all = vectors[:, 2 * shard_rows :].reshape(1, -1).astype(f32)
    qkv_all, pieces, down_rows = fence(qkv_all, pieces, down_rows)
    out_all = lax.all_gather(w_out, "fsdp", axis=0, tiled=True)

    normed, query, keys_values = project(tokens_in, gain_attn, qkv_all, bias_all, cosine, sine)
    keys_values, direct = fence(keys_values, direct)
    direct = turn(direct)
    kv_pieces = [keys_values] + [
        lax.ppermute(keys_values, "ctx", [(j, (j + s) % blocks) for j in range(blocks)])
        for s in range(1, blocks)
    ]
    kv_pieces, pieces, own_cot = fence(kv_pieces, pieces, cotangent)
    for _ in range(2, blocks - 1):
        pieces.append(ring(pieces[-1]))

    def from_chip(chip):
        return lax.ppermute(own_cot, "fsdp", [(j, j ^ chip) for j in range(shards)])

    chips = [chip for chip in range(2, shards, 2) if chip & (chip - 1) == 0]
    cot_pieces = {chip: from_chip(chip) for chip in chips}
    mixed, totals = attend(info, query, kv_pieces)
    mixed, direct = fence(mixed, direct)
    source = tokens_in.astype(f32)
    hidden = source + dot(mixed, out_all, 1, 0)
    scale_two = lax.rsqrt(jnp.mean(hidden * hidden, -1, keepdims=True) + norm_eps)
    normed_two = (hidden * scale_two * gain_mlp).astype(bf16)

    normed_two, pieces, cot_pieces = fence(normed_two, pieces, cot_pieces)
    pieces.append(ring(pieces[-1]))
    normed_all = lax.all_gather(normed_two, "fsdp", axis=0, tiled=True)
    cot_pieces[0] = own_cot
    for chip in range(2, shards, 2):
        if chip not in cot_pieces:
            cot_pieces[chip] = from_chip(chip)
            cot_pieces[chip], pieces = fence(cot_pieces[chip], pieces)
    for chip in range(0, shards, 2):
        cot_pieces[chip ^ 1] = lax.ppermute(
            cot_pieces[chip], "fsdp", [(j, j ^ 1) for j in range(shards)]
        )
    order = list(cot_pieces)

    def cot_moves(place, shard):
        return [
            (i, pl.ds(0, rows), 0, pl.ds((shard ^ bits) * rows, rows))
            for i, bits in enumerate(order)
        ]

    (cot_all,) = moved(cot_moves, [cot_pieces[bits] for bits in order], [(shards * rows, width)])

    groups = shard_rows // part
    grouped = (shards, groups, part, full)
    rest = groups - blocks

    def column_moves(place, shard):
        every = pl.ds(0, shards)
        listed = []
        for k in range(2):
            for s in range(blocks):
                group = lax.rem(place - s + blocks, blocks)
                listed.append((s, (every, k), k, (every, group)))
            listed.append((blocks, (every, pl.ds(k * rest, rest)), k, (every, pl.ds(blocks, rest))))
        return listed

    sources = [piece.reshape(shards, 2, part, full) for piece in pieces]
    sources.append(direct.reshape(shards, 2 * rest, part, full))
    columns = moved(column_moves, sources, [grouped] * 2)
    gate_cols, up_cols = (array.reshape(width, full) for array in columns)
    cuts = 2
    activation, to_gate, to_up, *down_terms = feed_forward(
        normed_all, cot_all, gate_cols, up_cols, units, rows, cuts
    )

    def to_rows(terms):
        return turn(terms.reshape(shards, shard_rows, full)).reshape(width, full)

    def merged(terms):
        return merge_columns(terms.reshape(shards, shard_rows, full), units)

    def to_owner(terms):
        return lax.psum_scatter(terms, "fsdp", scatter_dimension=0, tiled=True)

    def through_attention(part_grad):
        grad_hidden, gain_terms, grad_branch, grad_mixed = norm_back(
            part_grad, cotangent, hidden, gain_mlp, out_all
        )
        gain_terms = gain_terms[0]
        grad_query, kv_terms = attend_back(
            info, query, grad_mixed, totals, cosine, sine, kv_pieces
        )
        return grad_hidden, gain_terms, grad_branch, grad_query, kv_terms

    def kv_owner(kv_terms):
        return lax.psum_scatter(kv_terms, "ctx", scatter_dimension=0)

    def projected_grad(grad_query, kv_terms):
        grad_kv = kv_terms.astype(f32)
        grad_key = grad_kv[0].reshape(rows, KV_HEADS, HEAD)
        rolled = jnp.concatenate([grad_key[..., HEAD // 2 :], grad_key[..., : HEAD // 2]], -1)
        grad_key = grad_key * cosine[:, None, :] - rolled * sine[:, None, :]
        return jnp.concatenate(
            [grad_query, grad_key.reshape(rows, K_WIDTH).astype(bf16), grad_kv[1].astype(bf16)], 1
        )

    def to_tokens(grad_projected, grad_hidden):
        scale_one = lax.rsqrt(jnp.mean(source * source, -1, keepdims=True) + norm_eps)
        grad_normed = dot(grad_projected, qkv_all, 1, 1)
        scaled = grad_normed * gain_attn
        grad_tokens = (
            grad_hidden
            + scale_one * scaled
            - source * scale_one**3 * jnp.mean(source * scaled, -1, keepdims=True)
        ).astype(bf16)
        bias_terms = jnp.sum(grad_projected.astype(f32), 0)
        return grad_tokens, jnp.sum(grad_normed * source * scale_one, 0), bias_terms

    def out_grad(mixed, grad_branch):
        return dot(mixed, grad_branch, 0, 0).astype(bf16)

    def own_sums(*terms):
        total = summed_in_plane(jnp.concatenate([t.reshape(shards, -1) for t in terms], 1))
        return lax.dynamic_index_in_dim(total, shard, 0, False)

    grad_gate, grad_up = unit_grads(cot_all, down_rows, to_gate, to_up, rows)
    mlp_grad = through_columns(grad_gate, grad_up, gate_cols, up_cols, rows)
    if blocks == 4:
        line = CtxLine()
        line.add(down_terms)
        mlp_grad, grad_gate, grad_up, act = line.round(
            mlp_grad, grad_gate, grad_up, activation
        )
        part_grad = to_owner(mlp_grad)
        gate_terms = column_grad(normed_all, grad_gate, cuts)
        (up_terms,) = column_grad(normed_all, grad_up, 1)
        gate_terms, up_terms, act = line.round(gate_terms, up_terms, act)
        line.add(gate_terms)
        up_terms = to_rows(up_terms)
        grad_hidden, gain_mlp_terms, grad_branch, grad_query, kv_terms = through_attention(
            part_grad
        )
        kv_sums = kv_owner(kv_terms)
        grad_hidden, grad_branch, grad_query, mixed_now, kv_terms, up_terms = line.round(
            grad_hidden, grad_branch, grad_query, mixed, kv_terms, up_terms
        )
        out_terms = out_grad(mixed_now, grad_branch)
        split = width // 2
        line.add([up_terms[:split], up_terms[split:]])
        grad_query, out_terms = line.round(grad_query, out_terms)
        out_terms = to_owner(out_terms)
        grad_projected = projected_grad(grad_query, kv_sums)
        qkv_terms = dot(normed, grad_projected, 0, 0).astype(bf16)
        grad_tokens, gain_attn_terms, bias_terms = to_tokens(grad_projected, grad_hidden)
        qkv_terms, grad_tokens, gain_attn_terms, bias_terms, act = line.round(
            qkv_terms, grad_tokens, gain_attn_terms, bias_terms, act
        )
        qkv_terms = to_owner(qkv_terms)
        small = own_sums(gain_attn_terms, gain_mlp_terms, bias_terms)
        mlp_terms = through_rows(act, down_rows, rows)
        small, mlp_terms, out_terms = line.round(small, mlp_terms, out_terms)
        mlp_out = to_owner(mlp_terms)
        line.add([out_terms])
        gate_terms = to_rows(jnp.concatenate(line.sums(cuts, 2 * cuts)))
        (qkv_terms,) = line.round(qkv_terms)
        line.add([[qkv_terms, small]])
        line.round()
        (gate_terms,) = line.round(gate_terms)
        down_sums = line.sums(0, cuts)
        up_sum, up_more, out_sum, (qkv_sum, small) = line.sums(2 * cuts, 2 * cuts + 4)
        up_terms = jnp.concatenate([up_sum, up_more])
    else:
        part_grad = to_owner(mlp_grad)
        gate_terms = column_grad(normed_all, grad_gate, cuts)
        up_terms = column_grad(normed_all, grad_up, cuts)
        gate_terms, up_terms = (to_rows(jnp.concatenate(t)) for t in (gate_terms, up_terms))
        mlp_out = to_owner(through_rows(activation, down_rows, rows))
        grad_hidden, gain_mlp_terms, grad_branch, grad_query, kv_terms = through_attention(
            part_grad
        )
        kv_terms = kv_owner(kv_terms)
        out_terms = to_owner(out_grad(mixed, grad_branch))
        grad_projected = projected_grad(grad_query, kv_terms)
        qkv_terms = to_owner(dot(normed, grad_projected, 0, 0).astype(bf16))
        grad_tokens, gain_attn_terms, bias_terms = to_tokens(grad_projected, grad_hidden)
        small = own_sums(gain_attn_terms, gain_mlp_terms, bias_terms)
        down_sums, gate_terms, up_terms, out_sum, qkv_sum, small = lax.psum(
            (down_terms, gate_terms, up_terms, out_terms, qkv_terms, small), "ctx"
        )

    grad_down_w = jnp.concatenate(down_sums).astype(f32)
    grad_out_w = out_sum.astype(f32)
    grad_qkv_w = qkv_sum.astype(f32)
    out_tokens = (hidden + mlp_out.astype(f32)).astype(bf16)

    return (
        out_tokens,
        grad_tokens,
        small[:shard_rows],
        grad_qkv_w,
        small[2 * shard_rows :],
        grad_out_w,
        small[shard_rows : 2 * shard_rows],
        merged(gate_terms),
        merged(up_terms),
        grad_down_w,
    )


def solution(mesh):
    in_specs = (
        P(("fsdp", "ctx"), None),
        P("fsdp", None),
        P("fsdp"),
        P("fsdp", None),
        P("fsdp"),
        P("fsdp", None),
        P("fsdp"),
        P("fsdp", None),
        P("fsdp", None),
        P("fsdp", None),
        P(("fsdp", "ctx"), None),
    )
    out_specs = (
        P(("fsdp", "ctx"), None),
        P(("fsdp", "ctx"), None),
        P("fsdp"),
        P("fsdp", None),
        P("fsdp"),
        P("fsdp", None),
        P("fsdp"),
        P("fsdp", None),
        P("fsdp", None),
        P("fsdp", None),
    )
    return jax.shard_map(local, mesh=mesh, in_specs=in_specs, out_specs=out_specs, check_vma=False)
```

```python
import jax
import jax.numpy as jnp
from jax import lax
from jax.experimental import pallas as pl
from jax.experimental.pallas import tpu as pltpu
from jax.sharding import PartitionSpec as P

HEADS = 12
KV_HEADS = 2
HEAD = 128
GROUP = HEADS // KV_HEADS
Q_WIDTH = HEADS * HEAD
K_WIDTH = KV_HEADS * HEAD

norm_eps = 1e-06
rope_base = 1000000.0
masked_score = -1e30
score_scale = HEAD ** (-0.5)
score_scale_two = score_scale * 1.4426950408889634
bf16 = jnp.bfloat16
f32 = jnp.float32
light = pl.CostEstimate(flops=1 << 20, bytes_accessed=1 << 16, transcendentals=0)


def dot(left_side, right_side, left_dim, right_dim):
    return lax.dot_general(
        left_side,
        right_side,
        (((left_dim,), (right_dim,)), ((), ())),
        preferred_element_type=f32,
    )


def kernel_params(mib):
    return pltpu.CompilerParams(vmem_limit_bytes=mib * 1024 * 1024)


def padded(size):
    return (size + 127) // 128 * 128


def whole(shape):
    return pl.BlockSpec(shape, lambda *_: (0,) * len(shape))


def split_columns(weight, shard_count):
    rows, width = weight.shape
    cols = width // shard_count
    full = padded(cols)
    step = 48 if rows % 48 == 0 else rows

    def kernel(in_ref, out_ref):
        for shard in range(shard_count):
            out_ref[shard, :, :cols] = in_ref[:, shard * cols : (shard + 1) * cols]
            if full > cols:
                out_ref[shard, :, cols:] = jnp.zeros((step, full - cols), weight.dtype)

    return pl.pallas_call(
        kernel,
        grid=(rows // step,),
        in_specs=[pl.BlockSpec((step, width), lambda i: (i, 0))],
        out_specs=pl.BlockSpec((shard_count, step, full), lambda i: (0, i, 0)),
        out_shape=jax.ShapeDtypeStruct((shard_count, rows, full), weight.dtype),
        compiler_params=kernel_params(32),
        cost_estimate=light,
    )(weight)


def merge_columns(parts, cols):
    shards, rows, full = parts.shape
    width = shards * cols
    step = 48 if rows % 48 == 0 else rows

    def kernel(in_ref, out_ref):
        for shard in range(shards):
            part = in_ref[shard, :, :cols]
            out_ref[:, shard * cols : (shard + 1) * cols] = part.astype(f32)

    return pl.pallas_call(
        kernel,
        grid=(rows // step,),
        in_specs=[pl.BlockSpec((shards, step, full), lambda i: (0, i, 0))],
        out_specs=pl.BlockSpec((step, width), lambda i: (i, 0)),
        out_shape=jax.ShapeDtypeStruct((rows, width), f32),
        compiler_params=kernel_params(40),
        cost_estimate=light,
    )(parts)


def moved(moves, arrays, shapes):
    def kernel(at_ref, *refs):
        sources, targets, sems = refs[: len(arrays)], refs[len(arrays) : -1], refs[-1]
        copies = [
            pltpu.make_async_copy(
                sources[source].at[where], targets[target].at[there], sems.at[i]
            )
            for i, (source, where, target, there) in enumerate(moves(at_ref[0], at_ref[1]))
        ]
        for copy in copies:
            copy.start()
        for copy in copies:
            copy.wait()

    anywhere = pl.BlockSpec(memory_space=pl.ANY)
    at = jnp.stack([lax.axis_index("ctx"), lax.axis_index("fsdp")]).astype(jnp.int32)
    return pl.pallas_call(
        kernel,
        in_specs=[pl.BlockSpec(memory_space=pltpu.SMEM)] + [anywhere] * len(arrays),
        out_specs=[anywhere] * len(shapes),
        out_shape=[jax.ShapeDtypeStruct(shape, bf16) for shape in shapes],
        scratch_shapes=[pltpu.SemaphoreType.DMA((len(moves(0, 0)),))],
        compiler_params=kernel_params(16),
        cost_estimate=light,
    )(at, *arrays)


def project(tokens_in, gain, weights, bias, cosine, sine):
    rows, width = tokens_in.shape
    tile = K_WIDTH
    query_steps = Q_WIDTH // tile

    def kernel(x_ref, gain_ref, w_ref, bias_ref, cos_ref, sin_ref, normed_ref, q_ref, kv_ref):
        step = pl.program_id(0)

        @pl.when(step == 0)
        def _():
            source = x_ref[...].astype(f32)
            scale = lax.rsqrt(jnp.mean(source * source, -1, keepdims=True) + norm_eps)
            normed_ref[...] = (source * scale * gain_ref[...]).astype(bf16)

        out = dot(normed_ref[...], w_ref[...], 1, 0) + bias_ref[...]
        heads = []
        for head in range(tile // HEAD):
            part = out[:, head * HEAD : (head + 1) * HEAD]
            turned = part * cos_ref[...] + pltpu.roll(part, HEAD // 2, 1) * sin_ref[...]
            heads.append(jnp.where(step <= query_steps, turned, part).astype(bf16))

        @pl.when(step < query_steps)
        def _():
            for head, value in enumerate(heads):
                q_ref[:, head * HEAD : (head + 1) * HEAD] = value

        @pl.when(step >= query_steps)
        def _():
            for head, value in enumerate(heads):
                kv_ref[:, head * HEAD : (head + 1) * HEAD] = value

    return pl.pallas_call(
        kernel,
        grid=(query_steps + 2,),
        in_specs=[
            whole((rows, width)),
            whole((1, width)),
            pl.BlockSpec((width, tile), lambda i: (0, i)),
            pl.BlockSpec((1, tile), lambda i: (0, i)),
            whole((rows, HEAD)),
            whole((rows, HEAD)),
        ],
        out_specs=[
            whole((rows, width)),
            pl.BlockSpec((rows, tile), lambda i: (0, jnp.minimum(i, query_steps - 1))),
            pl.BlockSpec((rows, tile), lambda i: (0, jnp.maximum(i - query_steps, 0))),
        ],
        out_shape=[
            jax.ShapeDtypeStruct((rows, width), bf16),
            jax.ShapeDtypeStruct((rows, Q_WIDTH), bf16),
            jax.ShapeDtypeStruct((rows, 2 * K_WIDTH), bf16),
        ],
        compiler_params=kernel_params(32),
        cost_estimate=light,
    )(tokens_in, gain, weights, bias, cosine, sine)


def fill_bias(info_ref, bias_ref, count, rows):
    query_pos = info_ref[0] * rows + lax.broadcasted_iota(jnp.int32, (rows, rows), 1)
    for piece in range(count):
        key_pos = info_ref[1 + piece] * rows + lax.broadcasted_iota(jnp.int32, (rows, rows), 0)
        bias_ref[piece * rows : (piece + 1) * rows, :] = jnp.where(
            key_pos <= query_pos, 0.0, masked_score
        )


def attend(info, query, kv_pieces):
    rows = query.shape[0]
    count = len(kv_pieces)

    def kernel(info_ref, q_ref, *refs):
        keys, values = refs[:count], refs[count : 2 * count]
        mixed_ref, total_ref, bias_ref, score_ref = refs[2 * count :]

        @pl.when(pl.program_id(0) == 0)
        def _():
            fill_bias(info_ref, bias_ref, count, rows)

        q = q_ref[...]
        top = None
        for piece in range(count):
            at = slice(piece * rows, (piece + 1) * rows)
            score = dot(keys[piece][...], q, 1, 1) * score_scale_two + bias_ref[at, :]
            score_ref[at, :] = score
            peak = jnp.max(score, 0, keepdims=True)
            top = peak if top is None else jnp.maximum(top, peak)
        total = jnp.zeros((1, rows), f32)
        mixed = jnp.zeros((HEAD, rows), f32)
        for piece in range(count):
            weight = jnp.exp2(score_ref[piece * rows : (piece + 1) * rows, :] - top)
            total += jnp.sum(weight, 0, keepdims=True)
            mixed += dot(values[piece][...], weight.astype(bf16), 0, 0)
        mixed_ref[...] = (mixed / total).T.astype(bf16)
        total_ref[0] = top + jnp.log2(total)

    key_spec = pl.BlockSpec((rows, HEAD), lambda h: (0, h // GROUP))
    value_spec = pl.BlockSpec((rows, HEAD), lambda h: (0, KV_HEADS + h // GROUP))
    head_spec = pl.BlockSpec((rows, HEAD), lambda h: (0, h))
    return pl.pallas_call(
        kernel,
        grid=(HEADS,),
        in_specs=[pl.BlockSpec(memory_space=pltpu.SMEM), head_spec]
        + [key_spec] * count
        + [value_spec] * count,
        out_specs=[head_spec, pl.BlockSpec((1, 1, rows), lambda h: (h, 0, 0))],
        out_shape=[
            jax.ShapeDtypeStruct((rows, Q_WIDTH), bf16),
            jax.ShapeDtypeStruct((HEADS, 1, rows), f32),
        ],
        scratch_shapes=[pltpu.VMEM((count * rows, rows), f32)] * 2,
        compiler_params=kernel_params(32),
        cost_estimate=light,
    )(info, query, *kv_pieces, *kv_pieces)


def norm_back(part_grad, cotangent, hidden, gain, out_all):
    rows, width = hidden.shape
    tile = 256

    def kernel(p_ref, c_ref, h_ref, gain_ref, w_ref, gh_ref, gain_out_ref, branch_ref, mixed_ref):
        @pl.when(pl.program_id(0) == 0)
        def _():
            part, h = p_ref[...].astype(f32), h_ref[...]
            scale = lax.rsqrt(jnp.mean(h * h, -1, keepdims=True) + norm_eps)
            scaled = part * gain_ref[...]
            grad = (
                c_ref[...].astype(f32)
                + scale * scaled
                - h * (scale * scale * scale) * jnp.mean(h * scaled, -1, keepdims=True)
            )
            gh_ref[...] = grad
            gain_out_ref[...] = jnp.sum(part * h * scale, 0, keepdims=True)
            branch_ref[...] = grad.astype(bf16)

        mixed_ref[...] = dot(branch_ref[...], w_ref[...], 1, 1).astype(bf16)

    return pl.pallas_call(
        kernel,
        grid=(out_all.shape[0] // tile,),
        in_specs=[whole((rows, width))] * 3
        + [whole((1, width)), pl.BlockSpec((tile, width), lambda i: (i, 0))],
        out_specs=[whole((rows, width)), whole((1, width)), whole((rows, width))]
        + [pl.BlockSpec((rows, tile), lambda i: (0, i))],
        out_shape=[
            jax.ShapeDtypeStruct((rows, width), f32),
            jax.ShapeDtypeStruct((1, width), f32),
            jax.ShapeDtypeStruct((rows, width), bf16),
            jax.ShapeDtypeStruct((rows, out_all.shape[0]), bf16),
        ],
        compiler_params=kernel_params(32),
        cost_estimate=light,
    )(part_grad, cotangent, hidden, gain, out_all)


def attend_back(info, query, grad_mixed, totals, cosine, sine, kv_pieces):
    rows = query.shape[0]
    count = len(kv_pieces)

    def kernel(info_ref, q_ref, g_ref, total_ref, cos_ref, sin_ref, *refs):
        keys, values = refs[:count], refs[count : 2 * count]
        dq_ref = refs[2 * count]
        kv_ref, bias_ref, p_ref, dp_ref, sum_ref = refs[2 * count + 1 :]
        head = pl.program_id(0)

        @pl.when(head == 0)
        def _():
            fill_bias(info_ref, bias_ref, count, rows)

        @pl.when(head % GROUP == 0)
        def _():
            sum_ref[...] = jnp.zeros_like(sum_ref)

        q, g, total = q_ref[...], g_ref[...], total_ref[0]
        delta = jnp.zeros((1, rows), f32)
        for piece in range(count):
            at = slice(piece * rows, (piece + 1) * rows)
            score = dot(keys[piece][...], q, 1, 1) * score_scale_two + bias_ref[at, :]
            p = jnp.exp2(score - total)
            dp = dot(values[piece][...], g, 1, 1)
            p_ref[at, :] = p
            dp_ref[at, :] = dp
            delta += jnp.sum(p * dp, 0, keepdims=True)
        dq = jnp.zeros((HEAD, rows), f32)
        for piece in range(count):
            at = slice(piece * rows, (piece + 1) * rows)
            p = p_ref[at, :]
            ds = (p * (dp_ref[at, :] - delta) * score_scale).astype(bf16)
            dq += dot(keys[piece][...], ds, 0, 0)
            sum_ref[piece, 0] += dot(ds, q, 1, 0)
            sum_ref[piece, 1] += dot(p.astype(bf16), g, 1, 0)
        dq = dq.T
        dq_ref[...] = (dq * cos_ref[...] - pltpu.roll(dq, HEAD // 2, 1) * sin_ref[...]).astype(bf16)

        @pl.when(head % GROUP == GROUP - 1)
        def _():
            for piece in range(count):
                kv_ref[info_ref[1 + count + piece]] = sum_ref[piece].astype(bf16)

    key_spec = pl.BlockSpec((rows, HEAD), lambda h: (0, h // GROUP))
    value_spec = pl.BlockSpec((rows, HEAD), lambda h: (0, KV_HEADS + h // GROUP))
    head_spec = pl.BlockSpec((rows, HEAD), lambda h: (0, h))
    return pl.pallas_call(
        kernel,
        grid=(HEADS,),
        in_specs=[
            pl.BlockSpec(memory_space=pltpu.SMEM),
            head_spec,
            head_spec,
            pl.BlockSpec((1, 1, rows), lambda h: (h, 0, 0)),
            whole((rows, HEAD)),
            whole((rows, HEAD)),
        ]
        + [key_spec] * count
        + [value_spec] * count,
        out_specs=[head_spec]
        + [pl.BlockSpec((count, 2, rows, HEAD), lambda h: (0, 0, 0, h // GROUP))],
        out_shape=[jax.ShapeDtypeStruct((rows, Q_WIDTH), bf16)]
        + [jax.ShapeDtypeStruct((count, 2, rows, K_WIDTH), bf16)],
        scratch_shapes=[pltpu.VMEM((count * rows, rows), f32)] * 3
        + [pltpu.VMEM((count, 2, rows, HEAD), f32)],
        compiler_params=kernel_params(32),
        cost_estimate=light,
    )(info, query, grad_mixed, totals, cosine, sine, *kv_pieces, *kv_pieces)


def once(shape):
    return pl.BlockSpec(shape, lambda *_: (0,) * len(shape), pipeline_mode=pl.Buffered(1))


def token_rows(count, rows):
    return 2 * rows if count % (2 * rows) == 0 else rows


def feed_forward(normed, cotangent, gate_cols, up_cols, units_here, rows, cuts):
    count, width = normed.shape
    units = gate_cols.shape[1]
    rows = token_rows(count, rows)
    steps, part, tile = count // rows, units_here // cuts, 256

    def kernel(x_ref, c_ref, wg_ref, wu_ref, act_ref, to_gate_ref, to_up_ref, *refs):
        down_refs, turned_ref = refs[:cuts], refs[cuts]
        step = pl.program_id(0)

        @pl.when(step < steps)
        def _():
            x = x_ref[...]
            gate = dot(x, wg_ref[...], 1, 0)
            up = dot(x, wu_ref[...], 1, 0)
            sigmoid = jax.nn.sigmoid(gate)
            swished = gate * sigmoid
            act = (swished * up).astype(bf16)
            act_ref[...] = act
            turned_ref[:, pl.ds(pl.multiple_of(step * rows, rows), rows)] = act.T
            to_up_ref[...] = swished.astype(bf16)
            to_gate_ref[...] = (up * sigmoid * (1.0 + gate * (1.0 - sigmoid))).astype(bf16)

        @pl.when(step >= steps)
        def _():
            for cut, down_ref in enumerate(down_refs):
                turned = turned_ref[cut * part : (cut + 1) * part, :]
                down_ref[...] = dot(turned, c_ref[...], 1, 0).astype(bf16)

    def early(i):
        return (jnp.minimum(i, steps - 1), 0)

    def late(i):
        return (0, jnp.maximum(i - steps, 0))

    return pl.pallas_call(
        kernel,
        grid=(steps + width // tile,),
        in_specs=[
            pl.BlockSpec((rows, width), early),
            pl.BlockSpec((count, tile), late),
            once((width, units)),
            once((width, units)),
        ],
        out_specs=[pl.BlockSpec((rows, units), early)] * 3 + [pl.BlockSpec((part, tile), late)] * cuts,
        out_shape=[jax.ShapeDtypeStruct((count, units), bf16)] * 3
        + [jax.ShapeDtypeStruct((part, width), bf16)] * cuts,
        scratch_shapes=[pltpu.VMEM((units, count), bf16)],
        compiler_params=kernel_params(58),
        cost_estimate=light,
    )(normed, cotangent, gate_cols, up_cols)


def unit_grads(cotangent, down_rows, to_gate, to_up, rows):
    count, width = cotangent.shape
    units = down_rows.shape[0]
    rows = token_rows(count, rows)

    def kernel(c_ref, wd_ref, tg_ref, tu_ref, dg_ref, du_ref):
        grad_act = dot(c_ref[...], wd_ref[...], 1, 1)
        dg_ref[...] = (grad_act * tg_ref[...].astype(f32)).astype(bf16)
        du_ref[...] = (grad_act * tu_ref[...].astype(f32)).astype(bf16)

    unit_spec = pl.BlockSpec((rows, units), lambda i: (i, 0))
    return pl.pallas_call(
        kernel,
        grid=(count // rows,),
        in_specs=[
            pl.BlockSpec((rows, width), lambda i: (i, 0)),
            once((units, width)),
            unit_spec,
            unit_spec,
        ],
        out_specs=[unit_spec] * 2,
        out_shape=[jax.ShapeDtypeStruct((count, units), bf16)] * 2,
        compiler_params=kernel_params(58),
        cost_estimate=light,
    )(cotangent, down_rows, to_gate, to_up)


def through_columns(grad_gate, grad_up, gate_cols, up_cols, rows):
    count, units = grad_gate.shape
    width = gate_cols.shape[0]
    rows = token_rows(count, rows)

    def kernel(dg_ref, du_ref, wg_ref, wu_ref, out_ref):
        out = dot(dg_ref[...], wg_ref[...], 1, 1) + dot(du_ref[...], wu_ref[...], 1, 1)
        out_ref[...] = out.astype(bf16)

    unit_spec = pl.BlockSpec((rows, units), lambda i: (i, 0))
    return pl.pallas_call(
        kernel,
        grid=(count // rows,),
        in_specs=[unit_spec, unit_spec, once((width, units)), once((width, units))],
        out_specs=pl.BlockSpec((rows, width), lambda i: (i, 0)),
        out_shape=jax.ShapeDtypeStruct((count, width), bf16),
        compiler_params=kernel_params(58),
        cost_estimate=light,
    )(grad_gate, grad_up, gate_cols, up_cols)


def column_grads(normed, grad_gate, grad_up, cuts):
    count, width = normed.shape
    units = grad_gate.shape[1]
    tile = 256
    each = width // tile // cuts

    def kernel(x_ref, g_ref, u_ref, *out_refs):
        step = pl.program_id(0)
        x = x_ref[...].T
        out = dot(x, g_ref[...], 1, 0).astype(bf16)
        for cut, out_ref in enumerate(out_refs[:cuts]):

            @pl.when(step // each == cut)
            def _():
                out_ref[...] = out

        out_refs[cuts][...] = dot(x, u_ref[...], 1, 0).astype(bf16)

    def cut_spec(cut):
        return pl.BlockSpec((tile, units), lambda i: (jnp.clip(i - cut * each, 0, each - 1), 0))

    *gate, up = pl.pallas_call(
        kernel,
        grid=(width // tile,),
        in_specs=[pl.BlockSpec((count, tile), lambda i: (0, i))] + [once((count, units))] * 2,
        out_specs=[cut_spec(cut) for cut in range(cuts)]
        + [pl.BlockSpec((tile, units), lambda i: (i, 0))],
        out_shape=[jax.ShapeDtypeStruct((width // cuts, units), bf16)] * cuts
        + [jax.ShapeDtypeStruct((width, units), bf16)],
        compiler_params=kernel_params(58),
        cost_estimate=light,
    )(normed, grad_gate, grad_up)
    return gate, up


def through_rows(activation, down_rows, rows):
    count, units = activation.shape
    width = down_rows.shape[1]
    rows = token_rows(count, rows)

    def kernel(act_ref, wd_ref, out_ref):
        out_ref[...] = dot(act_ref[...], wd_ref[...], 1, 0).astype(bf16)

    return pl.pallas_call(
        kernel,
        grid=(count // rows,),
        in_specs=[pl.BlockSpec((rows, units), lambda i: (i, 0)), once((units, width))],
        out_specs=pl.BlockSpec((rows, width), lambda i: (i, 0)),
        out_shape=jax.ShapeDtypeStruct((count, width), bf16),
        compiler_params=kernel_params(58),
        cost_estimate=light,
    )(activation, down_rows)


def rotary(positions):
    half = HEAD // 2
    frequency = rope_base ** (-(jnp.arange(half, dtype=f32) * 2.0) / HEAD)
    angles = positions.astype(f32)[:, None] * frequency[None, :]
    cosine, sine = jnp.cos(angles), jnp.sin(angles)
    return jnp.concatenate([cosine, cosine], 1), jnp.concatenate([-sine, sine], 1)


def fence(*values):
    return lax.optimization_barrier(values)


def added(left_side, right_side):
    def kernel(a_ref, b_ref, out_ref):
        out_ref[...] = (a_ref[...].astype(f32) + b_ref[...].astype(f32)).astype(out_ref.dtype)

    def one(a, b):
        steps = [n for n in (2, 3, 5) if a.ndim == 2 and a.shape[0] % (16 * n) == 0]
        if not steps:
            return (a.astype(f32) + b.astype(f32)).astype(a.dtype)
        block = pl.BlockSpec((a.shape[0] // steps[0], a.shape[1]), lambda i: (i, 0))
        return pl.pallas_call(
            kernel,
            grid=(steps[0],),
            in_specs=[block] * 2,
            out_specs=block,
            out_shape=jax.ShapeDtypeStruct(a.shape, a.dtype),
            compiler_params=kernel_params(16),
            cost_estimate=light,
        )(a, b)

    return jax.tree.map(one, left_side, right_side)


class CtxLine:
    def __init__(self):
        place = lax.axis_index("ctx")
        self.outer = (place == 0) | (place == 3)
        self.waiting = []
        self.chunks, self.inward, self.across, self.pair_sums = [], [], [], []
        self.totals, self.outward = [], []

    def add(self, chunks):
        self.waiting += list(chunks)
        self.send()

    def send(self):
        ready = len(self.pair_sums)
        while self.waiting and len(self.chunks) < ready + (2 if ready > 2 else 1):
            chunk = self.waiting.pop(0)
            if ready > 2:
                self.inward[-1], chunk = fence(self.inward[-1], chunk)
            self.chunks.append(chunk)
            self.inward.append(lax.ppermute(chunk, "ctx", [(0, 1), (3, 2)]))

    def round(self, *values):
        step = len(self.pair_sums)
        more = step < len(self.chunks)
        last = len(self.totals)
        if more:
            self.inward[step], values = fence(self.inward[step], values)
            self.pair_sums.append(added(self.chunks[step], self.inward[step]))
        held = [
            (self.across, slice(last, None)),
            (self.pair_sums, slice(last + 1, None)),
            (self.outward, slice(last - 1, None) if last else slice(0, 0)),
        ]
        fenced, self.waiting, values = fence([array[at] for array, at in held], self.waiting, values)
        for (array, at), value in zip(held, fenced):
            array[at] = value
        self.send()
        if len(self.across) > last:
            self.totals.append(added(self.pair_sums[last], self.across[last]))
            self.outward.append(lax.ppermute(self.totals[-1], "ctx", [(1, 0), (2, 3)]))
        if more:
            self.across.append(lax.ppermute(self.pair_sums[step], "ctx", [(1, 2), (2, 1)]))
        return values

    def sums(self, first, last):
        return jax.tree.map(
            lambda back, total: jnp.where(self.outer, back, total),
            self.outward[first:last],
            self.totals[first:last],
        )


def summed_in_plane(vector):
    size = lax.axis_size("fsdp")
    bit = 1
    while bit < size:
        vector = vector + lax.ppermute(vector, "fsdp", [(j, j ^ bit) for j in range(size)])
        bit *= 2
    return vector


def local(
    tokens_in,
    block_order,
    norm_attn,
    w_qkv,
    b_qkv,
    w_out,
    norm_mlp,
    w_gate,
    w_up,
    w_down,
    cotangent,
):
    rows, width = tokens_in.shape
    shards = lax.axis_size("fsdp")
    blocks = lax.axis_size("ctx")
    shard = lax.axis_index("fsdp")
    place = lax.axis_index("ctx")
    shard_rows = w_gate.shape[0]
    units = w_down.shape[0]
    orders = block_order[0]
    owners = jnp.concatenate([place[None], (place - jnp.arange(blocks)) % blocks])
    info = jnp.sum(
        jnp.where(owners[:, None] == jnp.arange(blocks)[None, :], orders[None, :], 0), 1
    )
    info = jnp.concatenate([info, owners[1:]]).astype(jnp.int32)
    cosine, sine = rotary(info[0] * rows + jnp.arange(rows, dtype=jnp.int32))

    def turn(parts):
        return lax.all_to_all(parts, "fsdp", 0, 0)

    qkv_all = lax.all_gather(w_qkv, "fsdp", axis=0, tiled=True)
    vectors = lax.all_gather(jnp.concatenate([norm_attn, norm_mlp, b_qkv]), "fsdp", axis=0)
    part = 2 * shard_rows // 3 // blocks
    shared = part * blocks
    weights = (w_gate, w_up)
    parts = jnp.concatenate(
        [lax.dynamic_slice_in_dim(weight, place * part, part, 0) for weight in weights]
    )
    vectors, parts = fence(vectors, split_columns(parts, shards))
    pieces = [turn(parts)]

    def ring(piece):
        return lax.ppermute(piece, "ctx", [(j, (j + 1) % blocks) for j in range(blocks)])

    pieces.append(ring(pieces[0]))
    full = padded(units)
    down_rows = jnp.concatenate([w_down, jnp.zeros((full - units, width), bf16)])
    direct = split_columns(jnp.concatenate([weight[shared:] for weight in weights]), shards)
    gain_attn = vectors[:, :shard_rows].reshape(1, -1).astype(f32)
    gain_mlp = vectors[:, shard_rows : 2 * shard_rows].reshape(1, -1).astype(f32)
    bias_all = vectors[:, 2 * shard_rows :].reshape(1, -1).astype(f32)
    qkv_all, pieces, down_rows = fence(qkv_all, pieces, down_rows)
    out_all = lax.all_gather(w_out, "fsdp", axis=0, tiled=True)

    normed, query, keys_values = project(tokens_in, gain_attn, qkv_all, bias_all, cosine, sine)
    keys_values, direct = fence(keys_values, direct)
    direct = turn(direct)
    kv_pieces = [keys_values] + [
        lax.ppermute(keys_values, "ctx", [(j, (j + s) % blocks) for j in range(blocks)])
        for s in range(1, blocks)
    ]
    kv_pieces, pieces, own_cot = fence(kv_pieces, pieces, cotangent)
    for _ in range(2, blocks - 1):
        pieces.append(ring(pieces[-1]))

    def from_chip(chip):
        return lax.ppermute(own_cot, "fsdp", [(j, j ^ chip) for j in range(shards)])

    chips = [chip for chip in range(2, shards, 2) if chip & (chip - 1) == 0]
    cot_pieces = {chip: from_chip(chip) for chip in chips}
    mixed, totals = attend(info, query, kv_pieces)
    mixed, direct = fence(mixed, direct)
    source = tokens_in.astype(f32)
    hidden = source + dot(mixed, out_all, 1, 0)
    scale_two = lax.rsqrt(jnp.mean(hidden * hidden, -1, keepdims=True) + norm_eps)
    normed_two = (hidden * scale_two * gain_mlp).astype(bf16)

    normed_two, pieces, cot_pieces = fence(normed_two, pieces, cot_pieces)
    pieces.append(ring(pieces[-1]))
    normed_all = lax.all_gather(normed_two, "fsdp", axis=0, tiled=True)
    cot_pieces[0] = own_cot
    for chip in range(2, shards, 2):
        if chip not in cot_pieces:
            cot_pieces[chip] = from_chip(chip)
            cot_pieces[chip], pieces = fence(cot_pieces[chip], pieces)
    for chip in range(0, shards, 2):
        cot_pieces[chip ^ 1] = lax.ppermute(
            cot_pieces[chip], "fsdp", [(j, j ^ 1) for j in range(shards)]
        )
    order = list(cot_pieces)

    def cot_moves(place, shard):
        return [
            (i, pl.ds(0, rows), 0, pl.ds((shard ^ bits) * rows, rows))
            for i, bits in enumerate(order)
        ]

    (cot_all,) = moved(cot_moves, [cot_pieces[bits] for bits in order], [(shards * rows, width)])

    groups = shard_rows // part
    grouped = (shards, groups, part, full)
    rest = groups - blocks

    def column_moves(place, shard):
        every = pl.ds(0, shards)
        listed = []
        for k in range(2):
            for s in range(blocks):
                group = lax.rem(place - s + blocks, blocks)
                listed.append((s, (every, k), k, (every, group)))
            listed.append((blocks, (every, pl.ds(k * rest, rest)), k, (every, pl.ds(blocks, rest))))
        return listed

    sources = [piece.reshape(shards, 2, part, full) for piece in pieces]
    sources.append(direct.reshape(shards, 2 * rest, part, full))
    columns = moved(column_moves, sources, [grouped] * 2)
    gate_cols, up_cols = (array.reshape(width, full) for array in columns)
    cuts = 2
    activation, to_gate, to_up, *down_terms = feed_forward(
        normed_all, cot_all, gate_cols, up_cols, units, rows, cuts
    )

    def to_rows(terms):
        return turn(terms.reshape(shards, shard_rows, full)).reshape(width, full)

    def merged(terms):
        return merge_columns(terms.reshape(shards, shard_rows, full), units)

    def to_owner(terms):
        return lax.psum_scatter(terms, "fsdp", scatter_dimension=0, tiled=True)

    def through_attention(part_grad):
        grad_hidden, gain_terms, grad_branch, grad_mixed = norm_back(
            part_grad, cotangent, hidden, gain_mlp, out_all
        )
        gain_terms = gain_terms[0]
        grad_query, kv_terms = attend_back(
            info, query, grad_mixed, totals, cosine, sine, kv_pieces
        )
        return grad_hidden, gain_terms, grad_branch, grad_query, kv_terms

    def kv_owner(kv_terms):
        return lax.psum_scatter(kv_terms, "ctx", scatter_dimension=0)

    def projected_grad(grad_query, kv_terms):
        grad_kv = kv_terms.astype(f32)
        grad_key = grad_kv[0].reshape(rows, KV_HEADS, HEAD)
        rolled = jnp.concatenate([grad_key[..., HEAD // 2 :], grad_key[..., : HEAD // 2]], -1)
        grad_key = grad_key * cosine[:, None, :] - rolled * sine[:, None, :]
        return jnp.concatenate(
            [grad_query, grad_key.reshape(rows, K_WIDTH).astype(bf16), grad_kv[1].astype(bf16)], 1
        )

    def to_tokens(grad_projected, grad_hidden):
        scale_one = lax.rsqrt(jnp.mean(source * source, -1, keepdims=True) + norm_eps)
        grad_normed = dot(grad_projected, qkv_all, 1, 1)
        scaled = grad_normed * gain_attn
        grad_tokens = (
            grad_hidden
            + scale_one * scaled
            - source * scale_one**3 * jnp.mean(source * scaled, -1, keepdims=True)
        ).astype(bf16)
        bias_terms = jnp.sum(grad_projected.astype(f32), 0)
        return grad_tokens, jnp.sum(grad_normed * source * scale_one, 0), bias_terms

    def out_grad(mixed, grad_branch):
        return dot(mixed, grad_branch, 0, 0).astype(bf16)

    def own_sums(*terms):
        total = summed_in_plane(jnp.concatenate([t.reshape(shards, -1) for t in terms], 1))
        return lax.dynamic_index_in_dim(total, shard, 0, False)

    grad_gate, grad_up = unit_grads(cot_all, down_rows, to_gate, to_up, rows)
    mlp_grad = through_columns(grad_gate, grad_up, gate_cols, up_cols, rows)
    if blocks == 4:
        line = CtxLine()
        line.add(down_terms)
        mlp_grad, grad_gate, grad_up, act = line.round(
            mlp_grad, grad_gate, grad_up, activation
        )
        part_grad = to_owner(mlp_grad)
        gate_terms, up_terms = column_grads(normed_all, grad_gate, grad_up, cuts)
        gate_terms, up_terms, act = line.round(gate_terms, up_terms, act)
        line.add(gate_terms)
        up_terms = to_rows(up_terms)
        grad_hidden, gain_mlp_terms, grad_branch, grad_query, kv_terms = through_attention(
            part_grad
        )
        kv_sums = kv_owner(kv_terms)
        grad_hidden, grad_branch, grad_query, mixed_now, kv_terms, up_terms = line.round(
            grad_hidden, grad_branch, grad_query, mixed, kv_terms, up_terms
        )
        out_terms = out_grad(mixed_now, grad_branch)
        split = width // 2
        line.add([up_terms[:split], up_terms[split:]])
        grad_query, out_terms = line.round(grad_query, out_terms)
        out_terms = to_owner(out_terms)
        grad_projected = projected_grad(grad_query, kv_sums)
        qkv_terms = dot(normed, grad_projected, 0, 0).astype(bf16)
        grad_tokens, gain_attn_terms, bias_terms = to_tokens(grad_projected, grad_hidden)
        qkv_terms, grad_tokens, gain_attn_terms, bias_terms, act = line.round(
            qkv_terms, grad_tokens, gain_attn_terms, bias_terms, act
        )
        qkv_terms = to_owner(qkv_terms)
        small = own_sums(gain_attn_terms, gain_mlp_terms, bias_terms)
        mlp_terms = through_rows(act, down_rows, rows)
        small, mlp_terms, out_terms = line.round(small, mlp_terms, out_terms)
        mlp_out = to_owner(mlp_terms)
        line.add([out_terms])
        gate_terms = to_rows(jnp.concatenate(line.sums(cuts, 2 * cuts)))
        (qkv_terms,) = line.round(qkv_terms)
        line.add([[qkv_terms, small]])
        line.round()
        (gate_terms,) = line.round(gate_terms)
        down_sums = line.sums(0, cuts)
        up_sum, up_more, out_sum, (qkv_sum, small) = line.sums(2 * cuts, 2 * cuts + 4)
        up_terms = jnp.concatenate([up_sum, up_more])
    else:
        part_grad = to_owner(mlp_grad)
        gate_terms, up_terms = column_grads(normed_all, grad_gate, grad_up, cuts)
        gate_terms, up_terms = to_rows(jnp.concatenate(gate_terms)), to_rows(up_terms)
        mlp_out = to_owner(through_rows(activation, down_rows, rows))
        grad_hidden, gain_mlp_terms, grad_branch, grad_query, kv_terms = through_attention(
            part_grad
        )
        kv_terms = kv_owner(kv_terms)
        out_terms = to_owner(out_grad(mixed, grad_branch))
        grad_projected = projected_grad(grad_query, kv_terms)
        qkv_terms = to_owner(dot(normed, grad_projected, 0, 0).astype(bf16))
        grad_tokens, gain_attn_terms, bias_terms = to_tokens(grad_projected, grad_hidden)
        small = own_sums(gain_attn_terms, gain_mlp_terms, bias_terms)
        down_sums, gate_terms, up_terms, out_sum, qkv_sum, small = lax.psum(
            (down_terms, gate_terms, up_terms, out_terms, qkv_terms, small), "ctx"
        )

    grad_down_w = jnp.concatenate(down_sums).astype(f32)
    grad_out_w = out_sum.astype(f32)
    grad_qkv_w = qkv_sum.astype(f32)
    out_tokens = (hidden + mlp_out.astype(f32)).astype(bf16)

    return (
        out_tokens,
        grad_tokens,
        small[:shard_rows],
        grad_qkv_w,
        small[2 * shard_rows :],
        grad_out_w,
        small[shard_rows : 2 * shard_rows],
        merged(gate_terms),
        merged(up_terms),
        grad_down_w,
    )


def solution(mesh):
    in_specs = (
        P(("fsdp", "ctx"), None),
        P("fsdp", None),
        P("fsdp"),
        P("fsdp", None),
        P("fsdp"),
        P("fsdp", None),
        P("fsdp"),
        P("fsdp", None),
        P("fsdp", None),
        P("fsdp", None),
        P(("fsdp", "ctx"), None),
    )
    out_specs = (
        P(("fsdp", "ctx"), None),
        P(("fsdp", "ctx"), None),
        P("fsdp"),
        P("fsdp", None),
        P("fsdp"),
        P("fsdp", None),
        P("fsdp"),
        P("fsdp", None),
        P("fsdp", None),
        P("fsdp", None),
    )
    return jax.shard_map(local, mesh=mesh, in_specs=in_specs, out_specs=out_specs, check_vma=False)
```
